512 devices in a mesh: span: 64 (over x, z, core), wall: 8 (over y).
Axes of the slice: x: 4, y: 8, z: 8, core: 2. Of those that a mesh axis runs over, the one named last changes fastest.
Arguments:
- velocity: float32 [3, 2, 1536, 8192], P(None, None, 'wall', 'span'), may hold values from -6 to 6
- wave_x: float32 [2], replicated, may hold values from 0.01 to 0.1
Outputs:
- pressure: float32 [2, 1536, 8192], P(None, 'wall', 'span')
The draws below stay inside these ranges and needn't reach their ends.
All inputs are finite; a program needn't handle non-finite values.
Results may differ from the reference program's by a relative error of at most 0.0023.
Values sent between devices are 32-bit elements; how exact they have to be, the bound alone decides.
No kernel may reach another device: no remote copies, remote signals or barrier semaphores. Data moves between devices by JAX's collectives and lax.ppermute only.
A program may use at most 64 MiB of HBM per device.

```python
import math
import jax
import jax.numpy as jnp
from jax import lax

PLANES = 2
NY = 1536
NZ = 8192


def draw_velocity(key, part):
    key = jax.random.fold_in(key, 11)
    full_shape = (3, PLANES, NY, NZ)
    return jax.random.truncated_normal(key, -6.0, 6.0, full_shape, jnp.float32)


def setup_inputs(seed: int = 0) -> dict:
    seeds = jax.random.split(jax.random.key(seed), 3)
    velocity = draw_velocity(jax.random.fold_in(seeds[2], 71), 0)
    wave_x = jnp.clip(jnp.exp(jax.random.uniform(seeds[1], (PLANES,), jnp.float32, math.log(0.01), math.log(0.1))), 0.01, 0.1)
    return dict(velocity=velocity, wave_x=wave_x)


def tridiagonal_neumann(rhs_re, rhs_im, mode_shift):
    row_ids = jnp.arange(NY, dtype=jnp.int32)
    zero_line = jnp.zeros((NZ,), jnp.float32)

    def forward(state_in, entry):
        ratio_prev, prev_re, prev_im = state_in
        row_now, now_re, now_im = entry
        on_edge = jnp.logical_or(row_now == 0, row_now == NY - 1)
        diagonal = jnp.where(on_edge, -(1.0 + mode_shift), -(2.0 + mode_shift))
        pivot_val = diagonal - ratio_prev
        ratio_new = 1.0 / pivot_val
        next_re = (now_re - prev_re) / pivot_val
        next_im = (now_im - prev_im) / pivot_val
        return (ratio_new, next_re, next_im), (ratio_new, next_re, next_im)

    start_state = (zero_line, zero_line, zero_line)
    _, (ratios, reduced_re, reduced_im) = lax.scan(forward, start_state, (row_ids, rhs_re, rhs_im))

    def backward(state_in, entry):
        later_re, later_im = state_in
        ratio_now, now_re, now_im = entry
        next_re = now_re - ratio_now * later_re
        next_im = now_im - ratio_now * later_im
        return (next_re, next_im), (next_re, next_im)

    _, (solved_re, solved_im) = lax.scan(backward, (zero_line, zero_line), (ratios, reduced_re, reduced_im), reverse=True)
    return solved_re, solved_im


def one_plane(entry):
    plane, wave_now = entry
    stream = plane[0]
    normal = plane[1]
    spanwise = plane[2]
    zero_row = jnp.zeros((1, NZ), jnp.float32)
    v_above = jnp.concatenate([normal[1:], zero_row], 0)
    v_below = jnp.concatenate([zero_row, normal[:-1]], 0)
    source = wave_now * stream + 0.5 * (v_above - v_below) + 0.5 * (jnp.roll(spanwise, -1, 1) - jnp.roll(spanwise, 1, 1))
    spectrum = jnp.fft.fft(source, axis=1)
    mode_ids = jnp.arange(NZ, dtype=jnp.int32).astype(jnp.float32)
    mode_shift = wave_now * wave_now + (2.0 * jnp.sin(jnp.pi * mode_ids / NZ)) ** 2
    solved_re, solved_im = tridiagonal_neumann(jnp.real(spectrum).astype(jnp.float32), jnp.imag(spectrum).astype(jnp.float32), mode_shift)
    return jnp.real(jnp.fft.ifft(solved_re + 1j * solved_im, axis=1)).astype(jnp.float32)


def reference(velocity, wave_x):
    return lax.map(one_plane, (jnp.moveaxis(velocity, 1, 0), wave_x))
```

```python
import functools

import jax
import jax.numpy as jnp
import numpy as np
from jax import lax
from jax.experimental import pallas as pl
from jax.experimental.pallas import tpu as pltpu
from jax.sharding import Mesh, PartitionSpec as P

F32 = jnp.float32
EXACT = lax.Precision.HIGHEST
NZ = 8192
OUTER = 64
INNER = 128
HALF = 32
ROWS = 6
SLAB = 192
LEVELS = 8
SPAN = ("xh", "xl", "zc")


def dft_tables():
    d = np.arange(OUTER)
    j = np.arange(INNER)
    k1 = np.arange(HALF)
    turn = 2 * np.pi * np.outer(k1, d) / OUTER
    outer = np.concatenate([np.cos(turn), -np.sin(turn)], 0)
    outer[HALF] = np.where(d % 2 == 0, 1.0, -1.0)
    weight = np.full(OUTER, 2.0)
    weight[0] = 1.0
    weight[HALF] = 1.0
    outer_back = (outer * weight[:, None]).T / NZ
    twist = 2 * np.pi * np.outer(k1, j) / NZ
    twist_cos, twist_sin = np.cos(twist), np.sin(twist)
    m = np.arange(64)
    inner = np.zeros((256, 256))
    for h in range(2):
        ang = 2 * np.pi * np.outer(j, 64 * h + m) / INNER
        re, im = slice(128 * h, 128 * h + 64), slice(128 * h + 64, 128 * h + 128)
        inner[:INNER, re], inner[INNER:, re] = np.cos(ang), np.sin(ang)
        inner[:INNER, im], inner[INNER:, im] = -np.sin(ang), np.cos(ang)
    first = np.zeros((256, 256))
    ang = 2 * np.pi * np.outer(j, m) / INNER
    first[:INNER, :64], first[:INNER, 64:128] = np.cos(ang), -np.sin(ang)
    first[:INNER, 64] = np.where(j % 2 == 0, 1.0, -1.0)
    ang = 2 * np.pi * np.outer(j, HALF + 64 * m) / NZ
    first[INNER:, 128:192], first[INNER:, 192:] = np.cos(ang), -np.sin(ang)
    double = np.full(256, 2.0)
    double[0] = double[64] = 1.0
    first_back = (first * double[None, :]).T
    inner_back = inner.T
    k = np.zeros((HALF, 256))
    for h in range(2):
        for part in range(2):
            at = 128 * h + 64 * part
            k[:, at : at + 64] = k1[:, None] + 64 * (64 * h + m)[None, :]
    k[0, :64] = k[0, 64:128] = 64 * m
    k[0, 64] = NZ // 2
    k[0, 128:192] = k[0, 192:] = HALF + 64 * m
    wave2 = (2 * np.sin(np.pi * k / NZ)) ** 2
    share = np.zeros((16, 8, 128))
    for c in range(16):
        for g in range(2):
            for hi in range(2):
                for h in range(2):
                    share[c, 4 * g + 2 * hi + h] = wave2[16 * hi + c, 128 * h : 128 * h + 128]
    names = dict(
        outer=outer, outer_back=outer_back, twist_cos=twist_cos, twist_sin=twist_sin,
        inner=inner, first=first, inner_back=inner_back, first_back=first_back,
        wave2=wave2, share=share.reshape(128, 128),
    )
    return {key: np.asarray(value, np.float32) for key, value in names.items()}


def dot(a, b):
    return jnp.dot(a, b, precision=EXACT, preferred_element_type=F32)


def ids(shape, dim):
    return lax.broadcasted_iota(jnp.int32, shape, dim)


def source_kernel(wave_ref, vel_ref, out_ref):
    shape = (SLAB, INNER)
    row, lane = ids(shape, 0), ids(shape, 1)
    gather = (ids((32, SLAB), 1) // ROWS == ids((32, SLAB), 0)).astype(F32)
    block_id = ids((32, INNER), 0)
    for plane in range(2):
        u, v, w = (vel_ref[c, plane] for c in range(3))
        above = jnp.where(row == SLAB - 1, 0.0, pltpu.roll(v, SLAB - 1, 0))
        below = jnp.where(row == 0, 0.0, pltpu.roll(v, 1, 0))
        after = jnp.where(lane == INNER - 1, 0.0, pltpu.roll(w, INNER - 1, 1))
        before = jnp.where(lane == 0, 0.0, pltpu.roll(w, 1, 1))
        source = wave_ref[plane] * u + 0.5 * ((above - below) + (after - before))
        for i in range(32):
            at = 8 * (32 * plane + i)
            out_ref[at : at + ROWS, :] = source[ROWS * i : ROWS * i + ROWS]
        ends = jnp.where(block_id == 0, v[0:1], jnp.where(block_id == 31, v[SLAB - 1 :], 0.0))
        out_ref[pl.ds(256 * plane + 6, 32, stride=8), :] = ends
        place = row % ROWS
        edges = jnp.where(lane == place, w[:, 0:1], jnp.where(lane == 64 + place, w[:, INNER - 1 :], 0.0))
        out_ref[pl.ds(256 * plane + 7, 32, stride=8), :] = dot(gather, edges)


def factors(diag):
    ratios = [1.0 / diag]
    for _ in range(ROWS - 1):
        ratios.append(1.0 / (diag - ratios[-1]))
    carry = [jnp.ones_like(diag)]
    for i in range(1, ROWS):
        carry.append(ratios[i - 1] * carry[-1])
    column = [None] * ROWS
    column[-1] = -ratios[-1] * carry[-1]
    for i in range(ROWS - 2, -1, -1):
        column[i] = ratios[i] * (column[i + 1] - carry[i])
    return ratios, column


def factor_kernel(wave_ref, wave2_ref, share_ref, ratio_ref, column_ref, merge_ref):
    wave = wave_ref[lax.axis_index("xh")]
    ratios, column = factors(2.0 + (wave * wave + wave2_ref[...]))
    for i in range(ROWS):
        ratio_ref[HALF * i : HALF * (i + 1), :] = ratios[i]
        column_ref[HALF * i : HALF * (i + 1), :] = column[i]
    mine = pl.multiple_of(8 * lax.axis_index("zc"), 8)
    _, column = factors(2.0 + (wave * wave + share_ref[pl.ds(mine, 8), :]))
    near, far = column[0], column[-1]
    for level in range(LEVELS):
        inv = 1.0 / ((1.0 - near) * (1.0 + near))
        merge_ref[level, 0] = near
        merge_ref[level, 1] = far
        merge_ref[level, 2] = inv
        merge_ref[level, 3] = -far * inv
        merge_ref[level, 4] = near * far * inv
        near, far = near + near * (far * far * inv), -far * far * inv
    merge_ref[LEVELS, 0] = 0.5 / (1.0 + near + far)
    merge_ref[LEVELS, 1] = 0.5 / (1.0 + near - far)
    for i in range(2, 5):
        merge_ref[LEVELS, i] = jnp.zeros_like(near)


def forward_kernel(in_ref, outer_ref, cos_ref, sin_ref, inner_ref, first_ref, ratio_ref, ends_ref, local_ref):
    lane = ids((OUTER, INNER), 1)
    edge = in_ref[pl.ds(7, OUTER, stride=8), :]
    edge_after = 0.5 * pltpu.roll(edge, OUTER - 1, 0)
    edge_before = -0.5 * pltpu.roll(edge, 1, 0)
    lines = []
    for r in range(ROWS):
        line = in_ref[pl.ds(r, OUTER, stride=8), :]
        fix = jnp.where(lane == INNER - 1, edge_after[:, r : r + 1], 0.0)
        fix = jnp.where(lane == 0, edge_before[:, 64 + r : 65 + r], fix)
        lines.append(line + fix)
    lines.append(in_ref[pl.ds(6, OUTER, stride=8), :])
    freq = dot(outer_ref[...], jnp.concatenate(lines, 1))
    cos, sin = cos_ref[...], sin_ref[...]
    turned = []
    for r in range(ROWS + 1):
        re, im = (freq[HALF * p : HALF * (p + 1), INNER * r : INNER * (r + 1)] for p in range(2))
        turned.append(jnp.concatenate([re * cos + im * sin, im * cos - re * sin], 1))
    full = dot(jnp.concatenate(turned, 0), inner_ref[...])
    heads = [t[0:1] for t in turned] + [jnp.zeros((1, 256), F32)]
    head = dot(jnp.concatenate(heads, 0), first_ref[...])
    is_first = ids((HALF, 256), 0) == 0
    modes = [
        jnp.where(is_first, head[r : r + 1], full[HALF * r : HALF * (r + 1)]) for r in range(ROWS + 1)
    ]
    ratios = [ratio_ref[HALF * i : HALF * (i + 1), :] for i in range(ROWS)]
    carry = [modes[0]]
    for i in range(1, ROWS):
        carry.append(modes[i] + ratios[i - 1] * carry[-1])
    value = -ratios[-1] * carry[-1]
    last = value
    local_ref[HALF * (ROWS - 1) :, :] = value
    for i in range(ROWS - 2, -1, -1):
        value = ratios[i] * (value - carry[i])
        local_ref[HALF * i : HALF * (i + 1), :] = value
    block = lax.axis_index("xl") * 16 + lax.axis_index("zc")
    wall = lax.axis_index("wall")
    low = jnp.where(jnp.logical_and(block == 0, wall > 0), 0.5, 0.0)
    high = jnp.where(jnp.logical_and(block == 31, wall < 7), 0.5, 0.0)
    ends = (value - low * modes[ROWS], last + high * modes[ROWS])
    for g in range(2):
        for hi in range(2):
            for h in range(2):
                part = ends[g][16 * hi : 16 * hi + 16, 128 * h : 128 * h + 128]
                ends_ref[pl.ds(4 * g + 2 * hi + h, 16, stride=8), :] = part


def swap(tile):
    return pltpu.roll(tile, 4, 0)


def merge_up(tiles, coef, is_low, keep):
    near, far, inv = (coef[i] for i in range(3))
    merged = []
    for left, right in zip(tiles[0::2], tiles[1::2]):
        inside = jnp.where(is_low, swap(left), swap(right))
        inside = (inside - near * swap(inside)) * inv
        keep.append(inside)
        merged.append(jnp.where(is_low, left, right) - far * swap(inside))
    return merged


def spread_down(outers, insides, coef, is_low):
    direct, cross = coef[3], coef[4]
    spread = []
    for outer, inside in zip(outers, insides):
        inside = inside + direct * outer + cross * swap(outer)
        spread.append(jnp.where(is_low, outer, inside))
        spread.append(jnp.where(is_low, inside, outer))
    return spread


def reduce_kernel(in_ref, merge_ref, root_ref, inside_ref):
    is_low = ids((8, 128), 0) < 4
    tiles = [in_ref[8 * b : 8 * b + 8, :] for b in range(16)]
    keep = []
    for level in range(4):
        tiles = merge_up(tiles, merge_ref.at[level], is_low, keep)
    for b in range(16):
        root_ref[8 * b : 8 * b + 8, :] = tiles[0]
    for n, tile in enumerate(keep):
        inside_ref[8 * n : 8 * n + 8, :] = tile
    inside_ref[120:128, :] = tiles[0]


def spread_kernel(in_ref, inside_ref, merge_ref, out_ref, leaf_ref):
    is_low = ids((8, 128), 0) < 4
    order = [8 * (s % 2) + s // 2 for s in range(16)]
    tiles = [in_ref[8 * b : 8 * b + 8, :] for b in order]
    kept = []
    for level in range(4):
        keep = []
        tiles = merge_up(tiles, merge_ref.at[4 + level], is_low, keep)
        kept.append(keep)
    even, odd = merge_ref[LEVELS, 0], merge_ref[LEVELS, 1]
    ends = tiles[0]
    other = swap(ends)
    outers = [(ends + other) * even + (ends - other) * odd]
    for level in range(3, -1, -1):
        outers = spread_down(outers, kept[level], merge_ref.at[4 + level], is_low)
    for s in range(16):
        leaf_ref[8 * s : 8 * s + 8, :] = outers[s]
    mine = 2 * lax.axis_index("wall") + lax.axis_index("xl")
    outers = [leaf_ref[pl.ds(pl.multiple_of(8 * mine, 8), 8), :]]
    starts = (0, 8, 12, 14, 15)
    for level in range(3, -1, -1):
        insides = [inside_ref[8 * n : 8 * n + 8, :] for n in range(starts[level], starts[level + 1])]
        outers = spread_down(outers, insides, merge_ref.at[level], is_low)
    for b in range(16):
        out_ref[8 * b : 8 * b + 8, :] = outers[b]


def backward_kernel(in_ref, local_ref, column_ref, outer_ref, cos_ref, sin_ref, inner_ref, first_ref, out_ref):
    def side(g):
        halves = []
        for h in range(2):
            parts = [in_ref[pl.ds(4 * g + 2 * hi + h, 16, stride=8), :] for hi in range(2)]
            halves.append(jnp.concatenate(parts, 0))
        return jnp.concatenate(halves, 1)

    low, high = side(0), side(1)
    columns = [column_ref[HALF * i : HALF * (i + 1), :] for i in range(ROWS)]
    modes = [
        local_ref[HALF * i : HALF * (i + 1), :] - (low * columns[i] + high * columns[ROWS - 1 - i])
        for i in range(ROWS)
    ]
    full = dot(jnp.concatenate(modes, 0), inner_ref[...])
    heads = [t[0:1] for t in modes] + [jnp.zeros((2, 256), F32)]
    head = dot(jnp.concatenate(heads, 0), first_ref[...])
    is_first = ids((HALF, 256), 0) == 0
    cos, sin = cos_ref[...], sin_ref[...]
    turned = []
    for r in range(ROWS):
        step = jnp.where(is_first, head[r : r + 1], full[HALF * r : HALF * (r + 1)])
        re, im = step[:, :INNER], step[:, INNER:]
        turned.append(jnp.concatenate([re * cos - im * sin, im * cos + re * sin], 0))
    lines = dot(outer_ref[...], jnp.concatenate(turned, 1))
    for r in range(ROWS):
        out_ref[pl.ds(r, OUTER, stride=8), :] = lines[:, INNER * r : INNER * (r + 1)]
    for r in range(ROWS, 8):
        out_ref[pl.ds(r, OUTER, stride=8), :] = jnp.zeros((OUTER, INNER), F32)


def place_kernel(in_ref, out_ref):
    for p in range(OUTER):
        at = ROWS * (p % 32)
        out_ref[p // 32, at : at + ROWS, :] = in_ref[8 * p : 8 * p + ROWS, :]


SMEM = pl.BlockSpec(memory_space=pltpu.SMEM)
VMEM = pl.BlockSpec(memory_space=pltpu.VMEM)


def call(kernel, shapes, specs, *operands, scratch=()):
    outs = [jax.ShapeDtypeStruct(s, F32) for s in shapes]
    return pl.pallas_call(
        kernel,
        out_shape=outs if len(outs) > 1 else outs[0],
        in_specs=specs,
        out_specs=[VMEM] * len(outs) if len(outs) > 1 else VMEM,
        scratch_shapes=list(scratch),
        compiler_params=pltpu.CompilerParams(vmem_limit_bytes=24 << 20),
    )(*operands)


def exchange(block, axes):
    return lax.all_to_all(block, axes, split_axis=0, concat_axis=0, tiled=True)


def on_device(velocity, wave_x):
    t = {key: jnp.asarray(value) for key, value in dft_tables().items()}
    sent = call(source_kernel, [(512, 128)], [SMEM, VMEM], wave_x, velocity)
    ratio, column, merge = call(
        factor_kernel, [(192, 256), (192, 256), (LEVELS + 1, 5, 8, 128)],
        [SMEM, VMEM, VMEM], wave_x, t["wave2"], t["share"],
    )
    lines = exchange(sent.reshape(64, 8, 128), SPAN).reshape(512, 128)
    ends, local = call(
        forward_kernel, [(128, 128), (192, 256)], [VMEM] * 7,
        lines, t["outer"], t["twist_cos"], t["twist_sin"], t["inner"], t["first"], ratio,
    )
    ends = exchange(ends.reshape(16, 8, 128), "zc").reshape(128, 128)
    root, inside = call(reduce_kernel, [(128, 128), (128, 128)], [VMEM] * 2, ends, merge)
    roots = exchange(root.reshape(16, 8, 128), ("xl", "wall")).reshape(128, 128)
    outer = call(
        spread_kernel, [(128, 128)], [VMEM] * 3, roots, inside, merge,
        scratch=[pltpu.VMEM((128, 128), F32)],
    )
    outer = exchange(outer.reshape(16, 8, 128), "zc").reshape(128, 128)
    back = call(
        backward_kernel, [(512, 128)], [VMEM] * 8,
        outer, local, column, t["outer_back"], t["twist_cos"], t["twist_sin"], t["inner_back"], t["first_back"],
    )
    back = exchange(back.reshape(64, 8, 128), SPAN).reshape(512, 128)
    return call(place_kernel, [(2, SLAB, INNER)], [VMEM], back)


def solution(mesh):
    fine = Mesh(mesh.devices.reshape(2, 2, 16, 8), ("xh", "xl", "zc", "wall"))
    placed = (P(None, None, "wall", SPAN), P())
    return jax.shard_map(
        on_device, mesh=fine, in_specs=placed, out_specs=P(None, "wall", SPAN), check_vma=False
    )
```

```python
import jax
import jax.numpy as jnp
import numpy as np
from jax import lax
from jax.experimental import pallas as pl
from jax.experimental.pallas import tpu as pltpu
from jax.sharding import PartitionSpec as P

F32 = jnp.float32
EXACT = lax.Precision.HIGHEST
NY, NZ = 1536, 8192
WALLS, STRIPS = 8, 64
ROWS, COLS = NY // WALLS, NZ // STRIPS
HALF = ROWS // 2


def sine_table(n):
    i = np.arange(1, n + 1)
    return np.sqrt(2 / (n + 1)) * np.sin(np.pi * np.outer(i, i) / (n + 1)), 4 * np.sin(np.pi * i / (2 * (n + 1))) ** 2


def tables():
    sine_y, mu_box = sine_table(ROWS)
    sine_z, lam = sine_table(COLS)
    sine_wide = np.zeros((ROWS, 256))
    sine_wide[:, :ROWS] = sine_y
    ends_y = np.zeros((8, ROWS))
    ends_y[0], ends_y[1] = sine_y[0], sine_y[-1]
    ends_z = np.zeros((8, COLS))
    ends_z[0], ends_z[1] = sine_z[0], sine_z[-1]
    edge_w = np.zeros((8, COLS))
    edge_w[0, 0], edge_w[1, -1] = -0.5, 0.5
    ends_tile = np.zeros((8, COLS))
    ends_tile[4] = ends_tile[6] = sine_z[0]
    ends_tile[5] = ends_tile[7] = sine_z[-1]
    r = np.arange(ROWS)
    wall = np.arange(WALLS)
    cosine = np.zeros((WALLS, 2 * ROWS, ROWS))
    fold = np.zeros((WALLS, 16, 64))
    spread = np.zeros((WALLS, 64, 16))
    ghost = np.zeros((WALLS, 64, ROWS))
    mu_col = np.zeros((WALLS, ROWS, COLS))
    mu_lane = np.zeros((WALLS, 24, COLS))
    for c in range(WALLS):
        mode = (c + 8 * np.arange(2)[:, None] + 16 * np.arange(HALF)[None, :]).reshape(-1)
        norm = np.where(mode == 0, np.sqrt(1 / NY), np.sqrt(2 / NY))
        angle = np.pi * np.outer(2 * r + 1, mode) / (2 * NY)
        cosine[c, :ROWS] = norm * np.cos(angle)
        cosine[c, ROWS:] = norm * np.sin(angle)
        for par in range(2):
            turn = np.pi * (c + 8 * par) * wall / 8
            for line in range(4):
                for w in range(WALLS):
                    for s in (line, line + 4):
                        fold[c, 4 * par + line, 8 * w + s] = np.cos(turn[w])
                        fold[c, 8 + 4 * par + line, 8 * w + s] = -np.sin(turn[w])
                    spread[c, 8 * w + line, 4 * par + line] = np.cos(turn[w])
                    spread[c, 8 * w + line, 8 + 4 * par + line] = -np.sin(turn[w])
        for w in range(WALLS):
            for g, y in enumerate((ROWS * w - 1, ROWS * (w + 1))):
                row = norm * np.cos(np.pi * mode * (2 * y + 1) / (2 * NY))
                ghost[c, 8 * w + 4 + g] = ghost[c, 8 * w + 6 + g] = row
        mu = 4 * np.sin(np.pi * mode / (2 * NY)) ** 2
        mu_col[c] = mu[:, None]
        six = np.stack([mu[:128]] * 4 + [np.concatenate([mu[128:], mu[128:]])] * 2)
        mu_lane[c] = np.concatenate([six] * 4)
    names = dict(
        sine_y=sine_y, sine_z=sine_z, sine_wide=sine_wide, ends_y=ends_y, ends_z=ends_z, edge_w=edge_w,
        ends_tile=ends_tile, both=mu_box[:, None] + lam[None, :], lam_col=np.repeat(lam[:, None], COLS, 1),
        lam_row=np.repeat(lam[None, :], 8, 0), cosine=cosine, fold=fold.reshape(-1, 64),
        spread=spread.reshape(-1, 16), ghost=ghost, mu_col=mu_col, mu_lane=mu_lane.reshape(-1, COLS),
    )
    return {key: np.asarray(value, np.float32) for key, value in names.items()}


def dot(a, b, dims=((1,), (0,))):
    return lax.dot_general(a, b, (dims, ((), ())), precision=EXACT, preferred_element_type=F32)


def ids(shape, dim):
    return lax.broadcasted_iota(jnp.int32, shape, dim)


def box_kernel(wave_ref, vel_ref, both_ref, sine_y_ref, sine_z_ref, wide_ref, ends_y_ref, ends_z_ref, edge_ref, out_ref, freq_ref):
    shape = (ROWS, COLS)
    row, lane = ids(shape, 0), ids(shape, 1)
    wall = lax.axis_index("wall")
    low = jnp.where(wall > 0, -0.5, 0.0)
    high = jnp.where(wall < WALLS - 1, 0.5, 0.0)
    sine_y, sine_z = sine_y_ref[...], sine_z_ref[...]
    edges, firsts, lasts = [], [], []
    for plane in range(2):
        u, v, w = (vel_ref[c, plane] for c in range(3))
        above = jnp.where(row == ROWS - 1, 0.0, pltpu.roll(v, ROWS - 1, 0))
        below = jnp.where(row == 0, 0.0, pltpu.roll(v, 1, 0))
        after = jnp.where(lane == COLS - 1, 0.0, pltpu.roll(w, COLS - 1, 1))
        before = jnp.where(lane == 0, 0.0, pltpu.roll(w, 1, 1))
        wave = wave_ref[plane]
        source = wave * u + 0.5 * ((above - below) + (after - before))
        freq = dot(dot(sine_y, source), sine_z)
        freq_ref[ROWS * plane : ROWS * (plane + 1), :] = freq
        inside = -freq / (wave * wave + both_ref[...])
        edge = dot(dot(ends_z_ref[...], inside, ((1,), (1,))), wide_ref[...])
        halo = dot(edge_ref[...], w, ((1,), (1,)))
        edge = edge + jnp.concatenate([halo, jnp.zeros((8, 256 - ROWS), F32)], 1)
        edges.append(edge[0:2])
        ends = dot(ends_y_ref[...], inside)
        rims = jnp.concatenate([low * v[0:1], high * v[ROWS - 1 :], jnp.zeros((6, COLS), F32)], 0)
        ends = ends + dot(rims, sine_z)
        firsts += [ends[0:1]] * 2
        lasts += [ends[1:2]] * 2
    tile = jnp.concatenate(edges + [jnp.concatenate([jnp.concatenate(firsts, 0), jnp.concatenate(lasts, 0)], 1)], 0)
    for w in range(WALLS):
        out_ref[8 * w : 8 * w + 8, :] = tile


def decay(shift):
    root = jnp.sqrt(shift * (shift + 4.0))
    delta = (shift + root) / (2.0 + shift + root)
    return 1.0 - delta, delta * (2.0 - delta), -jnp.log1p(-delta)


def factor_kernel(
    wave_ref, both_ref, lam_col_ref, lam_row_ref, mu_lane_ref, mu_col_ref, cosine_ref,
    solve_ref, reach_ref, chain_ref, cauchy_ref, left_ref, right_ref, mine_ref, mu_ref, sems,
):
    strip, wall = lax.axis_index("span"), lax.axis_index("wall")
    copies = [
        pltpu.make_async_copy(cosine_ref.at[wall], mine_ref, sems.at[0]),
        pltpu.make_async_copy(mu_col_ref.at[wall], mu_ref, sems.at[1]),
    ]
    for copy in copies:
        copy.start()
    waves = [wave_ref[p] * wave_ref[p] for p in range(2)]
    cell = ids((COLS, 256), 1)
    inside = cell < ROWS
    for p in range(2):
        solve_ref[ROWS * p : ROWS * (p + 1), :] = -1.0 / (waves[p] + both_ref[...])
        _, _, theta = decay(waves[p] + lam_col_ref[...])
        theta = jnp.concatenate([theta, theta], 1)
        whole = 1.0 / (1.0 - jnp.exp(-(2.0 * (ROWS + 1)) * theta))
        for side in range(2):
            step = jnp.where(inside, cell if side == 0 else ROWS - 1 - cell, 0).astype(F32)
            value = jnp.exp(-(step + 1.0) * theta) * (1.0 - jnp.exp(-2.0 * (ROWS - step) * theta)) * whole
            at = COLS * (2 * p + side)
            reach_ref[at : at + COLS, :] = jnp.where(inside, value, 0.0)
    row = ids((8, COLS), 0)
    rho, gap, theta = decay(jnp.where(row >= 6, waves[1], waves[0]) + lam_row_ref[...])
    period = 1.0 - jnp.exp(-2.0 * NY * theta)
    chain_ref[0] = rho
    chain_ref[1] = jnp.exp(-1.0 * ROWS * theta)
    chain_ref[2] = jnp.exp(-1.0 * (ROWS + 1) * theta)
    chain_ref[3] = jnp.where(row >= 4, 1.0 / (gap * period), 0.0)
    chain_ref[4] = period
    shape = (24, COLS)
    row, lane = ids(shape, 0), ids(shape, 1)
    place = row % 6
    second = jnp.logical_or(place // 2 == 1, jnp.logical_and(place >= 4, lane >= 64))
    mu = mu_lane_ref[pl.ds(pl.multiple_of(24 * wall, 8), 24), :]
    rho, gap, theta = decay(jnp.where(second, waves[1], waves[0]) + mu)
    scale = 1.0 / (gap * (1.0 - jnp.exp(-1.0 * NZ * theta)))
    cross = jnp.exp(-(COLS + 1.0) * theta)
    step = -1.0 * COLS * theta
    first = place % 2 == 0

    def reach(n):
        return jnp.exp(step * lax.bitwise_and(n, STRIPS - 1).astype(F32))

    for group in range(16):
        other = 4 * group + row // 6
        rows = slice(24 * group, 24 * (group + 1))
        coming, own = reach(strip - 1 - other), rho * reach(other - strip)
        left_ref[rows, :] = scale * jnp.where(first, cross * coming + own, coming + cross * own)
        own, coming = rho * reach(strip - other), reach(other - strip - 1)
        right_ref[rows, :] = scale * jnp.where(first, cross * own + coming, own + cross * coming)
    for copy in copies:
        copy.wait()
    for p in range(2):
        rows = slice(ROWS * p, ROWS * (p + 1))
        cauchy_ref[rows, :] = 1.0 / (mu_ref[...] + (waves[p] + lam_row_ref[0:1, :]))


def strip_kernel(in_ref, chain_ref, reach_ref, ends_ref, fold_ref, mine_ref, out_ref, own_ref, lows_ref, highs_ref):
    wall = lax.axis_index("wall")
    rho, block, cross, scale, period = (chain_ref[i] for i in range(5))
    up, down = [], []
    for w in range(WALLS):
        first, last = in_ref[8 * w : 8 * w + 8, 0:COLS], in_ref[8 * w : 8 * w + 8, COLS : 2 * COLS]
        up.append(last + cross * first)
        down.append(first + cross * last)
    seq = up + down[::-1]
    carry = seq[0]
    for i in range(1, 2 * WALLS):
        carry = carry * block + seq[i]
    sums = [carry]
    for i in range(2 * WALLS - 1):
        sums.append(block * sums[-1] + seq[i] * period)
    sums.append(sums[0])
    row = ids((8, COLS), 0)
    ends = ends_ref[...]
    parts = []
    for w in range(WALLS):
        low = scale * (sums[w] + rho * sums[2 * WALLS - w])
        high = scale * (rho * sums[w + 1] + sums[2 * WALLS - 1 - w])
        lows_ref[8 * w : 8 * w + 8, :] = low
        highs_ref[8 * w : 8 * w + 8, :] = high
        low, high = low * ends, high * ends
        planes = [jnp.where(row < 6, t, 0.0) for t in (low, high)] + [jnp.where(row < 6, 0.0, t) for t in (low, high)]
        parts.append(jnp.concatenate(planes, 1))
    mine = pl.ds(pl.multiple_of(8 * wall, 8), 8)
    own_ref[...] = jnp.where(row % 2 == 0, lows_ref[mine, :], highs_ref[mine, :])
    added = dot(jnp.concatenate(parts, 0), reach_ref[...])
    lines = jnp.where(ids((64, 256), 0) % 8 < 4, in_ref[...], added)
    folded = dot(fold_ref[pl.ds(pl.multiple_of(16 * wall, 16), 16), :], lines)
    modes = dot(folded[0:8, :ROWS], mine_ref[:ROWS, :]) + dot(folded[8:16, :ROWS], mine_ref[ROWS:, :])
    modes = jnp.where(ids((4, ROWS), 1) < HALF, modes[0:4], modes[4:8])
    tail = modes[:, COLS:]
    six = jnp.concatenate([modes[:, :COLS], jnp.concatenate([tail[0:2], tail[2:4]], 1)], 0)
    out = jnp.concatenate([six] * 4, 0)
    for group in range(16):
        out_ref[24 * group : 24 * (group + 1), :] = out


def ring_kernel(in_ref, left_ref, right_ref, mine_ref, spread_ref, ghost_ref, cauchy_ref, ends_z_ref, out_ref):
    wall = lax.axis_index("wall")
    pairs = []
    for weight_ref in (left_ref, right_ref):
        total = in_ref[0:24, :] * weight_ref[0:24, :]
        for group in range(1, 16):
            rows = slice(24 * group, 24 * (group + 1))
            total = total + in_ref[rows, :] * weight_ref[rows, :]
        six = (total[0:6] + total[6:12]) + (total[12:18] + total[18:24])
        pairs.append([six[2 * i : 2 * i + 1] + six[2 * i + 1 : 2 * i + 2] for i in range(3)])
    lines = []
    for plane in range(2):
        for side in range(2):
            tail = pairs[side][2][:, 64 * plane : 64 * plane + 64]
            lines.append(jnp.concatenate([pairs[side][plane], tail], 1))
    four = jnp.concatenate(lines, 0)
    even = ids((4, ROWS), 1) < HALF
    eight = jnp.concatenate([jnp.where(even, four, 0.0), jnp.where(even, 0.0, four)], 0)
    cells = [dot(eight, mine_ref[ROWS * k : ROWS * (k + 1), :], ((1,), (1,))) for k in range(2)]
    back = dot(spread_ref[pl.ds(pl.multiple_of(64 * wall, 64), 64), :], jnp.concatenate(cells, 0))
    ghost = ghost_ref[wall]
    rims = []
    for plane in range(2):
        both = jnp.concatenate([ghost * lines[2 * plane], ghost * lines[2 * plane + 1]], 0)
        both = dot(both, cauchy_ref[ROWS * plane : ROWS * (plane + 1), :])
        rims.append(both[:64] * ends_z_ref[0:1, :] + both[64:] * ends_z_ref[1:2, :])
    rim = jnp.where(ids((64, COLS), 0) % 8 < 6, rims[0], rims[1])
    out_ref[:, :COLS] = back[:, :COLS] + rim
    out_ref[:, COLS:] = jnp.concatenate([back[:, COLS:], jnp.zeros((64, 256 - ROWS), F32)], 1)


def final_kernel(in_ref, own_ref, freq_ref, solve_ref, sine_y_ref, sine_z_ref, ends_y_ref, ends_z_ref, out_ref):
    total = in_ref[0:8, :]
    for w in range(1, WALLS):
        total = total + in_ref[8 * w : 8 * w + 8, :]
    sine_y, sine_z = sine_y_ref[...], sine_z_ref[...]
    sides = dot(total[:, :ROWS], sine_y)
    rims = total[:, :COLS] + own_ref[...]
    for plane in range(2):
        rows = slice(ROWS * plane, ROWS * (plane + 1))
        lhs = jnp.concatenate([ends_y_ref[0:2, :], sides[2 * plane : 2 * plane + 2], jnp.zeros((4, ROWS), F32)], 0)
        rhs = jnp.concatenate([rims[4 + 2 * plane : 6 + 2 * plane], ends_z_ref[0:2, :], jnp.zeros((4, COLS), F32)], 0)
        freq = (freq_ref[rows, :] - dot(lhs, rhs, ((0,), (0,)))) * solve_ref[rows, :]
        out_ref[plane] = dot(dot(sine_y, freq), sine_z)


SMEM = pl.BlockSpec(memory_space=pltpu.SMEM)
VMEM = pl.BlockSpec(memory_space=pltpu.VMEM)
ANY = pl.BlockSpec(memory_space=pl.ANY)


def call(kernel, shapes, specs, *operands, scratch=()):
    outs = [jax.ShapeDtypeStruct(s, F32) for s in shapes]
    return pl.pallas_call(
        kernel,
        out_shape=outs if len(outs) > 1 else outs[0],
        in_specs=specs,
        out_specs=[VMEM] * len(outs) if len(outs) > 1 else VMEM,
        scratch_shapes=list(scratch),
        compiler_params=pltpu.CompilerParams(vmem_limit_bytes=24 << 20),
    )(*operands)


def exchange(block, axes):
    return lax.all_to_all(block, axes, split_axis=0, concat_axis=0, tiled=True)


def on_device(velocity, wave_x):
    t = {key: jnp.asarray(value) for key, value in tables().items()}
    sent, freq = call(
        box_kernel, [(64, 256), (2 * ROWS, COLS)], [SMEM] + [VMEM] * 8,
        wave_x, velocity, t["both"], t["sine_y"], t["sine_z"], t["sine_wide"], t["ends_y"], t["ends_z"], t["edge_w"],
    )
    solve, reach, chain, cauchy, left, right, mine = call(
        factor_kernel,
        [(2 * ROWS, COLS), (4 * COLS, 256), (5, 8, COLS), (2 * ROWS, COLS), (384, COLS), (384, COLS), (2 * ROWS, ROWS)],
        [SMEM] + [VMEM] * 4 + [ANY] * 2,
        wave_x, t["both"], t["lam_col"], t["lam_row"], t["mu_lane"], t["mu_col"], t["cosine"],
        scratch=[pltpu.VMEM((ROWS, COLS), F32), pltpu.SemaphoreType.DMA((2,))],
    )
    sent = exchange(sent.reshape(8, 8, 256), "wall").reshape(64, 256)
    modes, own = call(
        strip_kernel, [(384, COLS), (8, COLS)], [VMEM] * 6,
        sent, chain, reach, t["ends_tile"], t["fold"], mine,
        scratch=[pltpu.VMEM((64, COLS), F32)] * 2,
    )
    modes = exchange(modes.reshape(192, 2, COLS), "span").reshape(384, COLS)
    back = call(
        ring_kernel, [(64, 256)], [VMEM] * 8,
        modes, left, right, mine, t["spread"], t["ghost"], cauchy, t["ends_z"],
    )
    back = exchange(back.reshape(8, 8, 256), "wall").reshape(64, 256)
    return call(
        final_kernel, [(2, ROWS, COLS)], [VMEM] * 8,
        back, own, freq, solve, t["sine_y"], t["sine_z"], t["ends_y"], t["ends_z"],
    )


def solution(mesh):
    placed = (P(None, None, "wall", "span"), P())
    return jax.shard_map(
        on_device, mesh=mesh, in_specs=placed, out_specs=P(None, "wall", "span"), check_vma=False
    )
```

```python
import jax
import jax.numpy as jnp
import numpy as np
from jax import lax
from jax.experimental import pallas as pl
from jax.experimental.pallas import tpu as pltpu
from jax.sharding import PartitionSpec as P

F32 = jnp.float32
BF16 = jnp.bfloat16
EXACT = lax.Precision.HIGHEST
NY, NZ = 1536, 8192
WALLS, STRIPS = 8, 64
ROWS, COLS = NY // WALLS, NZ // STRIPS
HALF = ROWS // 2
SINE_Z, PICK, ENDS, BOX_ROWS = 384, 512, 768, 784
GHOST, WIDE_ROWS = 384, 448
SPREAD, FOLD, MU_LANE, NARROW_ROWS = 192, 256, 272, 296
LAM_ROW, ENDS_TILE, ENDS_Z, ENDS_Y, SHARED_ROWS = 128, 136, 144, 152, 168


def halves(table):
    high = table.astype(np.float32).astype(jnp.bfloat16).astype(np.float64)
    return high, table - high


def sine_table(n):
    i = np.arange(1, n + 1)
    return np.sqrt(2 / (n + 1)) * np.sin(np.pi * np.outer(i, i) / (n + 1)), 4 * np.sin(np.pi * i / (2 * (n + 1))) ** 2


def tables():
    sine_y, mu_box = sine_table(ROWS)
    sine_z, lam = sine_table(COLS)
    ends_tile = np.zeros((8, COLS))
    ends_tile[4] = ends_tile[6] = sine_z[0]
    ends_tile[5] = ends_tile[7] = sine_z[-1]
    r = np.arange(ROWS)
    wall = np.arange(WALLS)
    cosine = np.zeros((WALLS, 2 * ROWS, ROWS))
    fold = np.zeros((WALLS, 16, 64))
    spread = np.zeros((WALLS, 64, 16))
    ghost = np.zeros((WALLS, 64, ROWS))
    mu_col = np.zeros((WALLS, ROWS, COLS))
    mu_lane = np.zeros((WALLS, 24, COLS))
    for c in range(WALLS):
        mode = (c + 8 * np.arange(2)[:, None] + 16 * np.arange(HALF)[None, :]).reshape(-1)
        norm = np.where(mode == 0, np.sqrt(1 / NY), np.sqrt(2 / NY))
        angle = np.pi * np.outer(2 * r + 1, mode) / (2 * NY)
        cosine[c, :ROWS] = norm * np.cos(angle)
        cosine[c, ROWS:] = norm * np.sin(angle)
        for par in range(2):
            turn = np.pi * (c + 8 * par) * wall / 8
            for line in range(4):
                for w in range(WALLS):
                    for s in (line, line + 4):
                        fold[c, 4 * par + line, 8 * w + s] = np.cos(turn[w])
                        fold[c, 8 + 4 * par + line, 8 * w + s] = -np.sin(turn[w])
                    spread[c, 8 * w + line, 4 * par + line] = np.cos(turn[w])
                    spread[c, 8 * w + line, 8 + 4 * par + line] = -np.sin(turn[w])
        for w in range(WALLS):
            for g, y in enumerate((ROWS * w - 1, ROWS * (w + 1))):
                row = norm * np.cos(np.pi * mode * (2 * y + 1) / (2 * NY))
                ghost[c, 8 * w + 4 + g] = ghost[c, 8 * w + 6 + g] = row
        mu = 4 * np.sin(np.pi * mode / (2 * NY)) ** 2
        mu_col[c] = mu[:, None]
        six = np.stack([mu[:128]] * 4 + [np.concatenate([mu[128:], mu[128:]])] * 2)
        mu_lane[c] = np.concatenate([six] * 4)
    sine = np.zeros((2 * ROWS, 256))
    sine[:ROWS, :ROWS], sine[ROWS:, :ROWS] = halves(sine_y)
    pick = np.zeros((2 * COLS, COLS))
    for plane in range(2):
        pick[COLS * plane : COLS * (plane + 1), 2 * plane] = sine_z[0]
        pick[COLS * plane : COLS * (plane + 1), 2 * plane + 1] = sine_z[-1]
    ends = np.zeros((16, 256))
    ends[0:2, :ROWS], ends[8:10, :ROWS] = halves(sine_y[[0, -1]])
    boxes = np.concatenate([sine, np.concatenate(halves(sine_z), 1), np.concatenate(halves(pick), 1), ends])
    wide = np.zeros((WALLS, WIDE_ROWS, 256))
    wide[:, :GHOST, :ROWS], wide[:, GHOST:, :ROWS] = cosine, ghost
    narrow = np.zeros((WALLS, NARROW_ROWS, COLS))
    narrow[:, :SPREAD], narrow[:, SPREAD:FOLD, :16] = mu_col, spread
    narrow[:, FOLD:MU_LANE, :64], narrow[:, MU_LANE:] = fold, mu_lane
    ends_z = np.zeros((8, COLS))
    ends_z[0], ends_z[1] = sine_z[0], sine_z[-1]
    ends_y = np.zeros((8, 256))
    ends_y[0, :ROWS], ends_y[1, :ROWS] = sine_y[0], sine_y[-1]
    shared = np.concatenate([np.repeat(lam[:, None], COLS, 1), np.repeat(lam[None], 8, 0), ends_tile, ends_z, ends_y[:, :COLS], ends_y[:, COLS:]])
    both = mu_box[:, None] + lam[None, :]
    names = dict(both=both, wide=wide, narrow=narrow, shared=shared)
    return {key: np.asarray(value, np.float32) for key, value in names.items()}, np.asarray(boxes, np.float32)


def dot(a, b, dims=((1,), (0,))):
    return lax.dot_general(a, b, (dims, ((), ())), precision=EXACT, preferred_element_type=F32)


def ids(shape, dim):
    return lax.broadcasted_iota(jnp.int32, shape, dim)


def parts(value):
    high = value.astype(BF16).astype(F32)
    return [high.astype(BF16), (value - high).astype(BF16)]


def stacked(value):
    high = value.astype(BF16).astype(F32)
    return jnp.concatenate([high, value - high], 0).astype(BF16)


def joined(product, rows, at):
    here, beside = slice(at, at + COLS), slice(at + COLS, at + 2 * COLS)
    return product[:rows, here] + (product[:rows, beside] + product[rows:, here])


def fast(a, b):
    return jnp.dot(a, b, preferred_element_type=F32)


def box_kernel(
    wave_hbm, vel_hbm, both_hbm, boxes_hbm,
    out_ref, freq_ref, solve_ref, boxes_ref,
    wave_ref, vel_ref, both_ref, sems,
):
    pairs = [
        (wave_hbm, wave_ref), (both_hbm, both_ref),
        (vel_hbm.at[:, 0], vel_ref.at[:, 0]), (vel_hbm.at[:, 1], vel_ref.at[:, 1]), (boxes_hbm, boxes_ref),
    ]
    copies = [pltpu.make_async_copy(*pair, sems.at[i]) for i, pair in enumerate(pairs)]
    for copy in copies:
        copy.start()
    row, lane = ids((ROWS, COLS), 0), ids((ROWS, COLS), 1)
    wall = lax.axis_index("wall")
    low = jnp.where(wall > 0, -0.5, 0.0)
    high = jnp.where(wall < WALLS - 1, 0.5, 0.0)
    copies[0].wait()
    copies[1].wait()
    for plane in range(2):
        wave = wave_ref[plane]
        solve_ref[ROWS * plane : ROWS * (plane + 1), :] = -1.0 / (wave * wave + both_ref[...])
    sources, rims, halo = [], [], jnp.zeros((ROWS, COLS), F32)
    for plane in range(2):
        copies[2 + plane].wait()
        u, v, w = (vel_ref[c, plane] for c in range(3))
        above = jnp.where(row == ROWS - 1, 0.0, pltpu.roll(v, ROWS - 1, 0))
        below = jnp.where(row == 0, 0.0, pltpu.roll(v, 1, 0))
        after = jnp.where(lane == COLS - 1, 0.0, pltpu.roll(w, COLS - 1, 1))
        before = jnp.where(lane == 0, 0.0, pltpu.roll(w, 1, 1))
        sources += parts(wave_ref[plane] * u + 0.5 * ((above - below) + (after - before)))
        rims += [low * v[0:1], high * v[ROWS - 1 :]]
        for side in range(2):
            moved = pltpu.roll(w, 2 * plane + 2 * side, 1) if plane + side else w
            halo = jnp.where(lane == 2 * plane + side, (side - 0.5) * moved, halo)
    copies[4].wait()
    sine, sine_z = boxes_ref[:SINE_Z, :ROWS], boxes_ref[SINE_Z:PICK, :]
    product = fast(sine, jnp.concatenate(sources, 1))
    product = fast(jnp.concatenate([stacked(joined(product, ROWS, 256 * p)) for p in range(2)], 0), sine_z)
    insides = []
    for plane in range(2):
        freq = joined(product[2 * ROWS * plane : 2 * ROWS * (plane + 1)], ROWS, 0)
        rows = slice(ROWS * plane, ROWS * (plane + 1))
        freq_ref[rows, :] = freq
        insides.append(parts(freq * solve_ref[rows, :]))
    ends = fast(boxes_ref[ENDS:BOX_ROWS, :ROWS], jnp.concatenate(insides[0] + insides[1], 1))
    ends = [joined(ends, 8, 256 * p)[0:2] for p in range(2)]
    rims = fast(stacked(jnp.concatenate(rims + [jnp.zeros((4, COLS), F32)], 0)), sine_z)
    ends = jnp.concatenate(ends, 0) + joined(rims, 8, 0)[0:4]
    cols = jnp.concatenate([jnp.concatenate([insides[0][k], insides[1][k]], 1) for k in range(2)], 0)
    cols = joined(fast(cols, boxes_ref[PICK:ENDS, :]), ROWS, 0)
    cols = joined(fast(sine, jnp.concatenate(parts(cols), 1)), ROWS, 0) + halo
    edges = jnp.concatenate([cols, jnp.zeros((256 - ROWS, COLS), F32)], 0).T[0:4]
    tile = [jnp.concatenate([ends[i : i + 1], ends[i + 1 : i + 2]], 1) for i in (0, 0, 2, 2)]
    tile = jnp.concatenate([edges] + tile, 0)
    for w in range(WALLS):
        out_ref[8 * w : 8 * w + 8, :] = tile


def decay(shift):
    root = jnp.sqrt(shift * (shift + 4.0))
    delta = (shift + root) / (2.0 + shift + root)
    return 1.0 - delta, delta * (2.0 - delta), -jnp.log1p(-delta)


def factor_kernel(
    wave_hbm, wide_hbm, narrow_hbm, shared_hbm,
    reach_ref, chain_ref, cauchy_ref, left_ref, right_ref, wide_ref, narrow_ref, shared_ref,
    wave_ref, sems,
):
    strip, wall = lax.axis_index("span"), lax.axis_index("wall")
    pairs = [(wave_hbm, wave_ref), (shared_hbm, shared_ref), (narrow_hbm.at[wall], narrow_ref), (wide_hbm.at[wall], wide_ref)]
    copies = [pltpu.make_async_copy(*pair, sems.at[i]) for i, pair in enumerate(pairs)]
    for copy in copies:
        copy.start()
    for copy in copies[:3]:
        copy.wait()
    waves = [wave_ref[p] * wave_ref[p] for p in range(2)]
    cell = ids((COLS, 256), 1)
    inside = cell < ROWS
    for p in range(2):
        _, _, theta = decay(waves[p] + shared_ref[:LAM_ROW, :])
        theta = jnp.concatenate([theta, theta], 1)
        whole = 1.0 / (1.0 - jnp.exp(-(2.0 * (ROWS + 1)) * theta))
        for side in range(2):
            step = jnp.where(inside, cell if side == 0 else ROWS - 1 - cell, 0).astype(F32)
            value = jnp.exp(-(step + 1.0) * theta) * (1.0 - jnp.exp(-2.0 * (ROWS - step) * theta)) * whole
            at = COLS * (2 * p + side)
            reach_ref[at : at + COLS, :] = jnp.where(inside, value, 0.0)
    row = ids((8, COLS), 0)
    rho, gap, theta = decay(jnp.where(row >= 6, waves[1], waves[0]) + shared_ref[LAM_ROW:ENDS_TILE, :])
    period = 1.0 - jnp.exp(-2.0 * NY * theta)
    chain_ref[0] = rho
    chain_ref[1] = jnp.exp(-1.0 * ROWS * theta)
    chain_ref[2] = jnp.exp(-1.0 * (ROWS + 1) * theta)
    chain_ref[3] = jnp.where(row >= 4, 1.0 / (gap * period), 0.0)
    chain_ref[4] = period
    shape = (24, COLS)
    row, lane = ids(shape, 0), ids(shape, 1)
    place = row % 6
    second = jnp.logical_or(place // 2 == 1, jnp.logical_and(place >= 4, lane >= 64))
    rho, gap, theta = decay(jnp.where(second, waves[1], waves[0]) + narrow_ref[MU_LANE:, :])
    scale = 1.0 / (gap * (1.0 - jnp.exp(-1.0 * NZ * theta)))
    cross = jnp.exp(-(COLS + 1.0) * theta)
    step = -1.0 * COLS * theta
    first = place % 2 == 0

    def reach(n):
        return jnp.exp(step * lax.bitwise_and(n, STRIPS - 1).astype(F32))

    for group in range(16):
        other = 4 * group + row // 6
        rows = slice(24 * group, 24 * (group + 1))
        coming, own = reach(strip - 1 - other), rho * reach(other - strip)
        left_ref[rows, :] = scale * jnp.where(first, cross * coming + own, coming + cross * own)
        own, coming = rho * reach(strip - other), reach(other - strip - 1)
        right_ref[rows, :] = scale * jnp.where(first, cross * own + coming, own + cross * coming)
    for p in range(2):
        rows = slice(ROWS * p, ROWS * (p + 1))
        cauchy_ref[rows, :] = 1.0 / (narrow_ref[:SPREAD, :] + (waves[p] + shared_ref[LAM_ROW : LAM_ROW + 1, :]))
    copies[3].wait()


def strip_kernel(in_ref, chain_ref, reach_ref, wide_ref, narrow_ref, shared_ref, out_ref, own_ref, lows_ref, highs_ref):
    wall = lax.axis_index("wall")
    rho, block, cross, scale, period = (chain_ref[i] for i in range(5))
    up, down = [], []
    for w in range(WALLS):
        first, last = in_ref[8 * w : 8 * w + 8, 0:COLS], in_ref[8 * w : 8 * w + 8, COLS : 2 * COLS]
        up.append(last + cross * first)
        down.append(first + cross * last)
    seq = up + down[::-1]
    carry = seq[0]
    for i in range(1, 2 * WALLS):
        carry = carry * block + seq[i]
    sums = [carry]
    for i in range(2 * WALLS - 1):
        sums.append(block * sums[-1] + seq[i] * period)
    sums.append(sums[0])
    row = ids((8, COLS), 0)
    ends = shared_ref[ENDS_TILE:ENDS_Z, :]
    blocks = []
    for w in range(WALLS):
        low = scale * (sums[w] + rho * sums[2 * WALLS - w])
        high = scale * (rho * sums[w + 1] + sums[2 * WALLS - 1 - w])
        lows_ref[8 * w : 8 * w + 8, :] = low
        highs_ref[8 * w : 8 * w + 8, :] = high
        low, high = low * ends, high * ends
        planes = [jnp.where(row < 6, t, 0.0) for t in (low, high)] + [jnp.where(row < 6, 0.0, t) for t in (low, high)]
        blocks.append(jnp.concatenate(planes, 1))
    mine = pl.ds(pl.multiple_of(8 * wall, 8), 8)
    own_ref[...] = jnp.where(row % 2 == 0, lows_ref[mine, :], highs_ref[mine, :])
    added = dot(jnp.concatenate(blocks, 0), reach_ref[...])
    lines = jnp.where(ids((64, 256), 0) % 8 < 4, in_ref[...], added)
    folded = dot(narrow_ref[FOLD:MU_LANE, :64], lines)
    modes = dot(folded[0:8, :ROWS], wide_ref[:ROWS, :ROWS]) + dot(folded[8:16, :ROWS], wide_ref[ROWS:GHOST, :ROWS])
    modes = jnp.where(ids((4, ROWS), 1) < HALF, modes[0:4], modes[4:8])
    tail = modes[:, COLS:]
    six = jnp.concatenate([modes[:, :COLS], jnp.concatenate([tail[0:2], tail[2:4]], 1)], 0)
    out = jnp.concatenate([six] * 4, 0)
    for group in range(16):
        out_ref[24 * group : 24 * (group + 1), :] = out


def ring_kernel(in_ref, left_ref, right_ref, wide_ref, narrow_ref, cauchy_ref, shared_ref, out_ref):
    pairs = []
    for weight_ref in (left_ref, right_ref):
        total = in_ref[0:24, :] * weight_ref[0:24, :]
        for group in range(1, 16):
            rows = slice(24 * group, 24 * (group + 1))
            total = total + in_ref[rows, :] * weight_ref[rows, :]
        six = (total[0:6] + total[6:12]) + (total[12:18] + total[18:24])
        pairs.append([six[2 * i : 2 * i + 1] + six[2 * i + 1 : 2 * i + 2] for i in range(3)])
    lines = []
    for plane in range(2):
        for side in range(2):
            tail = pairs[side][2][:, 64 * plane : 64 * plane + 64]
            lines.append(jnp.concatenate([pairs[side][plane], tail], 1))
    four = jnp.concatenate(lines, 0)
    even = ids((4, ROWS), 1) < HALF
    eight = jnp.concatenate([jnp.where(even, four, 0.0), jnp.where(even, 0.0, four)], 0)
    cells = [dot(eight, wide_ref[ROWS * k : ROWS * (k + 1), :ROWS], ((1,), (1,))) for k in range(2)]
    back = dot(narrow_ref[SPREAD:FOLD, :16], jnp.concatenate(cells, 0))
    ghost = wide_ref[GHOST:, :ROWS]
    ends = shared_ref[ENDS_Z : ENDS_Z + 2, :]
    rims = []
    for plane in range(2):
        both = jnp.concatenate([ghost * lines[2 * plane], ghost * lines[2 * plane + 1]], 0)
        both = dot(both, cauchy_ref[ROWS * plane : ROWS * (plane + 1), :])
        rims.append(both[:64] * ends[0:1] + both[64:] * ends[1:2])
    rim = jnp.where(ids((64, COLS), 0) % 8 < 6, rims[0], rims[1])
    out_ref[:, :COLS] = back[:, :COLS] + rim
    out_ref[:, COLS:] = jnp.concatenate([back[:, COLS:], jnp.zeros((64, 256 - ROWS), F32)], 1)


def final_kernel(in_ref, own_ref, freq_ref, solve_ref, boxes_ref, shared_ref, out_ref):
    total = in_ref[0:8, :]
    for w in range(1, WALLS):
        total = total + in_ref[8 * w : 8 * w + 8, :]
    sine, sine_z = boxes_ref[:SINE_Z, :ROWS], boxes_ref[SINE_Z:PICK, :]
    both = stacked(total[:, :ROWS])
    sides = fast(both, boxes_ref[:ROWS, :])
    sides = sides[0:8] + (sides[8:16] + fast(both, boxes_ref[ROWS:SINE_Z, :])[0:8])
    rims = total[:, :COLS] + own_ref[...]
    ends_y = jnp.concatenate([shared_ref[ENDS_Y : ENDS_Y + 2, :], shared_ref[ENDS_Y + 8 : ENDS_Y + 10, :]], 1)
    freqs = []
    for plane in range(2):
        rows = slice(ROWS * plane, ROWS * (plane + 1))
        lhs = jnp.concatenate([ends_y, sides[2 * plane : 2 * plane + 2], jnp.zeros((4, 256), F32)], 0)[:, :ROWS]
        rhs = jnp.concatenate([rims[4 + 2 * plane : 6 + 2 * plane], shared_ref[ENDS_Z : ENDS_Z + 2, :], jnp.zeros((4, COLS), F32)], 0)
        freqs.append(stacked((freq_ref[rows, :] - dot(lhs, rhs, ((0,), (0,)))) * solve_ref[rows, :]))
    product = fast(jnp.concatenate(freqs, 0), sine_z)
    lines = [parts(joined(product[2 * ROWS * p : 2 * ROWS * (p + 1)], ROWS, 0)) for p in range(2)]
    product = fast(sine, jnp.concatenate(lines[0] + lines[1], 1))
    for plane in range(2):
        out_ref[plane] = joined(product, ROWS, 256 * plane)


SMEM = pl.BlockSpec(memory_space=pltpu.SMEM)
VMEM = pl.BlockSpec(memory_space=pltpu.VMEM)
HBM = pl.BlockSpec(memory_space=pltpu.HBM)


def call(kernel, shapes, specs, *operands, scratch=()):
    outs = [s if isinstance(s, jax.ShapeDtypeStruct) else jax.ShapeDtypeStruct(s, F32) for s in shapes]
    return pl.pallas_call(
        kernel,
        out_shape=outs if len(outs) > 1 else outs[0],
        in_specs=specs,
        out_specs=[VMEM] * len(outs) if len(outs) > 1 else VMEM,
        scratch_shapes=list(scratch),
        compiler_params=pltpu.CompilerParams(vmem_limit_bytes=24 << 20),
    )(*(pltpu.with_memory_space_constraint(x, pltpu.HBM) if s is HBM else x for s, x in zip(specs, operands)))


def exchange(block, axes):
    return lax.all_to_all(block, axes, split_axis=0, concat_axis=0, tiled=True)


def on_device(velocity, wave_x):
    names, boxes = tables()
    t = {key: jnp.asarray(value) for key, value in names.items()}
    sent, freq, solve, boxes = call(
        box_kernel,
        [(64, 256), (2 * ROWS, COLS), (2 * ROWS, COLS), jax.ShapeDtypeStruct((BOX_ROWS, 256), BF16)],
        [HBM] * 4, wave_x, velocity, t["both"], jnp.asarray(boxes, BF16),
        scratch=[
            pltpu.SMEM((2,), F32), pltpu.VMEM((3, 2, ROWS, COLS), F32), pltpu.VMEM((ROWS, COLS), F32),
            pltpu.SemaphoreType.DMA((5,)),
        ],
    )
    reach, chain, cauchy, left, right, wide, narrow, shared = call(
        factor_kernel,
        [
            (4 * COLS, 256), (5, 8, COLS), (2 * ROWS, COLS), (384, COLS), (384, COLS),
            (WIDE_ROWS, 256), (NARROW_ROWS, COLS), (SHARED_ROWS, COLS),
        ],
        [HBM] * 4, wave_x, t["wide"], t["narrow"], t["shared"],
        scratch=[pltpu.SMEM((2,), F32), pltpu.SemaphoreType.DMA((4,))],
    )
    sent = exchange(sent.reshape(8, 8, 256), "wall").reshape(64, 256)
    modes, own = call(
        strip_kernel, [(384, COLS), (8, COLS)], [VMEM] * 6,
        sent, chain, reach, wide, narrow, shared,
        scratch=[pltpu.VMEM((64, COLS), F32)] * 2,
    )
    modes = exchange(modes.reshape(192, 2, COLS), "span").reshape(384, COLS)
    back = call(ring_kernel, [(64, 256)], [VMEM] * 7, modes, left, right, wide, narrow, cauchy, shared)
    back = exchange(back.reshape(8, 8, 256), "wall").reshape(64, 256)
    return call(final_kernel, [(2, ROWS, COLS)], [VMEM] * 6, back, own, freq, solve, boxes, shared)


def solution(mesh):
    placed = (P(None, None, "wall", "span"), P())
    return jax.shard_map(
        on_device, mesh=mesh, in_specs=placed, out_specs=P(None, "wall", "span"), check_vma=False
    )
```

```python
import jax
import jax.numpy as jnp
import numpy as np
from jax import lax
from jax.experimental import pallas as pl
from jax.experimental.pallas import tpu as pltpu
from jax.sharding import Mesh, PartitionSpec as P

F32 = jnp.float32
BF16 = jnp.bfloat16
EXACT = lax.Precision.HIGHEST
NY, NZ = 1536, 8192
WALLS, STRIPS = 8, 64
PAIRS, PEERS = STRIPS // 2, 2 * WALLS
ROWS, COLS = NY // WALLS, NZ // STRIPS
OWNED = NY // PEERS
CHUNK = 10
SINE_Z, ENDS, EDGES, PICK, BOX_ROWS = 384, 512, 528, 544, 560
GHOST, MU_ROW, MU_COL, CLASS_ROWS = 0, 32, 40, 168
SPREAD, MIX_ROWS = 32, 160
PHI, LAM_ROW, ENDS_Z, ENDS_Y, SHARED_ROWS = 128, 136, 144, 152, 160


def halves(table):
    high = table.astype(np.float32).astype(BF16).astype(np.float64)
    return high, table - high


def sine_table(n):
    i = np.arange(1, n + 1)
    return np.sqrt(2 / (n + 1)) * np.sin(np.pi * np.outer(i, i) / (n + 1)), 4 * np.sin(np.pi * i / (2 * (n + 1))) ** 2


def tables():
    sine_y, mu_box = sine_table(ROWS)
    sine_z, lam = sine_table(COLS)
    ends_y, ends_z = sine_y[[0, -1]], sine_z[[0, -1]]
    boxes = np.zeros((BOX_ROWS, 256))
    boxes[:ROWS, :ROWS], boxes[ROWS:SINE_Z, :ROWS] = halves(sine_y)
    boxes[SINE_Z:ENDS, :COLS], boxes[SINE_Z:ENDS, COLS:] = halves(sine_z)
    boxes[ENDS : ENDS + 2, :ROWS], boxes[ENDS + 8 : ENDS + 10, :ROWS] = halves(ends_y)
    boxes[EDGES : EDGES + 2, :COLS], boxes[EDGES + 8 : EDGES + 10, :COLS] = halves(ends_z)
    boxes[PICK, 0], boxes[PICK + 1, COLS - 1] = -0.5, 0.5
    both = mu_box[:, None] + lam[None, :]
    shared = np.zeros((SHARED_ROWS, 256))
    shared[:PHI, :ROWS] = both.T
    shared[:PHI, ROWS:] = 1.0
    shared[PHI:LAM_ROW, :ROWS] = ends_y[0]
    shared[LAM_ROW:ENDS_Z, :COLS] = lam
    shared[ENDS_Z : ENDS_Z + 2, :COLS] = ends_z
    shared[ENDS_Y : ENDS_Y + 2, :ROWS] = ends_y
    r, wall = np.arange(ROWS), np.arange(WALLS)
    known = np.zeros((PEERS, CLASS_ROWS, COLS))
    mix = np.zeros((PEERS, MIX_ROWS, COLS))
    into = np.zeros((PEERS, 512, 256))
    back = np.zeros((PEERS, COLS, 1024))
    for c in range(PEERS):
        mode = c + PEERS * np.arange(OWNED)
        norm = np.where(mode == 0, np.sqrt(1 / NY), np.sqrt(2 / NY))
        angle = np.pi * np.outer(2 * r + 1, mode) / (2 * NY)
        turn = np.pi * c * wall / 8
        for k, wave in enumerate((np.cos(angle), np.sin(angle))):
            table = np.zeros((ROWS, COLS))
            table[:, :OWNED] = sine_y @ (norm * wave)
            high, low = halves(table)
            into[c, 256 * k : 256 * k + ROWS, :COLS], into[c, 256 * k : 256 * k + ROWS, COLS:] = high, low
            back[c, :, 256 * k : 256 * k + ROWS], back[c, :, 512 + 256 * k : 512 + 256 * k + ROWS] = high.T, low.T
        fold, spread = np.zeros((16, 64)), np.zeros((64, 16))
        for line in range(4):
            for core in range(2):
                box = 16 * line + 8 * core + wall
                fold[2 * line + core, box], fold[8 + 2 * line + core, box] = np.cos(turn), -np.sin(turn)
                spread[box, 2 * line + core], spread[box, 8 + 2 * line + core] = np.cos(turn), -np.sin(turn)
        mix[c, :16, :64], mix[c, 16:SPREAD, :64] = halves(fold)
        mix[c, SPREAD : SPREAD + 64, :16], mix[c, SPREAD + 64 :, :16] = halves(spread)
        for g in range(2):
            y = ROWS * (wall + g) + g - 1
            row = norm * np.cos(np.pi * np.outer(2 * y + 1, mode) / (2 * NY))
            for core in range(2):
                known[c, 16 * g + 8 * core : 16 * g + 8 * core + 8, :OWNED] = row
        mu = np.ones(COLS)
        mu[:OWNED] = 4 * np.sin(np.pi * mode / (2 * NY)) ** 2
        known[c, MU_ROW:MU_COL], known[c, MU_COL:] = mu, mu[:, None]
    whole = dict(both=both, shared=shared, known=known)
    half = dict(boxes=boxes, mix=mix, into=into, back=back)
    return {k: np.asarray(v, np.float32) for k, v in whole.items()}, {k: np.asarray(v, np.float32) for k, v in half.items()}


def dot(a, b, dims):
    return lax.dot_general(a, b, (dims, ((), ())), precision=EXACT, preferred_element_type=F32)


def fast(a, b, dims=((1,), (0,))):
    return lax.dot_general(a, b, (dims, ((), ())), preferred_element_type=F32)


def ids(shape, dim):
    return lax.broadcasted_iota(jnp.int32, shape, dim)


def pieces(value):
    high = value.astype(BF16).astype(F32)
    return high, value - high


def parts(value):
    return [piece.astype(BF16) for piece in pieces(value)]


def stacked(value):
    return jnp.concatenate(pieces(value), 0).astype(BF16)


def beside(value):
    return jnp.concatenate(parts(value), 1)


def joined(product, rows, width=COLS, at=0):
    here, other = slice(at, at + width), slice(at + width, at + 2 * width)
    return product[:rows, here] + (product[:rows, other] + product[rows:, here])


def start(pairs, sems):
    copies = [pltpu.make_async_copy(*pair, sems.at[i]) for i, pair in enumerate(pairs)]
    for copy in copies:
        copy.start()
    return copies


def pack(lines):
    tails = [jnp.concatenate([lines[side][:, COLS:ROWS], lines[2 + side][:, COLS:ROWS]], 1) for side in range(2)]
    return [line[:, :COLS] for line in lines] + tails


def unpack(rows):
    return [
        jnp.concatenate([rows[2 * plane + side], rows[4 + side][:, 64 * plane : 64 * plane + 64]], 1)
        for plane in range(2) for side in range(2)
    ]


def box_kernel(
    wave_hbm, vel_hbm, both_hbm, boxes_hbm,
    out_ref, freq_ref, solve_ref, boxes_ref,
    wave_ref, vel_ref, both_ref, sems,
):
    copies = start([
        (wave_hbm, wave_ref), (both_hbm, both_ref), (vel_hbm.at[:, 0], vel_ref.at[:, 0]),
        (vel_hbm.at[:, 1], vel_ref.at[:, 1]), (boxes_hbm, boxes_ref),
    ], sems)
    row, lane = ids((ROWS, COLS), 0), ids((ROWS, COLS), 1)
    wall = lax.axis_index("wall")
    low = jnp.where(wall > 0, -0.5, 0.0)
    high = jnp.where(wall < WALLS - 1, 0.5, 0.0)
    copies[0].wait()
    copies[1].wait()
    for plane in range(2):
        wave = wave_ref[plane]
        solve_ref[ROWS * plane : ROWS * (plane + 1), :] = -1.0 / (wave * wave + both_ref[...])
    sources, rims, sides = [], [], []
    for plane in range(2):
        copies[2 + plane].wait()
        u, v, w = (vel_ref[c, plane] for c in range(3))
        above = jnp.where(row == ROWS - 1, 0.0, pltpu.roll(v, ROWS - 1, 0))
        below = jnp.where(row == 0, 0.0, pltpu.roll(v, 1, 0))
        after = jnp.where(lane == COLS - 1, 0.0, pltpu.roll(w, COLS - 1, 1))
        before = jnp.where(lane == 0, 0.0, pltpu.roll(w, 1, 1))
        sources += parts(wave_ref[plane] * u + 0.5 * ((above - below) + (after - before)))
        rims += [low * v[0:1], high * v[ROWS - 1 :]]
        sides.append(parts(w))
    copies[4].wait()
    sine, sine_z = boxes_ref[:SINE_Z, :ROWS], boxes_ref[SINE_Z:ENDS, :]
    product = fast(sine, jnp.concatenate(sources, 1))
    product = fast(jnp.concatenate([stacked(joined(product, ROWS, at=256 * p)) for p in range(2)], 0), sine_z)
    insides = []
    for plane in range(2):
        freq = joined(product[2 * ROWS * plane : 2 * ROWS * (plane + 1)], ROWS)
        rows = slice(ROWS * plane, ROWS * (plane + 1))
        freq_ref[rows, :] = freq
        insides.append(parts(freq * solve_ref[rows, :]))
    pick, edge = boxes_ref[PICK:BOX_ROWS, :COLS], boxes_ref[EDGES:PICK, :COLS]
    across = ((1,), (1,))
    halo = [(fast(pick, high, across) + fast(pick, low, across))[0:2] for high, low in sides]
    halo = stacked(jnp.concatenate(halo + [jnp.zeros((4, ROWS), F32)], 0))
    left, right = fast(halo, boxes_ref[:ROWS, :]), fast(halo, boxes_ref[ROWS:SINE_Z, :])
    halo = (left[0:8] + (left[8:16] + right[0:8]))[:, :ROWS]
    lines = []
    for plane, (high, low) in enumerate(insides):
        left, right = fast(edge, high, across), fast(edge, low, across)
        line = left[0:2] + (left[8:10] + right[0:2]) + halo[2 * plane : 2 * plane + 2]
        lines += [line[0:1], line[1:2]]
    ends = fast(boxes_ref[ENDS:EDGES, :ROWS], jnp.concatenate(insides[0] + insides[1], 1))
    ends = [joined(ends, 8, at=256 * p)[0:2] for p in range(2)]
    rims = fast(stacked(jnp.concatenate(rims + [jnp.zeros((4, COLS), F32)], 0)), sine_z)
    ends = jnp.concatenate(ends, 0) + joined(rims, 8)[0:4]
    four = jnp.concatenate((pack(lines) + [ends]) * 4, 0)
    for group in range(PEERS // 4):
        out_ref[4 * CHUNK * group : 4 * CHUNK * (group + 1), :] = four


def decay(shift):
    root = jnp.sqrt(shift * (shift + 4.0))
    delta = (shift + root) / (2.0 + shift + root)
    return 1.0 - delta, delta * (2.0 - delta), -jnp.log1p(-delta)


def factor_kernel(
    wave_hbm, shared_hbm, known_hbm, mix_hbm, into_hbm, back_hbm,
    chain_ref, reach_ref, cauchy_ref, ring_ref, pair_ref, shared_ref, known_ref, mix_ref, into_ref, back_ref,
    wave_ref, sems,
):
    pair, mine = lax.axis_index("pair"), 8 * lax.axis_index("core") + lax.axis_index("wall")
    copies = start([
        (wave_hbm, wave_ref), (shared_hbm, shared_ref), (known_hbm.at[mine], known_ref), (mix_hbm.at[mine], mix_ref),
        (into_hbm.at[mine], into_ref), (back_hbm.at[mine], back_ref),
    ], sems)
    for copy in copies[:3]:
        copy.wait()
    waves = [wave_ref[p] * wave_ref[p] for p in range(2)]
    row = ids((8, COLS), 0)
    lam = shared_ref[LAM_ROW:ENDS_Z, :COLS]
    for p in range(2):
        at = COLS * p
        reach_ref[at : at + COLS, :] = beside(shared_ref[PHI : PHI + 1, :] / (waves[p] + shared_ref[:PHI, :]))
        cauchy_ref[at : at + COLS, :] = beside(1.0 / (known_ref[MU_COL:, :] + (waves[p] + lam[0:1])))
        rho, gap, theta = decay(waves[p] + lam)
        step = -1.0 * ROWS * theta
        scale = 1.0 / (gap * (1.0 - jnp.exp(-2.0 * NY * theta)))
        cross = jnp.exp(-(ROWS + 1.0) * theta)

        def reach(n):
            return jnp.exp(step * lax.bitwise_and(n, 15).astype(F32))

        for other in range(WALLS):
            up, down = reach(row - 1 - other) + rho * reach(15 - row - other), reach(row + other) + rho * reach(other - row)
            at = 32 * (WALLS * p + other)
            chain_ref[at : at + 8, :] = scale * (cross * up + down)
            chain_ref[at + 8 : at + 16, :] = scale * (up + cross * down)
            up, down = rho * reach(row - other) + reach(14 - row - other), rho * reach(row + 1 + other) + reach(other - row - 1)
            chain_ref[at + 16 : at + 24, :] = scale * (cross * up + down)
            chain_ref[at + 24 : at + 32, :] = scale * (up + cross * down)
    rho, gap, theta = decay(jnp.where(row >= 4, waves[1], waves[0]) + known_ref[MU_ROW:MU_COL, :])
    pair_ref[0:8, :] = jnp.exp(-(COLS + 1.0) * theta)
    pair_ref[8:16, :] = jnp.exp(-1.0 * COLS * theta)
    step = -2.0 * COLS * theta
    leftward = row % 2 == 0
    swapped = jnp.concatenate([step[0:2], step[4:6]] * 2, 0)
    for group in range(PAIRS // 2):
        other = 2 * group + row // 4
        n = lax.bitwise_and(jnp.where(leftward, other - pair - 1, pair - 1 - other), PAIRS - 1)
        ring_ref[8 * group : 8 * group + 8, :] = jnp.exp(swapped * n.astype(F32))
    period = 1.0 - jnp.exp(-1.0 * NZ * theta)
    for i, value in enumerate((rho, 1.0 / (gap * period), period, jnp.exp(-1.0 * COLS * theta))):
        pair_ref[16 + 8 * i : 24 + 8 * i, :] = jnp.concatenate([value[0:1], value[4:5]] * 4, 0)
    for copy in copies[3:]:
        copy.wait()


def strip_kernel(in_ref, chain_ref, reach_ref, pair_ref, shared_ref, mix_ref, into_ref, out_ref, own_ref, sums_ref, near_ref):
    box = [in_ref[pl.ds(i, PEERS, stride=CHUNK), :] for i in range(6)]
    ends = shared_ref[ENDS_Z : ENDS_Z + 2, :COLS]
    lines = unpack(box)
    even = ids((2 * PEERS, ROWS), 1) % 2 == 0
    added = []
    for plane in range(2):
        tops, bottoms = [], []
        for core in range(2):
            top = bottom = None
            for other in range(WALLS):
                at = 32 * (WALLS * plane + other)
                source = CHUNK * (WALLS * core + other) + 6 + 2 * plane
                first, last = in_ref[source : source + 1, :], in_ref[source + 1 : source + 2, :]
                weight = [chain_ref[at + 8 * i : at + 8 * i + 8, :] for i in range(4)]
                one, two = weight[0] * first + weight[1] * last, weight[2] * first + weight[3] * last
                top, bottom = (one, two) if top is None else (top + one, bottom + two)
            tops.append(top)
            bottoms.append(bottom)
        top, bottom = jnp.concatenate(tops, 0), jnp.concatenate(bottoms, 0)
        near_ref[pl.ds(2 * plane, PEERS, stride=8), :] = top
        near_ref[pl.ds(2 * plane + 1, PEERS, stride=8), :] = bottom
        sums = [value * ends[side : side + 1] for value in (top + bottom, top - bottom) for side in range(2)]
        product = fast(stacked(jnp.concatenate(sums, 0)), reach_ref[COLS * plane : COLS * (plane + 1), :])
        product = joined(product, 4 * PEERS, 256)[:, :ROWS]
        added.append(jnp.where(even, product[: 2 * PEERS], product[2 * PEERS :]))
    mine = 8 * lax.axis_index("core") + lax.axis_index("wall")
    own_ref[...] = near_ref[pl.ds(pl.multiple_of(8 * mine, 8), 8), :]
    lines = jnp.concatenate(lines, 0) + jnp.concatenate(added, 0)
    lines = jnp.concatenate([lines, jnp.zeros((4 * PEERS, 256 - ROWS), F32)], 1)
    folded = joined(fast(mix_ref[:SPREAD, :64], beside(lines)), 16, 256)
    folded = stacked(jnp.concatenate([folded[0:8], folded[8:16]], 1))
    modes = joined(fast(folded, into_ref[...]), 8)
    row = ids((8, COLS), 0)
    modes = modes + pair_ref[0:8, :] * jnp.where(row % 4 < 2, pltpu.roll(modes, 6, 0), pltpu.roll(modes, 2, 0))
    sums_ref[...] = modes
    modes = modes + pair_ref[8:16, :] * jnp.where(row % 2 == 0, pltpu.roll(modes, 7, 0), pltpu.roll(modes, 1, 0))
    out = jnp.concatenate([modes[0:1], modes[3:4], modes[4:5], modes[7:8]] * 2, 0)
    for group in range(PAIRS // 2):
        out_ref[8 * group : 8 * group + 8, :] = out


def ring_kernel(in_ref, sums_ref, ring_ref, pair_ref, known_ref, mix_ref, back_ref, cauchy_ref, shared_ref, out_ref):
    total = in_ref[0:8, :] * ring_ref[0:8, :]
    for group in range(1, PAIRS // 2):
        total = total + in_ref[8 * group : 8 * group + 8, :] * ring_ref[8 * group : 8 * group + 8, :]
    total = total[0:4] + total[4:8]
    rho, scale, period, block = (pair_ref[16 + 8 * i : 18 + 8 * i, :] for i in range(4))

    def planes(value, at, step):
        return jnp.concatenate([value[at : at + 1], value[at + step : at + step + 1]], 0)

    after, before = planes(total, 0, 2), planes(total, 1, 2)
    left0, left1, right0, right1 = (period * planes(sums_ref, i, 4) for i in range(4))
    coming, going = block * before + right0, block * after + left1
    left = [scale * (before + rho * (left0 + block * going)), scale * (coming + rho * going)]
    right = [scale * (rho * coming + going), scale * (rho * (right1 + block * coming) + after)]
    ghosts = [[side[p : p + 1] for side in left + right] for p in range(2)]
    cells = joined(fast(stacked(jnp.concatenate(ghosts[0] + ghosts[1], 0)), back_ref[...]), 8, 512)
    cells = jnp.concatenate([cells[:, :256], cells[:, 256:]], 0)
    cells = joined(fast(mix_ref[SPREAD:, :16], beside(cells)), 64, 256)
    for i, value in enumerate(pack([cells[PEERS * i : PEERS * (i + 1)] for i in range(4)])):
        out_ref[pl.ds(i, PEERS, stride=CHUNK), :] = value
    ends = shared_ref[ENDS_Z : ENDS_Z + 2, :COLS]
    known = known_ref[GHOST:MU_ROW, :]
    is_first = ids((32, COLS), 0) % 16 < 8
    for plane in range(2):
        both = [known * jnp.where(is_first, ghosts[plane][2 * side], ghosts[plane][2 * side + 1]) for side in range(2)]
        rims = joined(fast(stacked(jnp.concatenate(both, 0)), cauchy_ref[COLS * plane : COLS * (plane + 1), :]), 64)
        rims = rims[:32] * ends[0:1] + rims[32:] * ends[1:2]
        for side in range(2):
            out_ref[pl.ds(6 + 2 * plane + side, PEERS, stride=CHUNK), :] = rims[PEERS * side : PEERS * (side + 1)]


def final_kernel(in_ref, own_ref, freq_ref, solve_ref, boxes_ref, shared_ref, out_ref):
    step = 4 * CHUNK
    total = (in_ref[0:step, :] + in_ref[step : 2 * step, :]) + (in_ref[2 * step : 3 * step, :] + in_ref[3 * step :, :])
    total = (total[0:CHUNK] + total[CHUNK : 2 * CHUNK]) + (total[2 * CHUNK : 3 * CHUNK] + total[3 * CHUNK :])
    sides = unpack([total[i : i + 1] for i in range(6)])
    rims = total[6:10] + own_ref[0:4, :]
    sine, sine_z = boxes_ref[:SINE_Z, :ROWS], boxes_ref[SINE_Z:ENDS, :]
    freqs = []
    for plane in range(2):
        rows = slice(ROWS * plane, ROWS * (plane + 1))
        lhs = [shared_ref[ENDS_Y : ENDS_Y + 2, :ROWS]] + sides[2 * plane : 2 * plane + 2] + [jnp.zeros((4, ROWS), F32)]
        rhs = [rims[2 * plane : 2 * plane + 2], shared_ref[ENDS_Z : ENDS_Z + 2, :COLS], jnp.zeros((4, COLS), F32)]
        change = dot(jnp.concatenate(lhs, 0), jnp.concatenate(rhs, 0), ((0,), (0,)))
        freqs.append(stacked((freq_ref[rows, :] - change) * solve_ref[rows, :]))
    product = fast(jnp.concatenate(freqs, 0), sine_z)
    lines = [beside(joined(product[2 * ROWS * p : 2 * ROWS * (p + 1)], ROWS)) for p in range(2)]
    product = fast(sine, jnp.concatenate(lines, 1))
    for plane in range(2):
        out_ref[plane] = joined(product, ROWS, at=256 * plane)


VMEM = pl.BlockSpec(memory_space=pltpu.VMEM)
HBM = pl.BlockSpec(memory_space=pltpu.HBM)


def call(kernel, shapes, specs, *operands, scratch=()):
    outs = [jax.ShapeDtypeStruct(s[0], s[1]) if isinstance(s[0], tuple) else jax.ShapeDtypeStruct(s, F32) for s in shapes]
    operands = [pltpu.with_memory_space_constraint(x, pltpu.HBM) if s is HBM else x for s, x in zip(specs, operands)]
    return pl.pallas_call(
        kernel,
        out_shape=outs if len(outs) > 1 else outs[0],
        in_specs=specs,
        out_specs=[VMEM] * len(outs) if len(outs) > 1 else VMEM,
        scratch_shapes=list(scratch),
        compiler_params=pltpu.CompilerParams(vmem_limit_bytes=24 << 20),
    )(*operands)


def exchange(block, axes):
    return lax.all_to_all(block, axes, split_axis=0, concat_axis=0, tiled=True)


def on_device(velocity, wave_x):
    whole, half = tables()
    t = {k: jnp.asarray(v) for k, v in whole.items()} | {k: jnp.asarray(v, BF16) for k, v in half.items()}
    pltpu_smem = pltpu.SMEM((2,), F32)
    sent, freq, solve, boxes = call(
        box_kernel, [(PEERS * CHUNK, COLS), (2 * ROWS, COLS), (2 * ROWS, COLS), ((BOX_ROWS, 256), BF16)],
        [HBM] * 4, wave_x, velocity, t["both"], t["boxes"],
        scratch=[
            pltpu_smem, pltpu.VMEM((3, 2, ROWS, COLS), F32), pltpu.VMEM((ROWS, COLS), F32), pltpu.SemaphoreType.DMA((5,)),
        ],
    )
    chain, reach, cauchy, ring, pair, shared, known, mix, into, back = call(
        factor_kernel,
        [
            (64 * WALLS, COLS), ((2 * COLS, 512), BF16), ((2 * COLS, 256), BF16), (4 * PAIRS, COLS), (48, COLS),
            (SHARED_ROWS, 256), (CLASS_ROWS, COLS), ((MIX_ROWS, COLS), BF16), ((512, 256), BF16), ((COLS, 1024), BF16),
        ],
        [HBM] * 6, wave_x, t["shared"], t["known"], t["mix"], t["into"], t["back"],
        scratch=[pltpu_smem, pltpu.SemaphoreType.DMA((6,))],
    )
    half_chunk = (PEERS * CHUNK // 2, 2, COLS)
    sent = exchange(sent.reshape(half_chunk), ("core", "wall")).reshape(PEERS * CHUNK, COLS)
    modes, own, sums = call(
        strip_kernel, [(4 * PAIRS, COLS), (8, COLS), (8, COLS)], [VMEM] * 7,
        sent, chain, reach, pair, shared, mix, into, scratch=[pltpu.VMEM((8 * PEERS, COLS), F32)],
    )
    modes = exchange(modes.reshape(PAIRS, 4, COLS), "pair").reshape(4 * PAIRS, COLS)
    cells = call(
        ring_kernel, [(PEERS * CHUNK, COLS)], [VMEM] * 9, modes, sums, ring, pair, known, mix, back, cauchy, shared
    )
    cells = exchange(cells.reshape(half_chunk), ("core", "wall")).reshape(PEERS * CHUNK, COLS)
    return call(final_kernel, [(2, ROWS, COLS)], [VMEM] * 6, cells, own, freq, solve, boxes, shared)


def solution(mesh):
    fine = Mesh(mesh.devices.reshape(PAIRS, 2, WALLS), ("pair", "core", "wall"))
    placed = (P(None, None, "wall", ("pair", "core")), P())
    return jax.shard_map(
        on_device, mesh=fine, in_specs=placed, out_specs=P(None, "wall", ("pair", "core")), check_vma=False
    )
```

```python
import jax
import jax.numpy as jnp
import numpy as np
from jax import lax
from jax.experimental import pallas as pl
from jax.experimental.pallas import tpu as pltpu
from jax.sharding import Mesh, PartitionSpec as P

F32 = jnp.float32
BF16 = jnp.bfloat16
EXACT = lax.Precision.HIGHEST
NY, NZ = 1536, 8192
WALLS, STRIPS = 8, 64
PAIRS, PEERS = STRIPS // 2, 2 * WALLS
ROWS, COLS = NY // WALLS, NZ // STRIPS
OWNED = NY // PEERS
CHUNK = 10
SINE_Z, ENDS, EDGES, PICK, BOX_ROWS = 384, 512, 528, 544, 560
GHOST, MU_ROW, MU_COL, CLASS_ROWS = 0, 32, 40, 168
SPREAD, MIX_ROWS = 32, 160
PHI, LAM_ROW, ENDS_Z, MU_BOX, SHARED_ROWS = 128, 136, 144, 152, 160


def halves(table):
    high = table.astype(np.float32).astype(BF16).astype(np.float64)
    return high, table - high


def sine_table(n):
    i = np.arange(1, n + 1)
    return np.sqrt(2 / (n + 1)) * np.sin(np.pi * np.outer(i, i) / (n + 1)), 4 * np.sin(np.pi * i / (2 * (n + 1))) ** 2


def tables():
    sine_y, mu_box = sine_table(ROWS)
    sine_z, lam = sine_table(COLS)
    ends_y, ends_z = sine_y[[0, -1]], sine_z[[0, -1]]
    boxes = np.zeros((BOX_ROWS, 256))
    boxes[:ROWS, :ROWS], boxes[ROWS:SINE_Z, :ROWS] = halves(sine_y)
    boxes[SINE_Z:ENDS, :COLS], boxes[SINE_Z:ENDS, COLS:] = halves(sine_z)
    boxes[ENDS : ENDS + 2, :ROWS], boxes[ENDS + 8 : ENDS + 10, :ROWS] = halves(ends_y)
    boxes[EDGES : EDGES + 2, :COLS], boxes[EDGES + 8 : EDGES + 10, :COLS] = halves(ends_z)
    boxes[PICK, 0], boxes[PICK + 1, COLS - 1] = -0.5, 0.5
    both = mu_box[:, None] + lam[None, :]
    shared = np.zeros((SHARED_ROWS, 256))
    shared[:PHI, :ROWS] = both.T
    shared[:PHI, ROWS:] = 1.0
    shared[PHI:LAM_ROW, :ROWS] = ends_y[0]
    shared[LAM_ROW:ENDS_Z, :COLS] = lam
    shared[ENDS_Z : ENDS_Z + 2, :COLS] = ends_z
    shared[MU_BOX:] = 1.0
    shared[MU_BOX:, :ROWS] = mu_box
    r, wall = np.arange(ROWS), np.arange(WALLS)
    known = np.zeros((PEERS, CLASS_ROWS, COLS))
    mix = np.zeros((PEERS, MIX_ROWS, COLS))
    into = np.zeros((PEERS, 512, 256))
    back = np.zeros((PEERS, COLS, 1024))
    for c in range(PEERS):
        mode = c + PEERS * np.arange(OWNED)
        norm = np.where(mode == 0, np.sqrt(1 / NY), np.sqrt(2 / NY))
        angle = np.pi * np.outer(2 * r + 1, mode) / (2 * NY)
        turn = np.pi * c * wall / 8
        for k, wave in enumerate((np.cos(angle), np.sin(angle))):
            table = np.zeros((ROWS, COLS))
            table[:, :OWNED] = sine_y @ (norm * wave)
            high, low = halves(table)
            into[c, 256 * k : 256 * k + ROWS, :COLS], into[c, 256 * k : 256 * k + ROWS, COLS:] = high, low
            back[c, :, 256 * k : 256 * k + ROWS], back[c, :, 512 + 256 * k : 512 + 256 * k + ROWS] = high.T, low.T
        fold, spread = np.zeros((16, 64)), np.zeros((64, 16))
        for line in range(4):
            for core in range(2):
                box = 16 * line + 8 * core + wall
                fold[2 * line + core, box], fold[8 + 2 * line + core, box] = np.cos(turn), -np.sin(turn)
                spread[box, 2 * line + core], spread[box, 8 + 2 * line + core] = np.cos(turn), -np.sin(turn)
        mix[c, :16, :64], mix[c, 16:SPREAD, :64] = halves(fold)
        mix[c, SPREAD : SPREAD + 64, :16], mix[c, SPREAD + 64 :, :16] = halves(spread)
        for g in range(2):
            y = ROWS * (wall + g) + g - 1
            row = norm * np.cos(np.pi * np.outer(2 * y + 1, mode) / (2 * NY))
            for core in range(2):
                known[c, 16 * g + 8 * core : 16 * g + 8 * core + 8, :OWNED] = row
        mu = np.ones(COLS)
        mu[:OWNED] = 4 * np.sin(np.pi * mode / (2 * NY)) ** 2
        known[c, MU_ROW:MU_COL], known[c, MU_COL:] = mu, mu[:, None]
    whole = dict(both=both, shared=shared, known=known)
    half = dict(boxes=boxes, mix=mix, into=into, back=back)
    return {k: np.asarray(v, np.float32) for k, v in whole.items()}, {k: np.asarray(v, np.float32) for k, v in half.items()}


def dot(a, b, dims):
    return lax.dot_general(a, b, (dims, ((), ())), precision=EXACT, preferred_element_type=F32)


def fast(a, b, dims=((1,), (0,))):
    return lax.dot_general(a, b, (dims, ((), ())), preferred_element_type=F32)


def ids(shape, dim):
    return lax.broadcasted_iota(jnp.int32, shape, dim)


def pieces(value):
    high = value.astype(BF16).astype(F32)
    return high, value - high


def parts(value):
    return [piece.astype(BF16) for piece in pieces(value)]


def stacked(value):
    return jnp.concatenate(pieces(value), 0).astype(BF16)


def beside(value):
    return jnp.concatenate(parts(value), 1)


def joined(product, rows, width=COLS, at=0):
    here, other = slice(at, at + width), slice(at + width, at + 2 * width)
    return product[:rows, here] + (product[:rows, other] + product[rows:, here])


def start(pairs, sems):
    copies = [pltpu.make_async_copy(*pair, sems.at[i]) for i, pair in enumerate(pairs)]
    for copy in copies:
        copy.start()
    return copies


def pack(lines):
    tails = [jnp.concatenate([lines[side][:, COLS:ROWS], lines[2 + side][:, COLS:ROWS]], 1) for side in range(2)]
    return [line[:, :COLS] for line in lines] + tails


def unpack(rows):
    return [
        jnp.concatenate([rows[2 * plane + side], rows[4 + side][:, 64 * plane : 64 * plane + 64]], 1)
        for plane in range(2) for side in range(2)
    ]


def box_kernel(
    wave_hbm, vel_hbm, both_hbm, boxes_hbm,
    out_ref, inside_ref, boxes_ref,
    wave_ref, vel_ref, both_ref, solve_ref, sems,
):
    copies = start([
        (wave_hbm, wave_ref), (both_hbm, both_ref), (vel_hbm.at[:, 0], vel_ref.at[:, 0]),
        (vel_hbm.at[:, 1], vel_ref.at[:, 1]), (boxes_hbm, boxes_ref),
    ], sems)
    row, lane = ids((ROWS, COLS), 0), ids((ROWS, COLS), 1)
    wall = lax.axis_index("wall")
    low = jnp.where(wall > 0, -0.5, 0.0)
    high = jnp.where(wall < WALLS - 1, 0.5, 0.0)
    copies[0].wait()
    copies[1].wait()
    for plane in range(2):
        wave = wave_ref[plane]
        solve_ref[ROWS * plane : ROWS * (plane + 1), :] = -1.0 / (wave * wave + both_ref[...])
    sources, rims, sides = [], [], []
    for plane in range(2):
        copies[2 + plane].wait()
        u, v, w = (vel_ref[c, plane] for c in range(3))
        above = jnp.where(row == ROWS - 1, 0.0, pltpu.roll(v, ROWS - 1, 0))
        below = jnp.where(row == 0, 0.0, pltpu.roll(v, 1, 0))
        after = jnp.where(lane == COLS - 1, 0.0, pltpu.roll(w, COLS - 1, 1))
        before = jnp.where(lane == 0, 0.0, pltpu.roll(w, 1, 1))
        sources += parts(wave_ref[plane] * u + 0.5 * ((above - below) + (after - before)))
        rims += [low * v[0:1], high * v[ROWS - 1 :]]
        sides.append(parts(w))
    copies[4].wait()
    sine, sine_z = boxes_ref[:SINE_Z, :ROWS], boxes_ref[SINE_Z:ENDS, :]
    product = fast(sine, jnp.concatenate(sources, 1))
    product = fast(jnp.concatenate([stacked(joined(product, ROWS, at=256 * p)) for p in range(2)], 0), sine_z)
    insides = []
    for plane in range(2):
        freq = joined(product[2 * ROWS * plane : 2 * ROWS * (plane + 1)], ROWS)
        rows = slice(ROWS * plane, ROWS * (plane + 1))
        inside = freq * solve_ref[rows, :]
        inside_ref[rows, :] = inside
        insides.append(parts(inside))
    pick, edge = boxes_ref[PICK:BOX_ROWS, :COLS], boxes_ref[EDGES:PICK, :COLS]
    across = ((1,), (1,))
    halo = [(fast(pick, high, across) + fast(pick, low, across))[0:2] for high, low in sides]
    halo = stacked(jnp.concatenate(halo + [jnp.zeros((4, ROWS), F32)], 0))
    left, right = fast(halo, boxes_ref[:ROWS, :]), fast(halo, boxes_ref[ROWS:SINE_Z, :])
    halo = (left[0:8] + (left[8:16] + right[0:8]))[:, :ROWS]
    lines = []
    for plane, (high, low) in enumerate(insides):
        left, right = fast(edge, high, across), fast(edge, low, across)
        line = left[0:2] + (left[8:10] + right[0:2]) + halo[2 * plane : 2 * plane + 2]
        lines += [line[0:1], line[1:2]]
    ends = fast(boxes_ref[ENDS:EDGES, :ROWS], jnp.concatenate(insides[0] + insides[1], 1))
    ends = [joined(ends, 8, at=256 * p)[0:2] for p in range(2)]
    rims = fast(stacked(jnp.concatenate(rims + [jnp.zeros((4, COLS), F32)], 0)), sine_z)
    ends = jnp.concatenate(ends, 0) + joined(rims, 8)[0:4]
    four = jnp.concatenate((pack(lines) + [ends]) * 4, 0)
    for group in range(PEERS // 4):
        out_ref[4 * CHUNK * group : 4 * CHUNK * (group + 1), :] = four


def decay(shift):
    root = jnp.sqrt(shift * (shift + 4.0))
    delta = (shift + root) / (2.0 + shift + root)
    return 1.0 - delta, delta * (2.0 - delta), -jnp.log1p(-delta)


def factor_kernel(
    wave_hbm, shared_hbm, known_hbm, mix_hbm, into_hbm, back_hbm, inside_ref, boxes_ref,
    chain_ref, reach_ref, cauchy_ref, ring_ref, pair_ref, shared_ref, known_ref, mix_ref, into_ref, back_ref,
    base_ref, down_ref, across_ref,
    wave_ref, sems,
):
    pair, mine = lax.axis_index("pair"), 8 * lax.axis_index("core") + lax.axis_index("wall")
    copies = start([
        (wave_hbm, wave_ref), (shared_hbm, shared_ref), (known_hbm.at[mine], known_ref), (mix_hbm.at[mine], mix_ref),
        (into_hbm.at[mine], into_ref), (back_hbm.at[mine], back_ref),
    ], sems)
    for copy in copies[:3]:
        copy.wait()
    waves = [wave_ref[p] * wave_ref[p] for p in range(2)]
    row = ids((8, COLS), 0)
    lam = shared_ref[LAM_ROW:ENDS_Z, :COLS]
    for p in range(2):
        at = COLS * p
        reach_ref[at : at + COLS, :] = beside(shared_ref[PHI : PHI + 1, :] / (waves[p] + shared_ref[:PHI, :]))
        cauchy_ref[at : at + COLS, :] = beside(1.0 / (known_ref[MU_COL:, :] + (waves[p] + lam[0:1])))
        rho, gap, theta = decay(waves[p] + lam)
        step = -1.0 * ROWS * theta
        scale = 1.0 / (gap * (1.0 - jnp.exp(-2.0 * NY * theta)))
        cross = jnp.exp(-(ROWS + 1.0) * theta)

        def reach(n):
            return jnp.exp(step * lax.bitwise_and(n, 15).astype(F32))

        for other in range(WALLS):
            up, down = reach(row - 1 - other) + rho * reach(15 - row - other), reach(row + other) + rho * reach(other - row)
            at = 32 * (WALLS * p + other)
            chain_ref[at : at + 8, :] = scale * (cross * up + down)
            chain_ref[at + 8 : at + 16, :] = scale * (up + cross * down)
            up, down = rho * reach(row - other) + reach(14 - row - other), rho * reach(row + 1 + other) + reach(other - row - 1)
            chain_ref[at + 16 : at + 24, :] = scale * (cross * up + down)
            chain_ref[at + 24 : at + 32, :] = scale * (up + cross * down)
    rho, gap, theta = decay(jnp.where(row >= 4, waves[1], waves[0]) + known_ref[MU_ROW:MU_COL, :])
    pair_ref[0:8, :] = jnp.exp(-(COLS + 1.0) * theta)
    pair_ref[8:16, :] = jnp.exp(-1.0 * COLS * theta)
    step = -2.0 * COLS * theta
    leftward = row % 2 == 0
    swapped = jnp.concatenate([step[0:2], step[4:6]] * 2, 0)
    for group in range(PAIRS // 2):
        other = 2 * group + row // 4
        n = lax.bitwise_and(jnp.where(leftward, other - pair - 1, pair - 1 - other), PAIRS - 1)
        ring_ref[8 * group : 8 * group + 8, :] = jnp.exp(swapped * n.astype(F32))
    period = 1.0 - jnp.exp(-1.0 * NZ * theta)
    for i, value in enumerate((rho, 1.0 / (gap * period), period, jnp.exp(-1.0 * COLS * theta))):
        pair_ref[16 + 8 * i : 24 + 8 * i, :] = jnp.concatenate([value[0:1], value[4:5]] * 4, 0)
    sine, sine_z = boxes_ref[:SINE_Z, :ROWS], boxes_ref[SINE_Z:ENDS, :]
    product = fast(jnp.concatenate([stacked(inside_ref[ROWS * p : ROWS * (p + 1), :]) for p in range(2)], 0), sine_z)
    lines = [beside(joined(product[2 * ROWS * p : 2 * ROWS * (p + 1)], ROWS)) for p in range(2)]
    product = fast(sine, jnp.concatenate(lines, 1))
    for plane in range(2):
        base_ref[ROWS * plane : ROWS * (plane + 1), :] = joined(product, ROWS, at=256 * plane)
        for ref, shift, count in (
            (down_ref, shared_ref[LAM_ROW : LAM_ROW + 1, :COLS], ROWS), (across_ref, shared_ref[MU_BOX : MU_BOX + 1, :], COLS),
        ):
            _, _, theta = decay(waves[plane] + shift)
            whole = 1.0 / (1.0 - jnp.exp(-2.0 * (count + 1) * theta))
            step = ids((count, shift.shape[1]), 0).astype(F32)
            for side in range(2):
                n = step if side == 0 else count - 1.0 - step
                at = count * (2 * plane + side)
                ref[at : at + count, :] = jnp.exp(-(n + 1.0) * theta) * (1.0 - jnp.exp(-2.0 * (count - n) * theta)) * whole
    for copy in copies[3:]:
        copy.wait()


def strip_kernel(in_ref, chain_ref, reach_ref, pair_ref, shared_ref, mix_ref, into_ref, out_ref, own_ref, sums_ref, near_ref):
    box = [in_ref[pl.ds(i, PEERS, stride=CHUNK), :] for i in range(6)]
    ends = shared_ref[ENDS_Z : ENDS_Z + 2, :COLS]
    lines = unpack(box)
    even = ids((2 * PEERS, ROWS), 1) % 2 == 0
    added = []
    for plane in range(2):
        tops, bottoms = [], []
        for core in range(2):
            top = bottom = None
            for other in range(WALLS):
                at = 32 * (WALLS * plane + other)
                source = CHUNK * (WALLS * core + other) + 6 + 2 * plane
                first, last = in_ref[source : source + 1, :], in_ref[source + 1 : source + 2, :]
                weight = [chain_ref[at + 8 * i : at + 8 * i + 8, :] for i in range(4)]
                one, two = weight[0] * first + weight[1] * last, weight[2] * first + weight[3] * last
                top, bottom = (one, two) if top is None else (top + one, bottom + two)
            tops.append(top)
            bottoms.append(bottom)
        top, bottom = jnp.concatenate(tops, 0), jnp.concatenate(bottoms, 0)
        near_ref[pl.ds(2 * plane, PEERS, stride=8), :] = top
        near_ref[pl.ds(2 * plane + 1, PEERS, stride=8), :] = bottom
        sums = [value * ends[side : side + 1] for value in (top + bottom, top - bottom) for side in range(2)]
        product = fast(stacked(jnp.concatenate(sums, 0)), reach_ref[COLS * plane : COLS * (plane + 1), :])
        product = joined(product, 4 * PEERS, 256)[:, :ROWS]
        added.append(jnp.where(even, product[: 2 * PEERS], product[2 * PEERS :]))
    mine = 8 * lax.axis_index("core") + lax.axis_index("wall")
    own_ref[...] = near_ref[pl.ds(pl.multiple_of(8 * mine, 8), 8), :]
    lines = jnp.concatenate(lines, 0) + jnp.concatenate(added, 0)
    lines = jnp.concatenate([lines, jnp.zeros((4 * PEERS, 256 - ROWS), F32)], 1)
    folded = joined(fast(mix_ref[:SPREAD, :64], beside(lines)), 16, 256)
    folded = stacked(jnp.concatenate([folded[0:8], folded[8:16]], 1))
    modes = joined(fast(folded, into_ref[...]), 8)
    row = ids((8, COLS), 0)
    modes = modes + pair_ref[0:8, :] * jnp.where(row % 4 < 2, pltpu.roll(modes, 6, 0), pltpu.roll(modes, 2, 0))
    sums_ref[...] = modes
    modes = modes + pair_ref[8:16, :] * jnp.where(row % 2 == 0, pltpu.roll(modes, 7, 0), pltpu.roll(modes, 1, 0))
    out = jnp.concatenate([modes[0:1], modes[3:4], modes[4:5], modes[7:8]] * 2, 0)
    for group in range(PAIRS // 2):
        out_ref[8 * group : 8 * group + 8, :] = out


def ring_kernel(in_ref, sums_ref, ring_ref, pair_ref, known_ref, mix_ref, back_ref, cauchy_ref, shared_ref, out_ref):
    total = in_ref[0:8, :] * ring_ref[0:8, :]
    for group in range(1, PAIRS // 2):
        total = total + in_ref[8 * group : 8 * group + 8, :] * ring_ref[8 * group : 8 * group + 8, :]
    total = total[0:4] + total[4:8]
    rho, scale, period, block = (pair_ref[16 + 8 * i : 18 + 8 * i, :] for i in range(4))

    def planes(value, at, step):
        return jnp.concatenate([value[at : at + 1], value[at + step : at + step + 1]], 0)

    after, before = planes(total, 0, 2), planes(total, 1, 2)
    left0, left1, right0, right1 = (period * planes(sums_ref, i, 4) for i in range(4))
    coming, going = block * before + right0, block * after + left1
    left = [scale * (before + rho * (left0 + block * going)), scale * (coming + rho * going)]
    right = [scale * (rho * coming + going), scale * (rho * (right1 + block * coming) + after)]
    ghosts = [[side[p : p + 1] for side in left + right] for p in range(2)]
    cells = joined(fast(stacked(jnp.concatenate(ghosts[0] + ghosts[1], 0)), back_ref[...]), 8, 512)
    cells = jnp.concatenate([cells[:, :256], cells[:, 256:]], 0)
    cells = joined(fast(mix_ref[SPREAD:, :16], beside(cells)), 64, 256)
    for i, value in enumerate(pack([cells[PEERS * i : PEERS * (i + 1)] for i in range(4)])):
        out_ref[pl.ds(i, PEERS, stride=CHUNK), :] = value
    ends = shared_ref[ENDS_Z : ENDS_Z + 2, :COLS]
    known = known_ref[GHOST:MU_ROW, :]
    is_first = ids((32, COLS), 0) % 16 < 8
    for plane in range(2):
        both = [known * jnp.where(is_first, ghosts[plane][2 * side], ghosts[plane][2 * side + 1]) for side in range(2)]
        rims = joined(fast(stacked(jnp.concatenate(both, 0)), cauchy_ref[COLS * plane : COLS * (plane + 1), :]), 64)
        rims = rims[:32] * ends[0:1] + rims[32:] * ends[1:2]
        for side in range(2):
            out_ref[pl.ds(6 + 2 * plane + side, PEERS, stride=CHUNK), :] = rims[PEERS * side : PEERS * (side + 1)]


def final_kernel(in_ref, own_ref, base_ref, down_ref, across_ref, boxes_ref, out_hbm, out_ref, sems):
    step = 4 * CHUNK
    total = (in_ref[0:step, :] + in_ref[step : 2 * step, :]) + (in_ref[2 * step : 3 * step, :] + in_ref[3 * step :, :])
    total = (total[0:CHUNK] + total[CHUNK : 2 * CHUNK]) + (total[2 * CHUNK : 3 * CHUNK] + total[3 * CHUNK :])
    sides = unpack([total[i : i + 1] for i in range(6)])
    rims = total[6:10] + own_ref[0:4, :]
    sine, sine_z = boxes_ref[:SINE_Z, :ROWS], boxes_ref[SINE_Z:ENDS, :]
    copies = []
    for plane in range(2):
        down, across = [], []
        for side in range(2):
            at = 2 * plane + side
            down.append(rims[at : at + 1] * down_ref[ROWS * at : ROWS * (at + 1), :])
            across.append(sides[at] * across_ref[COLS * at : COLS * (at + 1), :ROWS])
        down = joined(fast(stacked(down[0] + down[1]), sine_z), ROWS)
        across = joined(fast(sine, stacked(across[0] + across[1]), ((1,), (1,))), ROWS)
        out_ref[plane] = base_ref[ROWS * plane : ROWS * (plane + 1), :] + (down + across)
        copies += start([(out_ref.at[plane], out_hbm.at[plane])], sems.at[pl.ds(plane, 1)])
    for copy in copies:
        copy.wait()


VMEM = pl.BlockSpec(memory_space=pltpu.VMEM)
HBM = pl.BlockSpec(memory_space=pltpu.HBM)


def call(kernel, shapes, specs, *operands, scratch=(), into=VMEM):
    outs = [jax.ShapeDtypeStruct(s[0], s[1]) if isinstance(s[0], tuple) else jax.ShapeDtypeStruct(s, F32) for s in shapes]
    operands = [pltpu.with_memory_space_constraint(x, pltpu.HBM) if s is HBM else x for s, x in zip(specs, operands)]
    return pl.pallas_call(
        kernel,
        out_shape=outs if len(outs) > 1 else outs[0],
        in_specs=specs,
        out_specs=[into] * len(outs) if len(outs) > 1 else into,
        scratch_shapes=list(scratch),
        compiler_params=pltpu.CompilerParams(vmem_limit_bytes=24 << 20),
    )(*operands)


def exchange(block, axes):
    return lax.all_to_all(block, axes, split_axis=0, concat_axis=0, tiled=True)


def on_device(velocity, wave_x):
    whole, half = tables()
    t = {k: jnp.asarray(v) for k, v in whole.items()} | {k: jnp.asarray(v, BF16) for k, v in half.items()}
    pltpu_smem = pltpu.SMEM((2,), F32)
    sent, inside, boxes = call(
        box_kernel, [(PEERS * CHUNK, COLS), (2 * ROWS, COLS), ((BOX_ROWS, 256), BF16)],
        [HBM] * 4, wave_x, velocity, t["both"], t["boxes"],
        scratch=[
            pltpu_smem, pltpu.VMEM((3, 2, ROWS, COLS), F32), pltpu.VMEM((ROWS, COLS), F32),
            pltpu.VMEM((2 * ROWS, COLS), F32), pltpu.SemaphoreType.DMA((5,)),
        ],
    )
    chain, reach, cauchy, ring, pair, shared, known, mix, into, back, base, down, across = call(
        factor_kernel,
        [
            (64 * WALLS, COLS), ((2 * COLS, 512), BF16), ((2 * COLS, 256), BF16), (4 * PAIRS, COLS), (48, COLS),
            (SHARED_ROWS, 256), (CLASS_ROWS, COLS), ((MIX_ROWS, COLS), BF16), ((512, 256), BF16), ((COLS, 1024), BF16),
            (2 * ROWS, COLS), (4 * ROWS, COLS), (4 * COLS, 256),
        ],
        [HBM] * 6 + [VMEM] * 2, wave_x, t["shared"], t["known"], t["mix"], t["into"], t["back"], inside, boxes,
        scratch=[pltpu_smem, pltpu.SemaphoreType.DMA((6,))],
    )
    half_chunk = (PEERS * CHUNK // 2, 2, COLS)
    sent = exchange(sent.reshape(half_chunk), ("core", "wall")).reshape(PEERS * CHUNK, COLS)
    modes, own, sums = call(
        strip_kernel, [(4 * PAIRS, COLS), (8, COLS), (8, COLS)], [VMEM] * 7,
        sent, chain, reach, pair, shared, mix, into, scratch=[pltpu.VMEM((8 * PEERS, COLS), F32)],
    )
    modes = exchange(modes.reshape(PAIRS, 4, COLS), "pair").reshape(4 * PAIRS, COLS)
    cells = call(
        ring_kernel, [(PEERS * CHUNK, COLS)], [VMEM] * 9, modes, sums, ring, pair, known, mix, back, cauchy, shared
    )
    cells = exchange(cells.reshape(half_chunk), ("core", "wall")).reshape(PEERS * CHUNK, COLS)
    return call(
        final_kernel, [(2, ROWS, COLS)], [VMEM] * 6, cells, own, base, down, across, boxes,
        scratch=[pltpu.VMEM((2, ROWS, COLS), F32), pltpu.SemaphoreType.DMA((2,))], into=HBM,
    )


def solution(mesh):
    fine = Mesh(mesh.devices.reshape(PAIRS, 2, WALLS), ("pair", "core", "wall"))
    placed = (P(None, None, "wall", ("pair", "core")), P())
    return jax.shard_map(
        on_device, mesh=fine, in_specs=placed, out_specs=P(None, "wall", ("pair", "core")), check_vma=False
    )
```

```python
import jax
import jax.numpy as jnp
import numpy as np
from jax import lax
from jax.experimental import pallas as pl
from jax.experimental.pallas import tpu as pltpu
from jax.sharding import Mesh, PartitionSpec as P

F32 = jnp.float32
BF16 = jnp.bfloat16
EXACT = lax.Precision.HIGHEST
NY, NZ = 1536, 8192
WALLS, STRIPS = 8, 64
PAIRS, PEERS = STRIPS // 2, 2 * WALLS
ROWS, COLS = NY // WALLS, NZ // STRIPS
GROUP = 4
OWNED = NY // PEERS
TILES = GROUP * OWNED // COLS
CHUNK = 10
SINE_Z, ENDS, EDGES, PICK, BOX_ROWS = 384, 512, 528, 544, 560
GHOST, MU_ROW, MU_COL, CLASS_ROWS = 0, 24, 48, 432
PHI, LAM_ROW, ENDS_Z, MU_BOX, SHARED_ROWS = 128, 136, 144, 152, 152


def halves(table):
    high = table.astype(np.float32).astype(BF16).astype(np.float64)
    return high, table - high


def sine_table(n):
    i = np.arange(1, n + 1)
    return np.sqrt(2 / (n + 1)) * np.sin(np.pi * np.outer(i, i) / (n + 1)), 4 * np.sin(np.pi * i / (2 * (n + 1))) ** 2


def tables():
    sine_y, mu_box = sine_table(ROWS)
    sine_z, lam = sine_table(COLS)
    ends_y, ends_z = sine_y[[0, -1]], sine_z[[0, -1]]
    boxes = np.zeros((BOX_ROWS, 256))
    boxes[:ROWS, :ROWS], boxes[ROWS:SINE_Z, :ROWS] = halves(sine_y)
    boxes[SINE_Z:ENDS, :COLS], boxes[SINE_Z:ENDS, COLS:] = halves(sine_z)
    boxes[ENDS : ENDS + 2, :ROWS], boxes[ENDS + 8 : ENDS + 10, :ROWS] = halves(ends_y)
    boxes[EDGES : EDGES + 2, :COLS], boxes[EDGES + 8 : EDGES + 10, :COLS] = halves(ends_z)
    boxes[PICK, 0], boxes[PICK + 1, COLS - 1] = -0.5, 0.5
    both = mu_box[:, None] + lam[None, :]
    shared = np.zeros((SHARED_ROWS, 256))
    shared[:PHI, :ROWS] = both.T
    shared[:PHI, ROWS:] = 1.0
    shared[PHI:LAM_ROW, :ROWS] = ends_y[0]
    shared[LAM_ROW:ENDS_Z, :COLS] = lam
    shared[ENDS_Z : ENDS_Z + 2, :COLS] = ends_z
    r, wall = np.arange(ROWS), np.arange(WALLS)
    known = np.zeros((GROUP, 4, CLASS_ROWS, COLS))
    mix = np.zeros((GROUP, 128, COLS))
    into = np.zeros((GROUP, 2 * GROUP * ROWS, 256))
    back = np.zeros((GROUP, 4, GROUP * OWNED, 4 * ROWS))
    for c in range(GROUP):
        fold = np.zeros((64, 64))
        for k in range(GROUP):
            mode = c + 4 * k + PEERS * np.arange(OWNED)
            norm = np.where(mode == 0, np.sqrt(1 / NY), np.sqrt(2 / NY))
            angle = np.pi * np.outer(2 * r + 1, mode) / (2 * NY)
            turn = np.pi * (c + 4 * k) * wall / 8
            for n, wave in enumerate((np.cos(angle), np.sin(angle))):
                rows = slice(ROWS * (2 * k + n), ROWS * (2 * k + n + 1))
                into[c, rows, :OWNED], into[c, rows, COLS : COLS + OWNED] = halves(sine_y @ (norm * wave))
            for line in range(4):
                for core in range(2):
                    box = 16 * line + 8 * core + wall
                    fold[16 * k + 2 * line + core, box] = np.cos(turn)
                    fold[16 * k + 8 + 2 * line + core, box] = -np.sin(turn)
        mix[c, :64, :64], mix[c, 64:, :64] = halves(fold)
        mode = (c + 4 * np.arange(GROUP)[:, None] + PEERS * np.arange(OWNED)[None, :]).reshape(-1)
        norm = np.where(mode == 0, np.sqrt(1 / NY), np.sqrt(2 / NY))
        mu = 4 * np.sin(np.pi * mode / (2 * NY)) ** 2
        for high in range(4):
            for low in range(2):
                w = 2 * high + low
                table = norm[:, None] * np.cos(np.pi * np.outer(mode, 2 * (ROWS * w + r) + 1) / (2 * NY)) @ sine_y
                here, other = slice(ROWS * low, ROWS * (low + 1)), slice(ROWS * (2 + low), ROWS * (3 + low))
                back[c, high, :, here], back[c, high, :, other] = halves(table)
                for g in range(2):
                    y = ROWS * (w + g) + g - 1
                    row = (norm * np.cos(np.pi * mode * (2 * y + 1) / (2 * NY))).reshape(TILES, COLS)
                    for core in range(2):
                        known[c, high, 4 * g + 2 * core + low : MU_ROW : 8] = row
            known[c, high, MU_ROW:MU_COL] = np.concatenate([np.repeat(mu.reshape(TILES, COLS), 4, 0)] * 2)
            known[c, high, MU_COL:] = mu[:, None]
    whole = dict(both=both, shared=shared, known=known)
    half = dict(boxes=boxes, mix=mix, into=into, back=back)
    return {k: np.asarray(v, np.float32) for k, v in whole.items()}, {k: np.asarray(v, np.float32) for k, v in half.items()}


def dot(a, b, dims):
    return lax.dot_general(a, b, (dims, ((), ())), precision=EXACT, preferred_element_type=F32)


def fast(a, b, dims=((1,), (0,))):
    return lax.dot_general(a, b, (dims, ((), ())), preferred_element_type=F32)


def ids(shape, dim):
    return lax.broadcasted_iota(jnp.int32, shape, dim)


def pieces(value):
    high = value.astype(BF16).astype(F32)
    return high, value - high


def parts(value):
    return [piece.astype(BF16) for piece in pieces(value)]


def stacked(value):
    return jnp.concatenate(pieces(value), 0).astype(BF16)


def beside(value):
    return jnp.concatenate(parts(value), 1)


def joined(product, rows, width=COLS, at=0):
    here, other = slice(at, at + width), slice(at + width, at + 2 * width)
    return product[:rows, here] + (product[:rows, other] + product[rows:, here])


def start(pairs, sems):
    copies = [pltpu.make_async_copy(*pair, sems.at[i]) for i, pair in enumerate(pairs)]
    for copy in copies:
        copy.start()
    return copies


def pack(lines):
    tails = [jnp.concatenate([lines[side][:, COLS:ROWS], lines[2 + side][:, COLS:ROWS]], 1) for side in range(2)]
    return [line[:, :COLS] for line in lines] + tails


def unpack(rows):
    return [
        jnp.concatenate([rows[2 * plane + side], rows[4 + side][:, 64 * plane : 64 * plane + 64]], 1)
        for plane in range(2) for side in range(2)
    ]


def box_kernel(
    wave_hbm, vel_hbm, both_hbm, boxes_hbm,
    out_ref, freq_ref, solve_ref, boxes_ref,
    wave_ref, vel_ref, both_ref, sems,
):
    copies = start([
        (wave_hbm, wave_ref), (both_hbm, both_ref), (vel_hbm.at[:, 0], vel_ref.at[:, 0]),
        (vel_hbm.at[:, 1], vel_ref.at[:, 1]), (boxes_hbm, boxes_ref),
    ], sems)
    row, lane = ids((ROWS, COLS), 0), ids((ROWS, COLS), 1)
    wall = 2 * lax.axis_index("high") + lax.axis_index("low")
    low = jnp.where(wall > 0, -0.5, 0.0)
    high = jnp.where(wall < WALLS - 1, 0.5, 0.0)
    copies[0].wait()
    copies[1].wait()
    for plane in range(2):
        wave = wave_ref[plane]
        solve_ref[ROWS * plane : ROWS * (plane + 1), :] = -1.0 / (wave * wave + both_ref[...])
    sources, rims, sides = [], [], []
    for plane in range(2):
        copies[2 + plane].wait()
        u, v, w = (vel_ref[c, plane] for c in range(3))
        above = jnp.where(row == ROWS - 1, 0.0, pltpu.roll(v, ROWS - 1, 0))
        below = jnp.where(row == 0, 0.0, pltpu.roll(v, 1, 0))
        after = jnp.where(lane == COLS - 1, 0.0, pltpu.roll(w, COLS - 1, 1))
        before = jnp.where(lane == 0, 0.0, pltpu.roll(w, 1, 1))
        sources += parts(wave_ref[plane] * u + 0.5 * ((above - below) + (after - before)))
        rims += [low * v[0:1], high * v[ROWS - 1 :]]
        sides.append(parts(w))
    copies[4].wait()
    sine, sine_z = boxes_ref[:SINE_Z, :ROWS], boxes_ref[SINE_Z:ENDS, :]
    product = fast(sine, jnp.concatenate(sources, 1))
    product = fast(jnp.concatenate([stacked(joined(product, ROWS, at=256 * p)) for p in range(2)], 0), sine_z)
    insides = []
    for plane in range(2):
        freq = joined(product[2 * ROWS * plane : 2 * ROWS * (plane + 1)], ROWS)
        rows = slice(ROWS * plane, ROWS * (plane + 1))
        freq_ref[rows, :] = freq
        insides.append(parts(freq * solve_ref[rows, :]))
    pick, edge = boxes_ref[PICK:BOX_ROWS, :COLS], boxes_ref[EDGES:PICK, :COLS]
    across = ((1,), (1,))
    halo = [(fast(pick, high, across) + fast(pick, low, across))[0:2] for high, low in sides]
    halo = stacked(jnp.concatenate(halo + [jnp.zeros((4, ROWS), F32)], 0))
    left, right = fast(halo, boxes_ref[:ROWS, :]), fast(halo, boxes_ref[ROWS:SINE_Z, :])
    halo = (left[0:8] + (left[8:16] + right[0:8]))[:, :ROWS]
    lines = []
    for plane, (high, low) in enumerate(insides):
        left, right = fast(edge, high, across), fast(edge, low, across)
        line = left[0:2] + (left[8:10] + right[0:2]) + halo[2 * plane : 2 * plane + 2]
        lines += [line[0:1], line[1:2]]
    ends = fast(boxes_ref[ENDS:EDGES, :ROWS], jnp.concatenate(insides[0] + insides[1], 1))
    ends = [joined(ends, 8, at=256 * p)[0:2] for p in range(2)]
    rims = fast(stacked(jnp.concatenate(rims + [jnp.zeros((4, COLS), F32)], 0)), sine_z)
    ends = jnp.concatenate(ends, 0) + joined(rims, 8)[0:4]
    four = jnp.concatenate((pack(lines) + [ends]) * 4, 0)
    for group in range(PEERS // 4):
        out_ref[4 * CHUNK * group : 4 * CHUNK * (group + 1), :] = four


def decay(shift):
    root = jnp.sqrt(shift * (shift + 4.0))
    delta = (shift + root) / (2.0 + shift + root)
    return 1.0 - delta, delta * (2.0 - delta), -jnp.log1p(-delta)


def factor_kernel(
    wave_hbm, shared_hbm, known_hbm, mix_hbm, into_hbm, back_hbm,
    chain_ref, reach_ref, cauchy_ref, ring_ref, pair_ref, rims_ref, mix_ref, into_ref, back_ref,
    wave_ref, shared_ref, known_ref, sems,
):
    pair, high = lax.axis_index("pair"), lax.axis_index("high")
    mine = 2 * lax.axis_index("core") + lax.axis_index("low")
    copies = start([
        (wave_hbm, wave_ref), (shared_hbm, shared_ref), (known_hbm.at[mine, high], known_ref), (mix_hbm.at[mine], mix_ref),
        (into_hbm.at[mine], into_ref), (back_hbm.at[mine, high], back_ref),
    ], sems)
    for copy in copies[:3]:
        copy.wait()
    waves = [wave_ref[p] * wave_ref[p] for p in range(2)]
    row = ids((8, COLS), 0)
    lam = shared_ref[LAM_ROW:ENDS_Z, :COLS]
    for p in range(2):
        at = COLS * p
        reach_ref[at : at + COLS, :] = beside(shared_ref[PHI : PHI + 1, :] / (waves[p] + shared_ref[:PHI, :]))
        rows = slice(GROUP * OWNED * p, GROUP * OWNED * (p + 1))
        cauchy_ref[rows, :] = beside(1.0 / (known_ref[MU_COL:, :] + (waves[p] + lam[0:1])))
        rho, gap, theta = decay(waves[p] + lam)
        step = -1.0 * ROWS * theta
        scale = 1.0 / (gap * (1.0 - jnp.exp(-2.0 * NY * theta)))
        cross = jnp.exp(-(ROWS + 1.0) * theta)

        def reach(n):
            return jnp.exp(step * lax.bitwise_and(n, 15).astype(F32))

        for other in range(WALLS):
            up, down = reach(row - 1 - other) + rho * reach(15 - row - other), reach(row + other) + rho * reach(other - row)
            at = 32 * (WALLS * p + other)
            chain_ref[at : at + 8, :] = scale * (cross * up + down)
            chain_ref[at + 8 : at + 16, :] = scale * (up + cross * down)
            up, down = rho * reach(row - other) + reach(14 - row - other), rho * reach(row + 1 + other) + reach(other - row - 1)
            chain_ref[at + 16 : at + 24, :] = scale * (cross * up + down)
            chain_ref[at + 24 : at + 32, :] = scale * (up + cross * down)
    place = ids((24, COLS), 0)
    second, leftward = place % 4 >= 2, place % 2 == 0
    mu = known_ref[MU_ROW:MU_COL, :]
    _, _, theta = decay(jnp.where(second, waves[1], waves[0]) + mu)
    step = -2.0 * COLS * theta
    for group in range(PAIRS // 2):
        other = 2 * group + place // 12
        n = lax.bitwise_and(jnp.where(leftward, other - pair - 1, pair - 1 - other), PAIRS - 1)
        ring_ref[24 * group : 24 * group + 24, :] = jnp.exp(step * n.astype(F32))
    coefs = [[], [], [], []]
    for tile in range(TILES):
        rho, gap, theta = decay(jnp.where(row >= 4, waves[1], waves[0]) + mu[4 * tile : 4 * tile + 1])
        block = jnp.exp(-1.0 * COLS * theta)
        pair_ref[8 * tile : 8 * tile + 8, :] = jnp.exp(-(COLS + 1.0) * theta)
        pair_ref[24 + 8 * tile : 32 + 8 * tile, :] = block
        period = 1.0 - jnp.exp(-1.0 * NZ * theta)
        for i, value in enumerate((rho, 1.0 / (gap * period), period, block)):
            coefs[i] += [value[0:1], value[4:5]]
    for i in range(4):
        pair_ref[48 + 8 * i : 56 + 8 * i, :] = jnp.concatenate(coefs[i] + coefs[i][:2], 0)
    rims_ref[0:24, :] = known_ref[GHOST:MU_ROW, :]
    rims_ref[24:32, :] = shared_ref[ENDS_Z:MU_BOX, :COLS]
    for copy in copies[3:]:
        copy.wait()


def strip_kernel(in_ref, chain_ref, reach_ref, pair_ref, rims_ref, mix_ref, into_ref, out_ref, own_ref, sums_ref, near_ref):
    box = [in_ref[pl.ds(i, PEERS, stride=CHUNK), :] for i in range(6)]
    ends = rims_ref[24:26, :]
    lines = unpack(box)
    even = ids((2 * PEERS, ROWS), 1) % 2 == 0
    added = []
    for plane in range(2):
        tops, bottoms = [], []
        for core in range(2):
            top = bottom = None
            for other in range(WALLS):
                at = 32 * (WALLS * plane + other)
                source = CHUNK * (WALLS * core + other) + 6 + 2 * plane
                first, last = in_ref[source : source + 1, :], in_ref[source + 1 : source + 2, :]
                weight = [chain_ref[at + 8 * i : at + 8 * i + 8, :] for i in range(4)]
                one, two = weight[0] * first + weight[1] * last, weight[2] * first + weight[3] * last
                top, bottom = (one, two) if top is None else (top + one, bottom + two)
            tops.append(top)
            bottoms.append(bottom)
        top, bottom = jnp.concatenate(tops, 0), jnp.concatenate(bottoms, 0)
        near_ref[pl.ds(2 * plane, PEERS, stride=8), :] = top
        near_ref[pl.ds(2 * plane + 1, PEERS, stride=8), :] = bottom
        sums = [value * ends[side : side + 1] for value in (top + bottom, top - bottom) for side in range(2)]
        product = fast(stacked(jnp.concatenate(sums, 0)), reach_ref[COLS * plane : COLS * (plane + 1), :])
        product = joined(product, 4 * PEERS, 256)[:, :ROWS]
        added.append(jnp.where(even, product[: 2 * PEERS], product[2 * PEERS :]))
    mine = 8 * lax.axis_index("core") + 2 * lax.axis_index("high") + lax.axis_index("low")
    own_ref[...] = near_ref[pl.ds(pl.multiple_of(8 * mine, 8), 8), :]
    lines = jnp.concatenate(lines, 0) + jnp.concatenate(added, 0)
    lines = jnp.concatenate([lines, jnp.zeros((4 * PEERS, 256 - ROWS), F32)], 1)
    folded = joined(fast(mix_ref[:, :64], beside(lines)), 64, 256)
    modes = []
    for k in range(GROUP):
        both = jnp.concatenate([folded[16 * k : 16 * k + 8, :ROWS], folded[16 * k + 8 : 16 * k + 16, :ROWS]], 1)
        modes.append(joined(fast(stacked(both), into_ref[2 * ROWS * k : 2 * ROWS * (k + 1), :]), 8))
    modes = [modes[0]] + [pltpu.roll(modes[k], COLS - 32 * k, 1) for k in range(1, GROUP)]
    row, lane = ids((8, COLS), 0), ids((8, COLS), 1)
    out = []
    for tile in range(TILES):
        value = jnp.where(lane < 96 - 32 * tile, modes[tile], modes[tile + 1])
        at = 8 * tile
        near = jnp.where(row % 4 < 2, pltpu.roll(value, 6, 0), pltpu.roll(value, 2, 0))
        value = value + pair_ref[at : at + 8, :] * near
        sums_ref[at : at + 8, :] = value
        near = jnp.where(row % 2 == 0, pltpu.roll(value, 7, 0), pltpu.roll(value, 1, 0))
        value = value + pair_ref[24 + at : 32 + at, :] * near
        out += [value[0:1], value[3:5], value[7:8]]
    out = jnp.concatenate(out * 2, 0)
    for group in range(PAIRS // 2):
        out_ref[24 * group : 24 * group + 24, :] = out


def ring_kernel(in_ref, sums_ref, ring_ref, pair_ref, rims_ref, back_ref, cauchy_ref, out_ref, far_ref, line_ref):
    total = in_ref[0:24, :] * ring_ref[0:24, :]
    for group in range(1, PAIRS // 2):
        total = total + in_ref[24 * group : 24 * group + 24, :] * ring_ref[24 * group : 24 * group + 24, :]
    far_ref[...] = total
    count = 2 * TILES
    after, before = (
        far_ref[pl.ds(i, count, stride=2), :] + far_ref[pl.ds(12 + i, count, stride=2), :] for i in range(2)
    )
    rho, scale, period, block = (pair_ref[48 + 8 * i : 48 + 8 * i + count, :] for i in range(4))
    left0, left1, right0, right1 = (period * sums_ref[pl.ds(i, count, stride=4), :] for i in range(4))
    coming, going = block * before + right0, block * after + left1
    ghosts = (
        scale * (before + rho * (left0 + block * going)), scale * (coming + rho * going),
        scale * (rho * coming + going), scale * (rho * (right1 + block * coming) + after),
    )
    for i, value in enumerate(ghosts):
        line_ref[pl.ds(i, count, stride=4), :] = value
    tiles = [line_ref[8 * tile : 8 * tile + 8, :] for tile in range(TILES)]
    cells = joined(fast(stacked(jnp.concatenate(tiles, 1)), back_ref[...]), 8, 2 * ROWS)
    ends = rims_ref[24:26, :]
    is_first = ids((8, COLS), 0) % 4 < 2
    rims = []
    for plane in range(2):
        both = []
        for side in range(2):
            at = 4 * plane + 2 * side
            lines = [jnp.where(is_first, tile[at : at + 1], tile[at + 1 : at + 2]) for tile in tiles]
            both.append(jnp.concatenate([rims_ref[8 * i : 8 * i + 8, :] * line for i, line in enumerate(lines)], 1))
        rows = slice(GROUP * OWNED * plane, GROUP * OWNED * (plane + 1))
        product = joined(fast(stacked(jnp.concatenate(both, 0)), cauchy_ref[rows, :]), 16)
        rims.append(product[:8] * ends[0:1] + product[8:] * ends[1:2])
    out = []
    for core in range(2):
        for low in range(2):
            at = 2 * core + low
            out += pack([cells[2 * i + core : 2 * i + core + 1, ROWS * low : ROWS * (low + 1)] for i in range(4)])
            out += [rims[plane][4 * g + at : 4 * g + at + 1] for plane in range(2) for g in range(2)]
    out_ref[...] = jnp.concatenate(out, 0)


def final_kernel(in_ref, own_ref, freq_ref, solve_ref, boxes_ref, out_hbm, out_ref, sems):
    total = (in_ref[0:CHUNK, :] + in_ref[CHUNK : 2 * CHUNK, :]) + (in_ref[2 * CHUNK : 3 * CHUNK, :] + in_ref[3 * CHUNK :, :])
    sides = unpack([total[i : i + 1] for i in range(6)])
    rims = total[6:10] + own_ref[0:4, :]
    sine, sine_z = boxes_ref[:SINE_Z, :ROWS], boxes_ref[SINE_Z:ENDS, :]
    ends_y, ends_z = boxes_ref[ENDS:EDGES, :ROWS].astype(F32), boxes_ref[EDGES:PICK, :COLS].astype(F32)
    ends_y, ends_z = ends_y[0:2] + ends_y[8:10], ends_z[0:2] + ends_z[8:10]
    freqs = []
    for plane in range(2):
        rows = slice(ROWS * plane, ROWS * (plane + 1))
        lhs = pieces(jnp.concatenate([ends_y] + sides[2 * plane : 2 * plane + 2] + [jnp.zeros((4, ROWS), F32)], 0))
        rhs = pieces(jnp.concatenate([rims[2 * plane : 2 * plane + 2], ends_z, jnp.zeros((4, COLS), F32)], 0))
        lhs = jnp.concatenate([lhs[0], lhs[0], lhs[1], lhs[1]], 0).astype(BF16)
        rhs = jnp.concatenate([rhs[0], rhs[1], rhs[0], rhs[1]], 0).astype(BF16)
        freqs.append(stacked((freq_ref[rows, :] - fast(lhs, rhs, ((0,), (0,)))) * solve_ref[rows, :]))
    product = fast(jnp.concatenate(freqs, 0), sine_z)
    lines = [beside(joined(product[2 * ROWS * p : 2 * ROWS * (p + 1)], ROWS)) for p in range(2)]
    product = fast(sine, jnp.concatenate(lines, 1))
    copies = []
    for plane in range(2):
        out_ref[plane] = joined(product, ROWS, at=256 * plane)
        copies += start([(out_ref.at[plane], out_hbm.at[plane])], sems.at[pl.ds(plane, 1)])
    for copy in copies:
        copy.wait()


VMEM = pl.BlockSpec(memory_space=pltpu.VMEM)
HBM = pl.BlockSpec(memory_space=pltpu.HBM)


def call(kernel, shapes, specs, *operands, scratch=(), into=VMEM):
    outs = [jax.ShapeDtypeStruct(s[0], s[1]) if isinstance(s[0], tuple) else jax.ShapeDtypeStruct(s, F32) for s in shapes]
    operands = [pltpu.with_memory_space_constraint(x, pltpu.HBM) if s is HBM else x for s, x in zip(specs, operands)]
    return pl.pallas_call(
        kernel,
        out_shape=outs if len(outs) > 1 else outs[0],
        in_specs=specs,
        out_specs=[into] * len(outs) if len(outs) > 1 else into,
        scratch_shapes=list(scratch),
        compiler_params=pltpu.CompilerParams(vmem_limit_bytes=24 << 20),
    )(*operands)


def exchange(block, axes):
    return lax.all_to_all(block, axes, split_axis=0, concat_axis=0, tiled=True)


def on_device(velocity, wave_x):
    whole, half = tables()
    t = {k: jnp.asarray(v) for k, v in whole.items()} | {k: jnp.asarray(v, BF16) for k, v in half.items()}
    pltpu_smem = pltpu.SMEM((2,), F32)
    sent, freq, solve, boxes = call(
        box_kernel, [(PEERS * CHUNK, COLS), (2 * ROWS, COLS), (2 * ROWS, COLS), ((BOX_ROWS, 256), BF16)],
        [HBM] * 4, wave_x, velocity, t["both"], t["boxes"],
        scratch=[
            pltpu_smem, pltpu.VMEM((3, 2, ROWS, COLS), F32), pltpu.VMEM((ROWS, COLS), F32),
            pltpu.SemaphoreType.DMA((5,)),
        ],
    )
    chain, reach, cauchy, ring, pair, rims, mix, into, back = call(
        factor_kernel,
        [
            (64 * WALLS, COLS), ((2 * COLS, 512), BF16), ((2 * GROUP * OWNED, 256), BF16), (12 * PAIRS, COLS), (80, COLS),
            (32, COLS), ((128, COLS), BF16), ((2 * GROUP * ROWS, 256), BF16), ((GROUP * OWNED, 4 * ROWS), BF16),
        ],
        [HBM] * 6, wave_x, t["shared"], t["known"], t["mix"], t["into"], t["back"],
        scratch=[pltpu_smem, pltpu.VMEM((SHARED_ROWS, 256), F32), pltpu.VMEM((CLASS_ROWS, COLS), F32), pltpu.SemaphoreType.DMA((6,))],
    )
    sent = exchange(sent.reshape(PEERS * CHUNK // 2, 2, COLS), ("core", "high", "low")).reshape(PEERS * CHUNK, COLS)
    modes, own, sums = call(
        strip_kernel, [(12 * PAIRS, COLS), (8, COLS), (24, COLS)], [VMEM] * 7,
        sent, chain, reach, pair, rims, mix, into, scratch=[pltpu.VMEM((8 * PEERS, COLS), F32)],
    )
    modes = exchange(modes.reshape(6 * PAIRS, 2, COLS), "pair").reshape(12 * PAIRS, COLS)
    cells = call(
        ring_kernel, [(GROUP * CHUNK, COLS)], [VMEM] * 7, modes, sums, ring, pair, rims, back, cauchy,
        scratch=[pltpu.VMEM((24, COLS), F32)] * 2,
    )
    cells = exchange(cells.reshape(GROUP * CHUNK // 2, 2, COLS), ("core", "low")).reshape(GROUP * CHUNK, COLS)
    return call(
        final_kernel, [(2, ROWS, COLS)], [VMEM] * 5, cells, own, freq, solve, boxes,
        scratch=[pltpu.VMEM((2, ROWS, COLS), F32), pltpu.SemaphoreType.DMA((2,))], into=HBM,
    )


def solution(mesh):
    fine = Mesh(mesh.devices.reshape(PAIRS, 2, WALLS // 2, 2), ("pair", "core", "high", "low"))
    wall, span = ("high", "low"), ("pair", "core")
    return jax.shard_map(
        on_device, mesh=fine, in_specs=(P(None, None, wall, span), P()), out_specs=P(None, wall, span), check_vma=False
    )
```

```python
import jax
import jax.numpy as jnp
import numpy as np
from jax import lax
from jax.experimental import pallas as pl
from jax.experimental.pallas import tpu as pltpu
from jax.sharding import Mesh, PartitionSpec as P

F32 = jnp.float32
BF16 = jnp.bfloat16
EXACT = lax.Precision.HIGHEST
NY, NZ = 1536, 8192
WALLS, STRIPS = 8, 64
PAIRS, PEERS = STRIPS // 2, 2 * WALLS
ROWS, COLS = NY // WALLS, NZ // STRIPS
GROUP = 4
OWNED = NY // PEERS
TILES = GROUP * OWNED // COLS
CHUNK = 10
SINE_Z, ENDS, EDGES, PICK, BOX_ROWS = 384, 512, 528, 544, 560
GHOST, MU_ROW, MU_COL, CLASS_ROWS = 0, 24, 48, 432
PHI, LAM_ROW, ENDS_Z, MU_BOX, SHARED_ROWS = 128, 136, 144, 152, 152


def halves(table):
    high = table.astype(np.float32).astype(BF16).astype(np.float64)
    return high, table - high


def sine_table(n):
    i = np.arange(1, n + 1)
    return np.sqrt(2 / (n + 1)) * np.sin(np.pi * np.outer(i, i) / (n + 1)), 4 * np.sin(np.pi * i / (2 * (n + 1))) ** 2


def tables():
    sine_y, mu_box = sine_table(ROWS)
    sine_z, lam = sine_table(COLS)
    ends_y, ends_z = sine_y[[0, -1]], sine_z[[0, -1]]
    boxes = np.zeros((BOX_ROWS, 256))
    boxes[:ROWS, :ROWS], boxes[ROWS:SINE_Z, :ROWS] = halves(sine_y)
    boxes[SINE_Z:ENDS, :COLS], boxes[SINE_Z:ENDS, COLS:] = halves(sine_z)
    boxes[ENDS : ENDS + 2, :ROWS], boxes[ENDS + 8 : ENDS + 10, :ROWS] = halves(ends_y)
    boxes[EDGES : EDGES + 2, :COLS], boxes[EDGES + 8 : EDGES + 10, :COLS] = halves(ends_z)
    boxes[PICK, 0], boxes[PICK + 1, COLS - 1] = -0.5, 0.5
    both = mu_box[:, None] + lam[None, :]
    shared = np.zeros((SHARED_ROWS, 256))
    shared[:PHI, :ROWS] = both.T
    shared[:PHI, ROWS:] = 1.0
    shared[PHI:LAM_ROW, :ROWS] = ends_y[0]
    shared[LAM_ROW:ENDS_Z, :COLS] = lam
    shared[ENDS_Z : ENDS_Z + 2, :COLS] = ends_z
    r, wall = np.arange(ROWS), np.arange(WALLS)
    known = np.zeros((GROUP, 4, CLASS_ROWS, COLS))
    mix = np.zeros((GROUP, 128, COLS))
    into = np.zeros((GROUP, 2 * GROUP * ROWS, 256))
    back = np.zeros((GROUP, 4, GROUP * OWNED, 4 * ROWS))
    for c in range(GROUP):
        fold = np.zeros((64, 64))
        for k in range(GROUP):
            mode = c + 4 * k + PEERS * np.arange(OWNED)
            norm = np.where(mode == 0, np.sqrt(1 / NY), np.sqrt(2 / NY))
            angle = np.pi * np.outer(2 * r + 1, mode) / (2 * NY)
            turn = np.pi * (c + 4 * k) * wall / 8
            for n, wave in enumerate((np.cos(angle), np.sin(angle))):
                rows = slice(ROWS * (2 * k + n), ROWS * (2 * k + n + 1))
                into[c, rows, :OWNED], into[c, rows, COLS : COLS + OWNED] = halves(sine_y @ (norm * wave))
            for line in range(4):
                for core in range(2):
                    box = 16 * line + 8 * core + wall
                    fold[16 * k + 2 * line + core, box] = np.cos(turn)
                    fold[16 * k + 8 + 2 * line + core, box] = -np.sin(turn)
        mix[c, :64, :64], mix[c, 64:, :64] = halves(fold)
        mode = (c + 4 * np.arange(GROUP)[:, None] + PEERS * np.arange(OWNED)[None, :]).reshape(-1)
        norm = np.where(mode == 0, np.sqrt(1 / NY), np.sqrt(2 / NY))
        mu = 4 * np.sin(np.pi * mode / (2 * NY)) ** 2
        for high in range(4):
            for low in range(2):
                w = 2 * high + low
                table = norm[:, None] * np.cos(np.pi * np.outer(mode, 2 * (ROWS * w + r) + 1) / (2 * NY)) @ sine_y
                here, other = slice(ROWS * low, ROWS * (low + 1)), slice(ROWS * (2 + low), ROWS * (3 + low))
                back[c, high, :, here], back[c, high, :, other] = halves(table)
                for g in range(2):
                    y = ROWS * (w + g) + g - 1
                    row = (norm * np.cos(np.pi * mode * (2 * y + 1) / (2 * NY))).reshape(TILES, COLS)
                    for core in range(2):
                        known[c, high, 4 * g + 2 * core + low : MU_ROW : 8] = row
            known[c, high, MU_ROW:MU_COL] = np.concatenate([np.repeat(mu.reshape(TILES, COLS), 4, 0)] * 2)
            known[c, high, MU_COL:] = mu[:, None]
    whole = dict(both=both, shared=shared, known=known)
    half = dict(boxes=boxes, mix=mix, into=into, back=back)
    return {k: np.asarray(v, np.float32) for k, v in whole.items()}, {k: np.asarray(v, np.float32) for k, v in half.items()}


def dot(a, b, dims):
    return lax.dot_general(a, b, (dims, ((), ())), precision=EXACT, preferred_element_type=F32)


def fast(a, b, dims=((1,), (0,))):
    return lax.dot_general(a, b, (dims, ((), ())), preferred_element_type=F32)


def ids(shape, dim):
    return lax.broadcasted_iota(jnp.int32, shape, dim)


def pieces(value):
    high = value.astype(BF16).astype(F32)
    return high, value - high


def parts(value):
    return [piece.astype(BF16) for piece in pieces(value)]


def stacked(value):
    return jnp.concatenate(pieces(value), 0).astype(BF16)


def beside(value):
    return jnp.concatenate(parts(value), 1)


def joined(product, rows, width=COLS, at=0):
    here, other = slice(at, at + width), slice(at + width, at + 2 * width)
    return product[:rows, here] + (product[:rows, other] + product[rows:, here])


def start(pairs, sems):
    copies = [pltpu.make_async_copy(*pair, sems.at[i]) for i, pair in enumerate(pairs)]
    for copy in copies:
        copy.start()
    return copies


def pack(lines):
    tails = [jnp.concatenate([lines[side][:, COLS:ROWS], lines[2 + side][:, COLS:ROWS]], 1) for side in range(2)]
    return [line[:, :COLS] for line in lines] + tails


def unpack(rows):
    return [
        jnp.concatenate([rows[2 * plane + side], rows[4 + side][:, 64 * plane : 64 * plane + 64]], 1)
        for plane in range(2) for side in range(2)
    ]


def box_kernel(
    wave_hbm, vel_hbm, both_hbm, boxes_hbm, shared_hbm, known_hbm, mix_hbm, into_hbm, back_hbm,
    out_ref, freq_ref, solve_ref, boxes_ref,
    chain_ref, reach_ref, cauchy_ref, ring_ref, pair_ref, rims_ref, mix_ref, into_ref, back_ref,
    wave_ref, vel_ref, both_ref, shared_ref, known_ref, sems,
):
    mine, high = 2 * lax.axis_index("core") + lax.axis_index("low"), lax.axis_index("high")
    copies = start([
        (wave_hbm, wave_ref), (both_hbm, both_ref), (vel_hbm.at[:, 0], vel_ref.at[:, 0]),
        (vel_hbm.at[:, 1], vel_ref.at[:, 1]), (boxes_hbm, boxes_ref), (shared_hbm, shared_ref),
        (known_hbm.at[mine, high], known_ref), (mix_hbm.at[mine], mix_ref), (into_hbm.at[mine], into_ref),
        (back_hbm.at[mine, high], back_ref),
    ], sems)
    row, lane = ids((ROWS, COLS), 0), ids((ROWS, COLS), 1)
    wall = 2 * lax.axis_index("high") + lax.axis_index("low")
    low = jnp.where(wall > 0, -0.5, 0.0)
    high = jnp.where(wall < WALLS - 1, 0.5, 0.0)
    copies[0].wait()
    copies[1].wait()
    for plane in range(2):
        wave = wave_ref[plane]
        solve_ref[ROWS * plane : ROWS * (plane + 1), :] = -1.0 / (wave * wave + both_ref[...])
    sources, rims, sides = [], [], []
    for plane in range(2):
        copies[2 + plane].wait()
        u, v, w = (vel_ref[c, plane] for c in range(3))
        above = jnp.where(row == ROWS - 1, 0.0, pltpu.roll(v, ROWS - 1, 0))
        below = jnp.where(row == 0, 0.0, pltpu.roll(v, 1, 0))
        after = jnp.where(lane == COLS - 1, 0.0, pltpu.roll(w, COLS - 1, 1))
        before = jnp.where(lane == 0, 0.0, pltpu.roll(w, 1, 1))
        sources += parts(wave_ref[plane] * u + 0.5 * ((above - below) + (after - before)))
        rims += [low * v[0:1], high * v[ROWS - 1 :]]
        sides.append(parts(w))
    for copy in copies[4:7]:
        copy.wait()
    sine, sine_z = boxes_ref[:SINE_Z, :ROWS], boxes_ref[SINE_Z:ENDS, :]
    product = fast(sine, jnp.concatenate(sources, 1))
    product = fast(jnp.concatenate([stacked(joined(product, ROWS, at=256 * p)) for p in range(2)], 0), sine_z)
    insides = []
    for plane in range(2):
        freq = joined(product[2 * ROWS * plane : 2 * ROWS * (plane + 1)], ROWS)
        rows = slice(ROWS * plane, ROWS * (plane + 1))
        freq_ref[rows, :] = freq
        insides.append(parts(freq * solve_ref[rows, :]))
    pick, edge = boxes_ref[PICK:BOX_ROWS, :COLS], boxes_ref[EDGES:PICK, :COLS]
    across = ((1,), (1,))
    halo = [(fast(pick, high, across) + fast(pick, low, across))[0:2] for high, low in sides]
    halo = stacked(jnp.concatenate(halo + [jnp.zeros((4, ROWS), F32)], 0))
    left, right = fast(halo, boxes_ref[:ROWS, :]), fast(halo, boxes_ref[ROWS:SINE_Z, :])
    halo = (left[0:8] + (left[8:16] + right[0:8]))[:, :ROWS]
    lines = []
    for plane, (high, low) in enumerate(insides):
        left, right = fast(edge, high, across), fast(edge, low, across)
        line = left[0:2] + (left[8:10] + right[0:2]) + halo[2 * plane : 2 * plane + 2]
        lines += [line[0:1], line[1:2]]
    ends = fast(boxes_ref[ENDS:EDGES, :ROWS], jnp.concatenate(insides[0] + insides[1], 1))
    ends = [joined(ends, 8, at=256 * p)[0:2] for p in range(2)]
    rims = fast(stacked(jnp.concatenate(rims + [jnp.zeros((4, COLS), F32)], 0)), sine_z)
    ends = jnp.concatenate(ends, 0) + joined(rims, 8)[0:4]
    four = jnp.concatenate((pack(lines) + [ends]) * 4, 0)
    for group in range(PEERS // 4):
        out_ref[4 * CHUNK * group : 4 * CHUNK * (group + 1), :] = four
    factors(wave_ref, shared_ref, known_ref, chain_ref, reach_ref, cauchy_ref, ring_ref, pair_ref, rims_ref)
    for copy in copies[7:]:
        copy.wait()


def decay(shift):
    root = jnp.sqrt(shift * (shift + 4.0))
    delta = (shift + root) / (2.0 + shift + root)
    return 1.0 - delta, delta * (2.0 - delta), -jnp.log1p(-delta)


def factors(
    wave_ref, shared_ref, known_ref, chain_ref, reach_ref, cauchy_ref, ring_ref, pair_ref, rims_ref,
):
    pair = lax.axis_index("pair")
    waves = [wave_ref[p] * wave_ref[p] for p in range(2)]
    row = ids((8, COLS), 0)
    lam = shared_ref[LAM_ROW:ENDS_Z, :COLS]
    for p in range(2):
        at = COLS * p
        reach_ref[at : at + COLS, :] = beside(shared_ref[PHI : PHI + 1, :] / (waves[p] + shared_ref[:PHI, :]))
        rows = slice(GROUP * OWNED * p, GROUP * OWNED * (p + 1))
        cauchy_ref[rows, :] = beside(1.0 / (known_ref[MU_COL:, :] + (waves[p] + lam[0:1])))
        rho, gap, theta = decay(waves[p] + lam)
        step = -1.0 * ROWS * theta
        scale = 1.0 / (gap * (1.0 - jnp.exp(-2.0 * NY * theta)))
        cross = jnp.exp(-(ROWS + 1.0) * theta)

        def reach(n):
            return jnp.exp(step * lax.bitwise_and(n, 15).astype(F32))

        for other in range(WALLS):
            up, down = reach(row - 1 - other) + rho * reach(15 - row - other), reach(row + other) + rho * reach(other - row)
            at = 32 * (WALLS * p + other)
            chain_ref[at : at + 8, :] = scale * (cross * up + down)
            chain_ref[at + 8 : at + 16, :] = scale * (up + cross * down)
            up, down = rho * reach(row - other) + reach(14 - row - other), rho * reach(row + 1 + other) + reach(other - row - 1)
            chain_ref[at + 16 : at + 24, :] = scale * (cross * up + down)
            chain_ref[at + 24 : at + 32, :] = scale * (up + cross * down)
    place = ids((24, COLS), 0)
    second, leftward = place % 4 >= 2, place % 2 == 0
    mu = known_ref[MU_ROW:MU_COL, :]
    _, _, theta = decay(jnp.where(second, waves[1], waves[0]) + mu)
    step = -2.0 * COLS * theta
    for group in range(PAIRS // 2):
        other = 2 * group + place // 12
        n = lax.bitwise_and(jnp.where(leftward, other - pair - 1, pair - 1 - other), PAIRS - 1)
        ring_ref[24 * group : 24 * group + 24, :] = jnp.exp(step * n.astype(F32))
    coefs = [[], [], [], []]
    for tile in range(TILES):
        rho, gap, theta = decay(jnp.where(row >= 4, waves[1], waves[0]) + mu[4 * tile : 4 * tile + 1])
        block = jnp.exp(-1.0 * COLS * theta)
        pair_ref[8 * tile : 8 * tile + 8, :] = jnp.exp(-(COLS + 1.0) * theta)
        pair_ref[24 + 8 * tile : 32 + 8 * tile, :] = block
        period = 1.0 - jnp.exp(-1.0 * NZ * theta)
        for i, value in enumerate((rho, 1.0 / (gap * period), period, block)):
            coefs[i] += [value[0:1], value[4:5]]
    for i in range(4):
        pair_ref[48 + 8 * i : 56 + 8 * i, :] = jnp.concatenate(coefs[i] + coefs[i][:2], 0)
    rims_ref[0:24, :] = known_ref[GHOST:MU_ROW, :]
    rims_ref[24:32, :] = shared_ref[ENDS_Z:MU_BOX, :COLS]


def strip_kernel(in_ref, chain_ref, reach_ref, pair_ref, rims_ref, mix_ref, into_ref, out_ref, own_ref, sums_ref, near_ref):
    box = [in_ref[pl.ds(i, PEERS, stride=CHUNK), :] for i in range(6)]
    ends = rims_ref[24:26, :]
    lines = unpack(box)
    even = ids((2 * PEERS, ROWS), 1) % 2 == 0
    added = []
    for plane in range(2):
        tops, bottoms = [], []
        for core in range(2):
            top = bottom = None
            for other in range(WALLS):
                at = 32 * (WALLS * plane + other)
                source = CHUNK * (WALLS * core + other) + 6 + 2 * plane
                first, last = in_ref[source : source + 1, :], in_ref[source + 1 : source + 2, :]
                weight = [chain_ref[at + 8 * i : at + 8 * i + 8, :] for i in range(4)]
                one, two = weight[0] * first + weight[1] * last, weight[2] * first + weight[3] * last
                top, bottom = (one, two) if top is None else (top + one, bottom + two)
            tops.append(top)
            bottoms.append(bottom)
        top, bottom = jnp.concatenate(tops, 0), jnp.concatenate(bottoms, 0)
        near_ref[pl.ds(2 * plane, PEERS, stride=8), :] = top
        near_ref[pl.ds(2 * plane + 1, PEERS, stride=8), :] = bottom
        sums = [value * ends[side : side + 1] for value in (top + bottom, top - bottom) for side in range(2)]
        product = fast(stacked(jnp.concatenate(sums, 0)), reach_ref[COLS * plane : COLS * (plane + 1), :])
        product = joined(product, 4 * PEERS, 256)[:, :ROWS]
        added.append(jnp.where(even, product[: 2 * PEERS], product[2 * PEERS :]))
    mine = 8 * lax.axis_index("core") + 2 * lax.axis_index("high") + lax.axis_index("low")
    own_ref[...] = near_ref[pl.ds(pl.multiple_of(8 * mine, 8), 8), :]
    lines = jnp.concatenate(lines, 0) + jnp.concatenate(added, 0)
    lines = jnp.concatenate([lines, jnp.zeros((4 * PEERS, 256 - ROWS), F32)], 1)
    folded = joined(fast(mix_ref[:, :64], beside(lines)), 64, 256)
    modes = []
    for k in range(GROUP):
        both = jnp.concatenate([folded[16 * k : 16 * k + 8, :ROWS], folded[16 * k + 8 : 16 * k + 16, :ROWS]], 1)
        modes.append(joined(fast(stacked(both), into_ref[2 * ROWS * k : 2 * ROWS * (k + 1), :]), 8))
    modes = [modes[0]] + [pltpu.roll(modes[k], COLS - 32 * k, 1) for k in range(1, GROUP)]
    row, lane = ids((8, COLS), 0), ids((8, COLS), 1)
    out = []
    for tile in range(TILES):
        value = jnp.where(lane < 96 - 32 * tile, modes[tile], modes[tile + 1])
        at = 8 * tile
        near = jnp.where(row % 4 < 2, pltpu.roll(value, 6, 0), pltpu.roll(value, 2, 0))
        value = value + pair_ref[at : at + 8, :] * near
        sums_ref[at : at + 8, :] = value
        near = jnp.where(row % 2 == 0, pltpu.roll(value, 7, 0), pltpu.roll(value, 1, 0))
        value = value + pair_ref[24 + at : 32 + at, :] * near
        out += [value[0:1], value[3:5], value[7:8]]
    out = jnp.concatenate(out * 2, 0)
    for group in range(PAIRS // 2):
        out_ref[24 * group : 24 * group + 24, :] = out


def ring_kernel(in_ref, sums_ref, ring_ref, pair_ref, rims_ref, back_ref, cauchy_ref, out_ref, far_ref, line_ref):
    total = in_ref[0:24, :] * ring_ref[0:24, :]
    for group in range(1, PAIRS // 2):
        total = total + in_ref[24 * group : 24 * group + 24, :] * ring_ref[24 * group : 24 * group + 24, :]
    far_ref[...] = total
    count = 2 * TILES
    after, before = (
        far_ref[pl.ds(i, count, stride=2), :] + far_ref[pl.ds(12 + i, count, stride=2), :] for i in range(2)
    )
    rho, scale, period, block = (pair_ref[48 + 8 * i : 48 + 8 * i + count, :] for i in range(4))
    left0, left1, right0, right1 = (period * sums_ref[pl.ds(i, count, stride=4), :] for i in range(4))
    coming, going = block * before + right0, block * after + left1
    ghosts = (
        scale * (before + rho * (left0 + block * going)), scale * (coming + rho * going),
        scale * (rho * coming + going), scale * (rho * (right1 + block * coming) + after),
    )
    for i, value in enumerate(ghosts):
        line_ref[pl.ds(i, count, stride=4), :] = value
    tiles = [line_ref[8 * tile : 8 * tile + 8, :] for tile in range(TILES)]
    cells = joined(fast(stacked(jnp.concatenate(tiles, 1)), back_ref[...]), 8, 2 * ROWS)
    ends = rims_ref[24:26, :]
    is_first = ids((8, COLS), 0) % 4 < 2
    rims = []
    for plane in range(2):
        both = []
        for side in range(2):
            at = 4 * plane + 2 * side
            lines = [jnp.where(is_first, tile[at : at + 1], tile[at + 1 : at + 2]) for tile in tiles]
            both.append(jnp.concatenate([rims_ref[8 * i : 8 * i + 8, :] * line for i, line in enumerate(lines)], 1))
        rows = slice(GROUP * OWNED * plane, GROUP * OWNED * (plane + 1))
        product = joined(fast(stacked(jnp.concatenate(both, 0)), cauchy_ref[rows, :]), 16)
        rims.append(product[:8] * ends[0:1] + product[8:] * ends[1:2])
    out = []
    for core in range(2):
        for low in range(2):
            at = 2 * core + low
            out += pack([cells[2 * i + core : 2 * i + core + 1, ROWS * low : ROWS * (low + 1)] for i in range(4)])
            out += [rims[plane][4 * g + at : 4 * g + at + 1] for plane in range(2) for g in range(2)]
    out_ref[...] = jnp.concatenate(out, 0)


def final_kernel(in_ref, own_ref, freq_ref, solve_ref, boxes_ref, out_hbm, out_ref, sems):
    total = (in_ref[0:CHUNK, :] + in_ref[CHUNK : 2 * CHUNK, :]) + (in_ref[2 * CHUNK : 3 * CHUNK, :] + in_ref[3 * CHUNK :, :])
    sides = unpack([total[i : i + 1] for i in range(6)])
    rims = total[6:10] + own_ref[0:4, :]
    sine, sine_z = boxes_ref[:SINE_Z, :ROWS], boxes_ref[SINE_Z:ENDS, :]
    ends_y, ends_z = boxes_ref[ENDS:EDGES, :ROWS].astype(F32), boxes_ref[EDGES:PICK, :COLS].astype(F32)
    ends_y, ends_z = ends_y[0:2] + ends_y[8:10], ends_z[0:2] + ends_z[8:10]
    freqs = []
    for plane in range(2):
        rows = slice(ROWS * plane, ROWS * (plane + 1))
        lhs = pieces(jnp.concatenate([ends_y] + sides[2 * plane : 2 * plane + 2] + [jnp.zeros((4, ROWS), F32)], 0))
        rhs = pieces(jnp.concatenate([rims[2 * plane : 2 * plane + 2], ends_z, jnp.zeros((4, COLS), F32)], 0))
        lhs = jnp.concatenate([lhs[0], lhs[0], lhs[1], lhs[1]], 0).astype(BF16)
        rhs = jnp.concatenate([rhs[0], rhs[1], rhs[0], rhs[1]], 0).astype(BF16)
        freqs.append(stacked((freq_ref[rows, :] - fast(lhs, rhs, ((0,), (0,)))) * solve_ref[rows, :]))
    product = fast(jnp.concatenate(freqs, 0), sine_z)
    lines = [beside(joined(product[2 * ROWS * p : 2 * ROWS * (p + 1)], ROWS)) for p in range(2)]
    product = fast(sine, jnp.concatenate(lines, 1))
    copies = []
    for plane in range(2):
        out_ref[plane] = joined(product, ROWS, at=256 * plane)
        copies += start([(out_ref.at[plane], out_hbm.at[plane])], sems.at[pl.ds(plane, 1)])
    for copy in copies:
        copy.wait()


VMEM = pl.BlockSpec(memory_space=pltpu.VMEM)
HBM = pl.BlockSpec(memory_space=pltpu.HBM)


def call(kernel, shapes, specs, *operands, scratch=(), into=VMEM):
    outs = [jax.ShapeDtypeStruct(s[0], s[1]) if isinstance(s[0], tuple) else jax.ShapeDtypeStruct(s, F32) for s in shapes]
    operands = [pltpu.with_memory_space_constraint(x, pltpu.HBM) if s is HBM else x for s, x in zip(specs, operands)]
    return pl.pallas_call(
        kernel,
        out_shape=outs if len(outs) > 1 else outs[0],
        in_specs=specs,
        out_specs=[into] * len(outs) if len(outs) > 1 else into,
        scratch_shapes=list(scratch),
        compiler_params=pltpu.CompilerParams(vmem_limit_bytes=24 << 20),
    )(*operands)


def exchange(block, axes):
    return lax.all_to_all(block, axes, split_axis=0, concat_axis=0, tiled=True)


def on_device(velocity, wave_x):
    whole, half = tables()
    t = {k: jnp.asarray(v) for k, v in whole.items()} | {k: jnp.asarray(v, BF16) for k, v in half.items()}
    sent, freq, solve, boxes, chain, reach, cauchy, ring, pair, rims, mix, into, back = call(
        box_kernel,
        [
            (PEERS * CHUNK, COLS), (2 * ROWS, COLS), (2 * ROWS, COLS), ((BOX_ROWS, 256), BF16),
            (64 * WALLS, COLS), ((2 * COLS, 512), BF16), ((2 * GROUP * OWNED, 256), BF16), (12 * PAIRS, COLS), (80, COLS),
            (32, COLS), ((128, COLS), BF16), ((2 * GROUP * ROWS, 256), BF16), ((GROUP * OWNED, 4 * ROWS), BF16),
        ],
        [HBM] * 9,
        wave_x, velocity, t["both"], t["boxes"], t["shared"], t["known"], t["mix"], t["into"], t["back"],
        scratch=[
            pltpu.SMEM((2,), F32), pltpu.VMEM((3, 2, ROWS, COLS), F32), pltpu.VMEM((ROWS, COLS), F32),
            pltpu.VMEM((SHARED_ROWS, 256), F32), pltpu.VMEM((CLASS_ROWS, COLS), F32), pltpu.SemaphoreType.DMA((10,)),
        ],
    )
    sent = exchange(sent.reshape(PEERS * CHUNK // 2, 2, COLS), ("core", "high", "low")).reshape(PEERS * CHUNK, COLS)
    modes, own, sums = call(
        strip_kernel, [(12 * PAIRS, COLS), (8, COLS), (24, COLS)], [VMEM] * 7,
        sent, chain, reach, pair, rims, mix, into, scratch=[pltpu.VMEM((8 * PEERS, COLS), F32)],
    )
    modes = exchange(modes.reshape(6 * PAIRS, 2, COLS), "pair").reshape(12 * PAIRS, COLS)
    cells = call(
        ring_kernel, [(GROUP * CHUNK, COLS)], [VMEM] * 7, modes, sums, ring, pair, rims, back, cauchy,
        scratch=[pltpu.VMEM((24, COLS), F32)] * 2,
    )
    cells = exchange(cells.reshape(GROUP * CHUNK // 2, 2, COLS), ("core", "low")).reshape(GROUP * CHUNK, COLS)
    return call(
        final_kernel, [(2, ROWS, COLS)], [VMEM] * 5, cells, own, freq, solve, boxes,
        scratch=[pltpu.VMEM((2, ROWS, COLS), F32), pltpu.SemaphoreType.DMA((2,))], into=HBM,
    )


def solution(mesh):
    fine = Mesh(mesh.devices.reshape(PAIRS, 2, WALLS // 2, 2), ("pair", "core", "high", "low"))
    wall, span = ("high", "low"), ("pair", "core")
    return jax.shard_map(
        on_device, mesh=fine, in_specs=(P(None, None, wall, span), P()), out_specs=P(None, wall, span), check_vma=False
    )
```

```python
import jax
import jax.numpy as jnp
import numpy as np
from jax import lax
from jax.experimental import pallas as pl
from jax.experimental.pallas import tpu as pltpu
from jax.sharding import Mesh, PartitionSpec as P

F32 = jnp.float32
BF16 = jnp.bfloat16
EXACT = lax.Precision.HIGHEST
NY, NZ = 1536, 8192
WALLS, STRIPS = 8, 64
PAIRS, PEERS = STRIPS // 2, 2 * WALLS
FIRST, FIRST_WALL = 23, 4
ROWS, COLS = NY // WALLS, NZ // STRIPS
GROUP = 4
OWNED = NY // PEERS
TILES = GROUP * OWNED // COLS
CHUNK = 10
SINE_Z, ENDS, EDGES, PICK, BOX_ROWS = 384, 640, 656, 672, 688
GHOST, MU_ROW, MU_COL, CLASS_ROWS = 0, 24, 48, 432
PHI, LAM_ROW, ENDS_Z, MU_BOX, SHARED_ROWS = 128, 136, 144, 152, 152


def halves(table):
    high = table.astype(np.float32).astype(BF16).astype(np.float64)
    return high, table - high


def sine_table(n):
    i = np.arange(1, n + 1)
    return np.sqrt(2 / (n + 1)) * np.sin(np.pi * np.outer(i, i) / (n + 1)), 4 * np.sin(np.pi * i / (2 * (n + 1))) ** 2


def tables():
    sine_y, mu_box = sine_table(ROWS)
    sine_z, lam = sine_table(COLS)
    ends_y, ends_z = sine_y[[0, -1]], sine_z[[0, -1]]
    boxes = np.zeros((BOX_ROWS, 256))
    boxes[:ROWS, :ROWS], boxes[ROWS:SINE_Z, :ROWS] = halves(sine_y)
    boxes[SINE_Z : SINE_Z + COLS, :COLS], boxes[SINE_Z : SINE_Z + COLS, COLS:] = halves(sine_z)
    boxes[SINE_Z + COLS : ENDS, :COLS] = boxes[SINE_Z : SINE_Z + COLS, :COLS]
    boxes[ENDS : ENDS + 2, :ROWS], boxes[ENDS + 8 : ENDS + 10, :ROWS] = halves(ends_y)
    boxes[EDGES : EDGES + 2, :COLS], boxes[EDGES + 8 : EDGES + 10, :COLS] = halves(ends_z)
    boxes[PICK, 0], boxes[PICK + 1, COLS - 1] = -0.5, 0.5
    both = mu_box[:, None] + lam[None, :]
    shared = np.zeros((SHARED_ROWS, 256))
    shared[:PHI, :ROWS] = both.T
    shared[:PHI, ROWS:] = 1.0
    shared[PHI:LAM_ROW, :ROWS] = ends_y[0]
    shared[LAM_ROW:ENDS_Z, :COLS] = lam
    shared[ENDS_Z : ENDS_Z + 2, :COLS] = ends_z
    r, wall = np.arange(ROWS), np.arange(WALLS)
    known = np.zeros((GROUP, 4, CLASS_ROWS, COLS))
    mix = np.zeros((GROUP, 128, COLS))
    into = np.zeros((GROUP, 2 * GROUP * ROWS, 256))
    back = np.zeros((GROUP, 4, GROUP * OWNED, 4 * ROWS))
    for c in range(GROUP):
        fold = np.zeros((64, 64))
        for k in range(GROUP):
            mode = c + 4 * k + PEERS * np.arange(OWNED)
            norm = np.where(mode == 0, np.sqrt(1 / NY), np.sqrt(2 / NY))
            angle = np.pi * np.outer(2 * r + 1, mode) / (2 * NY)
            turn = np.pi * (c + 4 * k) * wall / 8
            for n, wave in enumerate((np.cos(angle), np.sin(angle))):
                rows = slice(ROWS * (2 * k + n), ROWS * (2 * k + n + 1))
                into[c, rows, :OWNED], into[c, rows, COLS : COLS + OWNED] = halves(sine_y @ (norm * wave))
            for line in range(4):
                for core in range(2):
                    box = 16 * line + 8 * core + (wall - FIRST_WALL) % WALLS
                    fold[16 * k + 2 * line + core, box] = np.cos(turn)
                    fold[16 * k + 8 + 2 * line + core, box] = -np.sin(turn)
        mix[c, :64, :64], mix[c, 64:, :64] = halves(fold)
        mode = (c + 4 * np.arange(GROUP)[:, None] + PEERS * np.arange(OWNED)[None, :]).reshape(-1)
        norm = np.where(mode == 0, np.sqrt(1 / NY), np.sqrt(2 / NY))
        mu = 4 * np.sin(np.pi * mode / (2 * NY)) ** 2
        for high in range(4):
            for low in range(2):
                w = 2 * high + low
                table = norm[:, None] * np.cos(np.pi * np.outer(mode, 2 * (ROWS * w + r) + 1) / (2 * NY)) @ sine_y
                here, other = slice(ROWS * low, ROWS * (low + 1)), slice(ROWS * (2 + low), ROWS * (3 + low))
                back[c, high, :, here], back[c, high, :, other] = halves(table)
                for g in range(2):
                    y = ROWS * (w + g) + g - 1
                    row = (norm * np.cos(np.pi * mode * (2 * y + 1) / (2 * NY))).reshape(TILES, COLS)
                    for core in range(2):
                        known[c, high, 4 * g + 2 * core + low : MU_ROW : 8] = row
            known[c, high, MU_ROW:MU_COL] = np.concatenate([np.repeat(mu.reshape(TILES, COLS), 4, 0)] * 2)
            known[c, high, MU_COL:] = mu[:, None]
    whole = dict(both=both, shared=shared, known=known)
    half = dict(boxes=boxes, mix=mix, into=into, back=back)
    return {k: np.asarray(v, np.float32) for k, v in whole.items()}, {k: np.asarray(v, np.float32) for k, v in half.items()}


def dot(a, b, dims):
    return lax.dot_general(a, b, (dims, ((), ())), precision=EXACT, preferred_element_type=F32)


def fast(a, b, dims=((1,), (0,))):
    return lax.dot_general(a, b, (dims, ((), ())), preferred_element_type=F32)


def ids(shape, dim):
    return lax.broadcasted_iota(jnp.int32, shape, dim)


def pieces(value):
    high = value.astype(BF16).astype(F32)
    return high, value - high


def parts(value):
    return [piece.astype(BF16) for piece in pieces(value)]


def stacked(value):
    return jnp.concatenate(pieces(value), 0).astype(BF16)


def beside(value):
    return jnp.concatenate(parts(value), 1)


def summed(product):
    return product[:, :COLS] + product[:, COLS:]


def joined(product, rows, width=COLS, at=0):
    here, other = slice(at, at + width), slice(at + width, at + 2 * width)
    return product[:rows, here] + (product[:rows, other] + product[rows:, here])


def start(pairs, sems):
    copies = [pltpu.make_async_copy(*pair, sems.at[i]) for i, pair in enumerate(pairs)]
    for copy in copies:
        copy.start()
    return copies


def pack(lines):
    tails = [jnp.concatenate([lines[side][:, COLS:ROWS], lines[2 + side][:, COLS:ROWS]], 1) for side in range(2)]
    return [line[:, :COLS] for line in lines] + tails


def unpack(rows):
    return [
        jnp.concatenate([rows[2 * plane + side], rows[4 + side][:, 64 * plane : 64 * plane + 64]], 1)
        for plane in range(2) for side in range(2)
    ]


def box_kernel(
    wave_hbm, vel_hbm, both_hbm, boxes_hbm, shared_hbm, known_hbm, mix_hbm, into_hbm, back_hbm,
    out_ref, freq_ref, solve_ref, boxes_ref,
    chain_ref, reach_ref, cauchy_ref, ring_ref, pair_ref, rims_ref, mix_ref, into_ref, back_ref,
    wave_ref, vel_ref, both_ref, shared_ref, known_ref, sems,
):
    mine, high = 2 * lax.axis_index("core") + lax.axis_index("low"), lax.axis_index("high")
    copies = start([
        (wave_hbm, wave_ref), (both_hbm, both_ref), (vel_hbm.at[:, 0], vel_ref.at[:, 0]),
        (vel_hbm.at[:, 1], vel_ref.at[:, 1]), (boxes_hbm, boxes_ref), (shared_hbm, shared_ref),
        (known_hbm.at[mine, high], known_ref), (mix_hbm.at[mine], mix_ref), (into_hbm.at[mine], into_ref),
        (back_hbm.at[mine, high], back_ref),
    ], sems)
    row, lane = ids((ROWS, COLS), 0), ids((ROWS, COLS), 1)
    wall = 2 * lax.axis_index("high") + lax.axis_index("low")
    low = jnp.where(wall > 0, -0.5, 0.0)
    high = jnp.where(wall < WALLS - 1, 0.5, 0.0)
    copies[0].wait()
    copies[1].wait()
    for plane in range(2):
        wave = wave_ref[plane]
        solve_ref[ROWS * plane : ROWS * (plane + 1), :] = -1.0 / (wave * wave + both_ref[...])
    sources, rims, sides = [], [], []
    for plane in range(2):
        copies[2 + plane].wait()
        u, v, w = (vel_ref[c, plane] for c in range(3))
        above = jnp.where(row == ROWS - 1, 0.0, pltpu.roll(v, ROWS - 1, 0))
        below = jnp.where(row == 0, 0.0, pltpu.roll(v, 1, 0))
        after = jnp.where(lane == COLS - 1, 0.0, pltpu.roll(w, COLS - 1, 1))
        before = jnp.where(lane == 0, 0.0, pltpu.roll(w, 1, 1))
        sources += parts(wave_ref[plane] * u + 0.5 * ((above - below) + (after - before)))
        rims += [low * v[0:1], high * v[ROWS - 1 :]]
        sides.append(parts(w))
    for copy in copies[4:7]:
        copy.wait()
    sine, sine_z = boxes_ref[:SINE_Z, :ROWS], boxes_ref[SINE_Z : SINE_Z + COLS, :]
    product = fast(sine, jnp.concatenate(sources, 1))
    product = fast(jnp.concatenate([stacked(joined(product, ROWS, at=256 * p)) for p in range(2)], 0), sine_z)
    insides = []
    for plane in range(2):
        freq = joined(product[2 * ROWS * plane : 2 * ROWS * (plane + 1)], ROWS)
        rows = slice(ROWS * plane, ROWS * (plane + 1))
        freq_ref[rows, :] = freq
        insides.append(parts(freq * solve_ref[rows, :]))
    pick, edge = boxes_ref[PICK:BOX_ROWS, :COLS], boxes_ref[EDGES:PICK, :COLS]
    across = ((1,), (1,))
    halo = [(fast(pick, high, across) + fast(pick, low, across))[0:2] for high, low in sides]
    halo = stacked(jnp.concatenate(halo + [jnp.zeros((4, ROWS), F32)], 0))
    left, right = fast(halo, boxes_ref[:ROWS, :]), fast(halo, boxes_ref[ROWS:SINE_Z, :])
    halo = (left[0:8] + (left[8:16] + right[0:8]))[:, :ROWS]
    lines = []
    for plane, (high, low) in enumerate(insides):
        left, right = fast(edge, high, across), fast(edge, low, across)
        line = left[0:2] + (left[8:10] + right[0:2]) + halo[2 * plane : 2 * plane + 2]
        lines += [line[0:1], line[1:2]]
    ends = fast(boxes_ref[ENDS:EDGES, :ROWS], jnp.concatenate(insides[0] + insides[1], 1))
    ends = [joined(ends, 8, at=256 * p)[0:2] for p in range(2)]
    rims = fast(stacked(jnp.concatenate(rims + [jnp.zeros((4, COLS), F32)], 0)), sine_z)
    ends = jnp.concatenate(ends, 0) + joined(rims, 8)[0:4]
    four = jnp.concatenate((pack(lines) + [ends]) * 4, 0)
    for group in range(PEERS // 4):
        out_ref[4 * CHUNK * group : 4 * CHUNK * (group + 1), :] = four
    factors(wave_ref, shared_ref, known_ref, chain_ref, reach_ref, cauchy_ref, ring_ref, pair_ref, rims_ref)
    for copy in copies[7:]:
        copy.wait()


def decay(shift):
    root = jnp.sqrt(shift * (shift + 4.0))
    delta = (shift + root) / (2.0 + shift + root)
    return 1.0 - delta, delta * (2.0 - delta), -jnp.log1p(-delta)


def factors(
    wave_ref, shared_ref, known_ref, chain_ref, reach_ref, cauchy_ref, ring_ref, pair_ref, rims_ref,
):
    pair = lax.axis_index("pair")
    waves = [wave_ref[p] * wave_ref[p] for p in range(2)]
    row = ids((8, COLS), 0)
    lam = shared_ref[LAM_ROW:ENDS_Z, :COLS]
    for p in range(2):
        at = COLS * p
        reach_ref[at : at + COLS, :] = beside(shared_ref[PHI : PHI + 1, :] / (waves[p] + shared_ref[:PHI, :]))
        rows = slice(GROUP * OWNED * p, GROUP * OWNED * (p + 1))
        cauchy_ref[rows, :] = beside(1.0 / (known_ref[MU_COL:, :] + (waves[p] + lam[0:1])))
        rho, gap, theta = decay(waves[p] + lam)
        step = -1.0 * ROWS * theta
        scale = 1.0 / (gap * (1.0 - jnp.exp(-2.0 * NY * theta)))
        cross = jnp.exp(-(ROWS + 1.0) * theta)

        def reach(n):
            return jnp.exp(step * lax.bitwise_and(n, 15).astype(F32))

        here = lax.bitwise_and(row + FIRST_WALL, WALLS - 1)
        for place in range(WALLS):
            other = (place + FIRST_WALL) % WALLS
            up = reach(here - 1 - other) + rho * reach(15 - here - other)
            down = reach(here + other) + rho * reach(other - here)
            at = 32 * (WALLS * p + place)
            chain_ref[at : at + 8, :] = scale * (cross * up + down)
            chain_ref[at + 8 : at + 16, :] = scale * (up + cross * down)
            up = rho * reach(here - other) + reach(14 - here - other)
            down = rho * reach(here + 1 + other) + reach(other - here - 1)
            chain_ref[at + 16 : at + 24, :] = scale * (cross * up + down)
            chain_ref[at + 24 : at + 32, :] = scale * (up + cross * down)
    place = ids((24, COLS), 0)
    second, leftward = place % 4 >= 2, place % 2 == 0
    mu = known_ref[MU_ROW:MU_COL, :]
    _, _, theta = decay(jnp.where(second, waves[1], waves[0]) + mu)
    step = -2.0 * COLS * theta
    for group in range(PAIRS // 2):
        other = FIRST + 2 * group + place // 12
        n = lax.bitwise_and(jnp.where(leftward, other - pair - 1, pair - 1 - other), PAIRS - 1)
        ring_ref[24 * group : 24 * group + 24, :] = jnp.exp(step * n.astype(F32))
    coefs = [[], [], [], []]
    for tile in range(TILES):
        rho, gap, theta = decay(jnp.where(row >= 4, waves[1], waves[0]) + mu[4 * tile : 4 * tile + 1])
        block = jnp.exp(-1.0 * COLS * theta)
        pair_ref[8 * tile : 8 * tile + 8, :] = jnp.exp(-(COLS + 1.0) * theta)
        pair_ref[24 + 8 * tile : 32 + 8 * tile, :] = block
        period = 1.0 - jnp.exp(-1.0 * NZ * theta)
        for i, value in enumerate((rho, 1.0 / (gap * period), period, block)):
            coefs[i] += [value[0:1], value[4:5]]
    for i in range(4):
        pair_ref[48 + 8 * i : 56 + 8 * i, :] = jnp.concatenate(coefs[i] + coefs[i][:2], 0)
    rims_ref[0:24, :] = known_ref[GHOST:MU_ROW, :]
    rims_ref[24:32, :] = shared_ref[ENDS_Z:MU_BOX, :COLS]


def strip_kernel(in_ref, chain_ref, reach_ref, pair_ref, rims_ref, mix_ref, into_ref, out_ref, own_ref, sums_ref, near_ref):
    box = [in_ref[pl.ds(i, PEERS, stride=CHUNK), :] for i in range(6)]
    ends = rims_ref[24:26, :]
    lines = unpack(box)
    even = ids((2 * PEERS, ROWS), 1) % 2 == 0
    added = []
    for plane in range(2):
        tops, bottoms = [], []
        for core in range(2):
            top = bottom = None
            for other in range(WALLS):
                at = 32 * (WALLS * plane + other)
                source = CHUNK * (WALLS * core + other) + 6 + 2 * plane
                first, last = in_ref[source : source + 1, :], in_ref[source + 1 : source + 2, :]
                weight = [chain_ref[at + 8 * i : at + 8 * i + 8, :] for i in range(4)]
                one, two = weight[0] * first + weight[1] * last, weight[2] * first + weight[3] * last
                top, bottom = (one, two) if top is None else (top + one, bottom + two)
            tops.append(top)
            bottoms.append(bottom)
        top, bottom = jnp.concatenate(tops, 0), jnp.concatenate(bottoms, 0)
        near_ref[pl.ds(2 * plane, PEERS, stride=8), :] = top
        near_ref[pl.ds(2 * plane + 1, PEERS, stride=8), :] = bottom
        sums = [value * ends[side : side + 1] for value in (top + bottom, top - bottom) for side in range(2)]
        product = fast(stacked(jnp.concatenate(sums, 0)), reach_ref[COLS * plane : COLS * (plane + 1), :])
        product = joined(product, 4 * PEERS, 256)[:, :ROWS]
        added.append(jnp.where(even, product[: 2 * PEERS], product[2 * PEERS :]))
    wall = 2 * lax.axis_index("high") + lax.axis_index("low")
    mine = 8 * lax.axis_index("core") + lax.bitwise_and(wall - FIRST_WALL, WALLS - 1)
    own_ref[...] = near_ref[pl.ds(pl.multiple_of(8 * mine, 8), 8), :]
    lines = jnp.concatenate(lines, 0) + jnp.concatenate(added, 0)
    lines = jnp.concatenate([lines, jnp.zeros((4 * PEERS, 256 - ROWS), F32)], 1)
    folded = joined(fast(mix_ref[:, :64], beside(lines)), 64, 256)
    modes = []
    for k in range(GROUP):
        both = jnp.concatenate([folded[16 * k : 16 * k + 8, :ROWS], folded[16 * k + 8 : 16 * k + 16, :ROWS]], 1)
        modes.append(joined(fast(stacked(both), into_ref[2 * ROWS * k : 2 * ROWS * (k + 1), :]), 8))
    modes = [modes[0]] + [pltpu.roll(modes[k], COLS - 32 * k, 1) for k in range(1, GROUP)]
    row, lane = ids((8, COLS), 0), ids((8, COLS), 1)
    out = []
    for tile in range(TILES):
        value = jnp.where(lane < 96 - 32 * tile, modes[tile], modes[tile + 1])
        at = 8 * tile
        near = jnp.where(row % 4 < 2, pltpu.roll(value, 6, 0), pltpu.roll(value, 2, 0))
        value = value + pair_ref[at : at + 8, :] * near
        sums_ref[at : at + 8, :] = value
        near = jnp.where(row % 2 == 0, pltpu.roll(value, 7, 0), pltpu.roll(value, 1, 0))
        value = value + pair_ref[24 + at : 32 + at, :] * near
        out += [value[0:1], value[3:5], value[7:8]]
    sums_ref[24:32, :] = jnp.zeros((8, COLS), F32)
    out = jnp.concatenate(out * 2, 0)
    for group in range(PAIRS // 2):
        out_ref[24 * group : 24 * group + 24, :] = out


def ring_kernel(in_ref, sums_ref, ring_ref, pair_ref, rims_ref, back_ref, cauchy_ref, out_ref, far_ref, line_ref):
    total = in_ref[0:24, :] * ring_ref[0:24, :]
    for group in range(1, PAIRS // 2):
        total = total + in_ref[24 * group : 24 * group + 24, :] * ring_ref[24 * group : 24 * group + 24, :]
    far_ref[0:24, :] = total
    far_ref[24:32, :] = jnp.zeros((8, COLS), F32)
    count = 2 * TILES
    after, before = (
        far_ref[pl.ds(i, count, stride=2), :] + far_ref[pl.ds(12 + i, count, stride=2), :] for i in range(2)
    )
    rho, scale, period, block = (pair_ref[48 + 8 * i : 48 + 8 * i + count, :] for i in range(4))
    left0, left1, right0, right1 = (period * sums_ref[pl.ds(i, count, stride=4), :] for i in range(4))
    coming, going = block * before + right0, block * after + left1
    ghosts = (
        scale * (before + rho * (left0 + block * going)), scale * (coming + rho * going),
        scale * (rho * coming + going), scale * (rho * (right1 + block * coming) + after),
    )
    for i, value in enumerate(ghosts):
        line_ref[pl.ds(i, count, stride=4), :] = value
    tiles = [line_ref[8 * tile : 8 * tile + 8, :] for tile in range(TILES)]
    cells = joined(fast(stacked(jnp.concatenate(tiles, 1)), back_ref[...]), 8, 2 * ROWS)
    ends = rims_ref[24:26, :]
    is_first = ids((8, COLS), 0) % 4 < 2
    rims = []
    for plane in range(2):
        both = []
        for side in range(2):
            at = 4 * plane + 2 * side
            lines = [jnp.where(is_first, tile[at : at + 1], tile[at + 1 : at + 2]) for tile in tiles]
            both.append(jnp.concatenate([rims_ref[8 * i : 8 * i + 8, :] * line for i, line in enumerate(lines)], 1))
        rows = slice(GROUP * OWNED * plane, GROUP * OWNED * (plane + 1))
        product = joined(fast(stacked(jnp.concatenate(both, 0)), cauchy_ref[rows, :]), 16)
        rims.append(product[:8] * ends[0:1] + product[8:] * ends[1:2])
    out = []
    for core in range(2):
        for low in range(2):
            at = 2 * core + low
            out += pack([cells[2 * i + core : 2 * i + core + 1, ROWS * low : ROWS * (low + 1)] for i in range(4)])
            out += [rims[plane][4 * g + at : 4 * g + at + 1] for plane in range(2) for g in range(2)]
    out_ref[...] = jnp.concatenate(out, 0)


def final_kernel(in_ref, own_ref, freq_ref, solve_ref, boxes_ref, out_hbm, out_ref, sems):
    total = (in_ref[0:CHUNK, :] + in_ref[CHUNK : 2 * CHUNK, :]) + (in_ref[2 * CHUNK : 3 * CHUNK, :] + in_ref[3 * CHUNK :, :])
    sides = unpack([total[i : i + 1] for i in range(6)])
    rims = total[6:10] + own_ref[0:4, :]
    sine, sine_z = boxes_ref[:SINE_Z, :ROWS], boxes_ref[SINE_Z:ENDS, :]
    ends_y, ends_z = boxes_ref[ENDS:EDGES, :ROWS].astype(F32), boxes_ref[EDGES:PICK, :COLS].astype(F32)
    ends_y, ends_z = ends_y[0:2] + ends_y[8:10], ends_z[0:2] + ends_z[8:10]
    freqs = []
    for plane in range(2):
        rows = slice(ROWS * plane, ROWS * (plane + 1))
        lhs = pieces(jnp.concatenate([ends_y] + sides[2 * plane : 2 * plane + 2] + [jnp.zeros((4, ROWS), F32)], 0))
        rhs = pieces(jnp.concatenate([rims[2 * plane : 2 * plane + 2], ends_z, jnp.zeros((4, COLS), F32)], 0))
        lhs = jnp.concatenate([lhs[0], lhs[0], lhs[1], lhs[1]], 0).astype(BF16)
        rhs = jnp.concatenate([rhs[0], rhs[1], rhs[0], rhs[1]], 0).astype(BF16)
        freqs.append(beside((freq_ref[rows, :] - fast(lhs, rhs, ((0,), (0,)))) * solve_ref[rows, :]))
    product = summed(fast(jnp.concatenate(freqs, 0), sine_z))
    lines = [beside(product[ROWS * p : ROWS * (p + 1)]) for p in range(2)]
    product = fast(sine, jnp.concatenate(lines, 1))
    copies = []
    for plane in range(2):
        out_ref[plane] = joined(product, ROWS, at=256 * plane)
        copies += start([(out_ref.at[plane], out_hbm.at[plane])], sems.at[pl.ds(plane, 1)])
    for copy in copies:
        copy.wait()


VMEM = pl.BlockSpec(memory_space=pltpu.VMEM)
HBM = pl.BlockSpec(memory_space=pltpu.HBM)


def call(kernel, shapes, specs, *operands, scratch=(), into=VMEM):
    outs = [jax.ShapeDtypeStruct(s[0], s[1]) if isinstance(s[0], tuple) else jax.ShapeDtypeStruct(s, F32) for s in shapes]
    operands = [pltpu.with_memory_space_constraint(x, pltpu.HBM) if s is HBM else x for s, x in zip(specs, operands)]
    return pl.pallas_call(
        kernel,
        out_shape=outs if len(outs) > 1 else outs[0],
        in_specs=specs,
        out_specs=[into] * len(outs) if len(outs) > 1 else into,
        scratch_shapes=list(scratch),
        compiler_params=pltpu.CompilerParams(vmem_limit_bytes=24 << 20),
    )(*operands)


def exchange(block, axes, order=None):
    groups = None if order is None else [order]
    return lax.all_to_all(block, axes, split_axis=0, concat_axis=0, tiled=True, axis_index_groups=groups)


def on_device(velocity, wave_x):
    whole, half = tables()
    t = {k: jnp.asarray(v) for k, v in whole.items()} | {k: jnp.asarray(v, BF16) for k, v in half.items()}
    sent, freq, solve, boxes, chain, reach, cauchy, ring, pair, rims, mix, into, back = call(
        box_kernel,
        [
            (PEERS * CHUNK, COLS), (2 * ROWS, COLS), (2 * ROWS, COLS), ((BOX_ROWS, 256), BF16),
            (64 * WALLS, COLS), ((2 * COLS, 512), BF16), ((2 * GROUP * OWNED, 256), BF16), (12 * PAIRS, COLS), (80, COLS),
            (32, COLS), ((128, COLS), BF16), ((2 * GROUP * ROWS, 256), BF16), ((GROUP * OWNED, 4 * ROWS), BF16),
        ],
        [HBM] * 9,
        wave_x, velocity, t["both"], t["boxes"], t["shared"], t["known"], t["mix"], t["into"], t["back"],
        scratch=[
            pltpu.SMEM((2,), F32), pltpu.VMEM((3, 2, ROWS, COLS), F32), pltpu.VMEM((ROWS, COLS), F32),
            pltpu.VMEM((SHARED_ROWS, 256), F32), pltpu.VMEM((CLASS_ROWS, COLS), F32), pltpu.SemaphoreType.DMA((10,)),
        ],
    )
    order = [WALLS * core + (FIRST_WALL + i) % WALLS for core in range(2) for i in range(WALLS)]
    sent = exchange(sent.reshape(PEERS * CHUNK // 2, 2, COLS), ("core", "high", "low"), order).reshape(PEERS * CHUNK, COLS)
    modes, own, sums = call(
        strip_kernel, [(12 * PAIRS, COLS), (8, COLS), (32, COLS)], [VMEM] * 7,
        sent, chain, reach, pair, rims, mix, into, scratch=[pltpu.VMEM((8 * PEERS, COLS), F32)],
    )
    modes = exchange(modes.reshape(6 * PAIRS, 2, COLS), "pair", [(FIRST + i) % PAIRS for i in range(PAIRS)]).reshape(12 * PAIRS, COLS)
    cells = call(
        ring_kernel, [(GROUP * CHUNK, COLS)], [VMEM] * 7, modes, sums, ring, pair, rims, back, cauchy,
        scratch=[pltpu.VMEM((32, COLS), F32)] * 2,
    )
    cells = exchange(cells.reshape(GROUP * CHUNK // 2, 2, COLS), ("core", "low")).reshape(GROUP * CHUNK, COLS)
    return call(
        final_kernel, [(2, ROWS, COLS)], [VMEM] * 5, cells, own, freq, solve, boxes,
        scratch=[pltpu.VMEM((2, ROWS, COLS), F32), pltpu.SemaphoreType.DMA((2,))], into=HBM,
    )


def solution(mesh):
    fine = Mesh(mesh.devices.reshape(PAIRS, 2, WALLS // 2, 2), ("pair", "core", "high", "low"))
    wall, span = ("high", "low"), ("pair", "core")
    return jax.shard_map(
        on_device, mesh=fine, in_specs=(P(None, None, wall, span), P()), out_specs=P(None, wall, span), check_vma=False
    )
```

```python
import jax
import jax.numpy as jnp
import numpy as np
from jax import lax
from jax.experimental import pallas as pl
from jax.experimental.pallas import tpu as pltpu
from jax.sharding import Mesh, PartitionSpec as P

F32 = jnp.float32
BF16 = jnp.bfloat16
EXACT = lax.Precision.HIGHEST
NY, NZ = 1536, 8192
WALLS, STRIPS = 8, 64
PAIRS, PEERS = STRIPS // 2, 2 * WALLS
FIRST, FIRST_WALL = 23, 4
ROWS, COLS = NY // WALLS, NZ // STRIPS
GROUP = 4
OWNED = NY // PEERS
TILES = GROUP * OWNED // COLS
CHUNK = 10
SINE_Z, ENDS, EDGES, PICK, BOX_ROWS = 384, 640, 656, 672, 688
GHOST, MU_ROW, MU_COL, CLASS_ROWS = 0, 24, 48, 432
PHI, LAM_ROW, ENDS_Z, MU_BOX, SHARED_ROWS = 128, 136, 144, 152, 152


def halves(table):
    high = table.astype(np.float32).astype(BF16).astype(np.float64)
    return high, table - high


def sine_table(n):
    i = np.arange(1, n + 1)
    return np.sqrt(2 / (n + 1)) * np.sin(np.pi * np.outer(i, i) / (n + 1)), 4 * np.sin(np.pi * i / (2 * (n + 1))) ** 2


def tables():
    sine_y, mu_box = sine_table(ROWS)
    sine_z, lam = sine_table(COLS)
    ends_y, ends_z = sine_y[[0, -1]], sine_z[[0, -1]]
    boxes = np.zeros((BOX_ROWS, 256))
    boxes[:ROWS, :ROWS], boxes[ROWS:SINE_Z, :ROWS] = halves(sine_y)
    boxes[SINE_Z : SINE_Z + COLS, :COLS], boxes[SINE_Z : SINE_Z + COLS, COLS:] = halves(sine_z)
    boxes[SINE_Z + COLS : ENDS, :COLS] = boxes[SINE_Z : SINE_Z + COLS, :COLS]
    boxes[ENDS : ENDS + 2, :ROWS], boxes[ENDS + 8 : ENDS + 10, :ROWS] = halves(ends_y)
    boxes[EDGES : EDGES + 2, :COLS], boxes[EDGES + 8 : EDGES + 10, :COLS] = halves(ends_z)
    boxes[PICK, 0], boxes[PICK + 1, COLS - 1] = -0.5, 0.5
    both = mu_box[:, None] + lam[None, :]
    shared = np.zeros((SHARED_ROWS, 256))
    shared[:PHI, :ROWS] = both.T
    shared[:PHI, ROWS:] = 1.0
    shared[PHI:LAM_ROW, :ROWS] = ends_y[0]
    shared[LAM_ROW:ENDS_Z, :COLS] = lam
    shared[ENDS_Z : ENDS_Z + 2, :COLS] = ends_z
    r, wall = np.arange(ROWS), np.arange(WALLS)
    known = np.zeros((GROUP, 4, CLASS_ROWS, COLS))
    mix = np.zeros((GROUP, 128, COLS))
    into = np.zeros((GROUP, 2 * GROUP * ROWS, 256))
    back = np.zeros((GROUP, 4, GROUP * OWNED, 4 * ROWS))
    for c in range(GROUP):
        fold = np.zeros((64, 64))
        for k in range(GROUP):
            mode = c + 4 * k + PEERS * np.arange(OWNED)
            norm = np.where(mode == 0, np.sqrt(1 / NY), np.sqrt(2 / NY))
            angle = np.pi * np.outer(2 * r + 1, mode) / (2 * NY)
            turn = np.pi * (c + 4 * k) * wall / 8
            for n, wave in enumerate((np.cos(angle), np.sin(angle))):
                rows = slice(ROWS * (2 * k + n), ROWS * (2 * k + n + 1))
                into[c, rows, :OWNED], into[c, rows, COLS : COLS + OWNED] = halves(sine_y @ (norm * wave))
            for line in range(4):
                for core in range(2):
                    box = 16 * line + 8 * (1 - core) + (wall - FIRST_WALL) % WALLS
                    fold[16 * k + 2 * line + core, box] = np.cos(turn)
                    fold[16 * k + 8 + 2 * line + core, box] = -np.sin(turn)
        mix[c, :64, :64], mix[c, 64:, :64] = halves(fold)
        mode = (c + 4 * np.arange(GROUP)[:, None] + PEERS * np.arange(OWNED)[None, :]).reshape(-1)
        norm = np.where(mode == 0, np.sqrt(1 / NY), np.sqrt(2 / NY))
        mu = 4 * np.sin(np.pi * mode / (2 * NY)) ** 2
        for high in range(4):
            for low in range(2):
                w = 2 * high + low
                table = norm[:, None] * np.cos(np.pi * np.outer(mode, 2 * (ROWS * w + r) + 1) / (2 * NY)) @ sine_y
                here, other = slice(ROWS * low, ROWS * (low + 1)), slice(ROWS * (2 + low), ROWS * (3 + low))
                back[c, high, :, here], back[c, high, :, other] = halves(table)
                for g in range(2):
                    y = ROWS * (w + g) + g - 1
                    row = (norm * np.cos(np.pi * mode * (2 * y + 1) / (2 * NY))).reshape(TILES, COLS)
                    for core in range(2):
                        known[c, high, 4 * g + 2 * core + low : MU_ROW : 8] = row
            known[c, high, MU_ROW:MU_COL] = np.concatenate([np.repeat(mu.reshape(TILES, COLS), 4, 0)] * 2)
            known[c, high, MU_COL:] = mu[:, None]
    whole = dict(both=both, shared=shared, known=known)
    half = dict(boxes=boxes, mix=mix, into=into, back=back)
    return {k: np.asarray(v, np.float32) for k, v in whole.items()}, {k: np.asarray(v, np.float32) for k, v in half.items()}


def dot(a, b, dims):
    return lax.dot_general(a, b, (dims, ((), ())), precision=EXACT, preferred_element_type=F32)


def fast(a, b, dims=((1,), (0,))):
    return lax.dot_general(a, b, (dims, ((), ())), preferred_element_type=F32)


def ids(shape, dim):
    return lax.broadcasted_iota(jnp.int32, shape, dim)


def pieces(value):
    high = value.astype(BF16).astype(F32)
    return high, value - high


def parts(value):
    return [piece.astype(BF16) for piece in pieces(value)]


def stacked(value):
    return jnp.concatenate(pieces(value), 0).astype(BF16)


def beside(value):
    return jnp.concatenate(parts(value), 1)


def summed(product):
    return product[:, :COLS] + product[:, COLS:]


def joined(product, rows, width=COLS, at=0):
    here, other = slice(at, at + width), slice(at + width, at + 2 * width)
    return product[:rows, here] + (product[:rows, other] + product[rows:, here])


def start(pairs, sems):
    copies = [pltpu.make_async_copy(*pair, sems.at[i]) for i, pair in enumerate(pairs)]
    for copy in copies:
        copy.start()
    return copies


def pack(lines):
    tails = [jnp.concatenate([lines[side][:, COLS:ROWS], lines[2 + side][:, COLS:ROWS]], 1) for side in range(2)]
    return [line[:, :COLS] for line in lines] + tails


def unpack(rows):
    return [
        jnp.concatenate([rows[2 * plane + side], rows[4 + side][:, 64 * plane : 64 * plane + 64]], 1)
        for plane in range(2) for side in range(2)
    ]


def box_kernel(
    wave_hbm, vel_hbm, both_hbm, boxes_hbm, shared_hbm, known_hbm, mix_hbm, into_hbm, back_hbm,
    out_ref, freq_ref, solve_ref, boxes_ref,
    chain_ref, reach_ref, cauchy_ref, ring_ref, pair_ref, rims_ref, mix_ref, into_ref, back_ref,
    wave_ref, vel_ref, both_ref, shared_ref, known_ref, sems,
):
    mine, high = 2 * lax.axis_index("core") + lax.axis_index("low"), lax.axis_index("high")
    copies = start([
        (wave_hbm, wave_ref), (both_hbm, both_ref), (vel_hbm.at[:, 0], vel_ref.at[:, 0]),
        (vel_hbm.at[:, 1], vel_ref.at[:, 1]), (boxes_hbm, boxes_ref), (shared_hbm, shared_ref),
        (known_hbm.at[mine, high], known_ref), (mix_hbm.at[mine], mix_ref), (into_hbm.at[mine], into_ref),
        (back_hbm.at[mine, high], back_ref),
    ], sems)
    row, lane = ids((ROWS, COLS), 0), ids((ROWS, COLS), 1)
    wall = 2 * lax.axis_index("high") + lax.axis_index("low")
    low = jnp.where(wall > 0, -0.5, 0.0)
    high = jnp.where(wall < WALLS - 1, 0.5, 0.0)
    copies[0].wait()
    copies[1].wait()
    for plane in range(2):
        wave = wave_ref[plane]
        solve_ref[ROWS * plane : ROWS * (plane + 1), :] = -1.0 / (wave * wave + both_ref[...])
    sources, rims, sides = [], [], []
    for plane in range(2):
        copies[2 + plane].wait()
        u, v, w = (vel_ref[c, plane] for c in range(3))
        above = jnp.where(row == ROWS - 1, 0.0, pltpu.roll(v, ROWS - 1, 0))
        below = jnp.where(row == 0, 0.0, pltpu.roll(v, 1, 0))
        after = jnp.where(lane == COLS - 1, 0.0, pltpu.roll(w, COLS - 1, 1))
        before = jnp.where(lane == 0, 0.0, pltpu.roll(w, 1, 1))
        sources += parts(wave_ref[plane] * u + 0.5 * ((above - below) + (after - before)))
        rims += [low * v[0:1], high * v[ROWS - 1 :]]
        sides.append(parts(w))
    for copy in copies[4:7]:
        copy.wait()
    sine, sine_z = boxes_ref[:SINE_Z, :ROWS], boxes_ref[SINE_Z : SINE_Z + COLS, :]
    product = fast(sine, jnp.concatenate(sources, 1))
    product = fast(jnp.concatenate([stacked(joined(product, ROWS, at=256 * p)) for p in range(2)], 0), sine_z)
    insides = []
    for plane in range(2):
        freq = joined(product[2 * ROWS * plane : 2 * ROWS * (plane + 1)], ROWS)
        rows = slice(ROWS * plane, ROWS * (plane + 1))
        freq_ref[rows, :] = freq
        insides.append(parts(freq * solve_ref[rows, :]))
    pick, edge = boxes_ref[PICK:BOX_ROWS, :COLS], boxes_ref[EDGES:PICK, :COLS]
    across = ((1,), (1,))
    halo = [(fast(pick, high, across) + fast(pick, low, across))[0:2] for high, low in sides]
    halo = stacked(jnp.concatenate(halo + [jnp.zeros((4, ROWS), F32)], 0))
    left, right = fast(halo, boxes_ref[:ROWS, :]), fast(halo, boxes_ref[ROWS:SINE_Z, :])
    halo = (left[0:8] + (left[8:16] + right[0:8]))[:, :ROWS]
    lines = []
    for plane, (high, low) in enumerate(insides):
        left, right = fast(edge, high, across), fast(edge, low, across)
        line = left[0:2] + (left[8:10] + right[0:2]) + halo[2 * plane : 2 * plane + 2]
        lines += [line[0:1], line[1:2]]
    ends = fast(boxes_ref[ENDS:EDGES, :ROWS], jnp.concatenate(insides[0] + insides[1], 1))
    ends = [joined(ends, 8, at=256 * p)[0:2] for p in range(2)]
    rims = fast(stacked(jnp.concatenate(rims + [jnp.zeros((4, COLS), F32)], 0)), sine_z)
    ends = jnp.concatenate(ends, 0) + joined(rims, 8)[0:4]
    four = jnp.concatenate((pack(lines) + [ends]) * 4, 0)
    for group in range(PEERS // 4):
        out_ref[4 * CHUNK * group : 4 * CHUNK * (group + 1), :] = four
    factors(wave_ref, shared_ref, known_ref, chain_ref, reach_ref, cauchy_ref, ring_ref, pair_ref, rims_ref)
    for copy in copies[7:]:
        copy.wait()


def decay(shift):
    root = jnp.sqrt(shift * (shift + 4.0))
    delta = (shift + root) / (2.0 + shift + root)
    return 1.0 - delta, delta * (2.0 - delta), -jnp.log1p(-delta)


def factors(
    wave_ref, shared_ref, known_ref, chain_ref, reach_ref, cauchy_ref, ring_ref, pair_ref, rims_ref,
):
    pair = lax.axis_index("pair")
    waves = [wave_ref[p] * wave_ref[p] for p in range(2)]
    row = ids((8, COLS), 0)
    lam = shared_ref[LAM_ROW:ENDS_Z, :COLS]
    for p in range(2):
        at = COLS * p
        reach_ref[at : at + COLS, :] = beside(shared_ref[PHI : PHI + 1, :] / (waves[p] + shared_ref[:PHI, :]))
        rows = slice(GROUP * OWNED * p, GROUP * OWNED * (p + 1))
        cauchy_ref[rows, :] = beside(1.0 / (known_ref[MU_COL:, :] + (waves[p] + lam[0:1])))
        rho, gap, theta = decay(waves[p] + lam)
        step = -1.0 * ROWS * theta
        scale = 1.0 / (gap * (1.0 - jnp.exp(-2.0 * NY * theta)))
        cross = jnp.exp(-(ROWS + 1.0) * theta)

        def reach(n):
            return jnp.exp(step * lax.bitwise_and(n, 15).astype(F32))

        here = lax.bitwise_and(row + FIRST_WALL, WALLS - 1)
        for place in range(WALLS):
            other = (place + FIRST_WALL) % WALLS
            up = reach(here - 1 - other) + rho * reach(15 - here - other)
            down = reach(here + other) + rho * reach(other - here)
            at = 32 * (WALLS * p + place)
            chain_ref[at : at + 8, :] = scale * (cross * up + down)
            chain_ref[at + 8 : at + 16, :] = scale * (up + cross * down)
            up = rho * reach(here - other) + reach(14 - here - other)
            down = rho * reach(here + 1 + other) + reach(other - here - 1)
            chain_ref[at + 16 : at + 24, :] = scale * (cross * up + down)
            chain_ref[at + 24 : at + 32, :] = scale * (up + cross * down)
    place = ids((24, COLS), 0)
    second, leftward = place % 4 >= 2, place % 2 == 0
    mu = known_ref[MU_ROW:MU_COL, :]
    _, _, theta = decay(jnp.where(second, waves[1], waves[0]) + mu)
    step = -2.0 * COLS * theta
    for group in range(PAIRS // 2):
        other = FIRST + 2 * group + place // 12
        n = lax.bitwise_and(jnp.where(leftward, other - pair - 1, pair - 1 - other), PAIRS - 1)
        ring_ref[24 * group : 24 * group + 24, :] = jnp.exp(step * n.astype(F32))
    coefs = [[], [], [], []]
    for tile in range(TILES):
        rho, gap, theta = decay(jnp.where(row >= 4, waves[1], waves[0]) + mu[4 * tile : 4 * tile + 1])
        block = jnp.exp(-1.0 * COLS * theta)
        pair_ref[8 * tile : 8 * tile + 8, :] = jnp.exp(-(COLS + 1.0) * theta)
        pair_ref[24 + 8 * tile : 32 + 8 * tile, :] = block
        period = 1.0 - jnp.exp(-1.0 * NZ * theta)
        for i, value in enumerate((rho, 1.0 / (gap * period), period, block)):
            coefs[i] += [value[0:1], value[4:5]]
    for i in range(4):
        pair_ref[48 + 8 * i : 56 + 8 * i, :] = jnp.concatenate(coefs[i] + coefs[i][:2], 0)
    rims_ref[0:24, :] = known_ref[GHOST:MU_ROW, :]
    rims_ref[24:32, :] = shared_ref[ENDS_Z:MU_BOX, :COLS]


def strip_kernel(in_ref, chain_ref, reach_ref, pair_ref, rims_ref, mix_ref, into_ref, out_ref, own_ref, sums_ref, near_ref):
    box = [in_ref[pl.ds(i, PEERS, stride=CHUNK), :] for i in range(6)]
    ends = rims_ref[24:26, :]
    lines = unpack(box)
    even = ids((2 * PEERS, ROWS), 1) % 2 == 0
    added = []
    for plane in range(2):
        tops, bottoms = [], []
        for core in range(2):
            top = bottom = None
            for other in range(WALLS):
                at = 32 * (WALLS * plane + other)
                source = CHUNK * (WALLS * core + other) + 6 + 2 * plane
                first, last = in_ref[source : source + 1, :], in_ref[source + 1 : source + 2, :]
                weight = [chain_ref[at + 8 * i : at + 8 * i + 8, :] for i in range(4)]
                one, two = weight[0] * first + weight[1] * last, weight[2] * first + weight[3] * last
                top, bottom = (one, two) if top is None else (top + one, bottom + two)
            tops.append(top)
            bottoms.append(bottom)
        top, bottom = jnp.concatenate(tops, 0), jnp.concatenate(bottoms, 0)
        near_ref[pl.ds(2 * plane, PEERS, stride=8), :] = top
        near_ref[pl.ds(2 * plane + 1, PEERS, stride=8), :] = bottom
        sums = [value * ends[side : side + 1] for value in (top + bottom, top - bottom) for side in range(2)]
        product = fast(stacked(jnp.concatenate(sums, 0)), reach_ref[COLS * plane : COLS * (plane + 1), :])
        product = joined(product, 4 * PEERS, 256)[:, :ROWS]
        added.append(jnp.where(even, product[: 2 * PEERS], product[2 * PEERS :]))
    wall = 2 * lax.axis_index("high") + lax.axis_index("low")
    mine = 8 * (1 - lax.axis_index("core")) + lax.bitwise_and(wall - FIRST_WALL, WALLS - 1)
    own_ref[...] = near_ref[pl.ds(pl.multiple_of(8 * mine, 8), 8), :]
    lines = jnp.concatenate(lines, 0) + jnp.concatenate(added, 0)
    lines = jnp.concatenate([lines, jnp.zeros((4 * PEERS, 256 - ROWS), F32)], 1)
    folded = joined(fast(mix_ref[:, :64], beside(lines)), 64, 256)
    modes = []
    for k in range(GROUP):
        both = jnp.concatenate([folded[16 * k : 16 * k + 8, :ROWS], folded[16 * k + 8 : 16 * k + 16, :ROWS]], 1)
        modes.append(joined(fast(stacked(both), into_ref[2 * ROWS * k : 2 * ROWS * (k + 1), :]), 8))
    modes = [modes[0]] + [pltpu.roll(modes[k], COLS - 32 * k, 1) for k in range(1, GROUP)]
    row, lane = ids((8, COLS), 0), ids((8, COLS), 1)
    out = []
    for tile in range(TILES):
        value = jnp.where(lane < 96 - 32 * tile, modes[tile], modes[tile + 1])
        at = 8 * tile
        near = jnp.where(row % 4 < 2, pltpu.roll(value, 6, 0), pltpu.roll(value, 2, 0))
        value = value + pair_ref[at : at + 8, :] * near
        sums_ref[at : at + 8, :] = value
        near = jnp.where(row % 2 == 0, pltpu.roll(value, 7, 0), pltpu.roll(value, 1, 0))
        value = value + pair_ref[24 + at : 32 + at, :] * near
        out += [value[0:1], value[3:5], value[7:8]]
    sums_ref[24:32, :] = jnp.zeros((8, COLS), F32)
    out = jnp.concatenate(out * 2, 0)
    for group in range(PAIRS // 2):
        out_ref[24 * group : 24 * group + 24, :] = out


def ring_kernel(in_ref, sums_ref, ring_ref, pair_ref, rims_ref, back_ref, cauchy_ref, out_ref, far_ref, line_ref):
    total = in_ref[0:24, :] * ring_ref[0:24, :]
    for group in range(1, PAIRS // 2):
        total = total + in_ref[24 * group : 24 * group + 24, :] * ring_ref[24 * group : 24 * group + 24, :]
    far_ref[0:24, :] = total
    far_ref[24:32, :] = jnp.zeros((8, COLS), F32)
    count = 2 * TILES
    after, before = (
        far_ref[pl.ds(i, count, stride=2), :] + far_ref[pl.ds(12 + i, count, stride=2), :] for i in range(2)
    )
    rho, scale, period, block = (pair_ref[48 + 8 * i : 48 + 8 * i + count, :] for i in range(4))
    left0, left1, right0, right1 = (period * sums_ref[pl.ds(i, count, stride=4), :] for i in range(4))
    coming, going = block * before + right0, block * after + left1
    ghosts = (
        scale * (before + rho * (left0 + block * going)), scale * (coming + rho * going),
        scale * (rho * coming + going), scale * (rho * (right1 + block * coming) + after),
    )
    for i, value in enumerate(ghosts):
        line_ref[pl.ds(i, count, stride=4), :] = value
    tiles = [line_ref[8 * tile : 8 * tile + 8, :] for tile in range(TILES)]
    cells = joined(fast(stacked(jnp.concatenate(tiles, 1)), back_ref[...]), 8, 2 * ROWS)
    ends = rims_ref[24:26, :]
    is_first = ids((8, COLS), 0) % 4 < 2
    rims = []
    for plane in range(2):
        both = []
        for side in range(2):
            at = 4 * plane + 2 * side
            lines = [jnp.where(is_first, tile[at : at + 1], tile[at + 1 : at + 2]) for tile in tiles]
            both.append(jnp.concatenate([rims_ref[8 * i : 8 * i + 8, :] * line for i, line in enumerate(lines)], 1))
        rows = slice(GROUP * OWNED * plane, GROUP * OWNED * (plane + 1))
        product = joined(fast(stacked(jnp.concatenate(both, 0)), cauchy_ref[rows, :]), 16)
        rims.append(product[:8] * ends[0:1] + product[8:] * ends[1:2])
    out = []
    for core in (1, 0):
        for low in range(2):
            at = 2 * core + low
            out += pack([cells[2 * i + core : 2 * i + core + 1, ROWS * low : ROWS * (low + 1)] for i in range(4)])
            out += [rims[plane][4 * g + at : 4 * g + at + 1] for plane in range(2) for g in range(2)]
    out_ref[...] = jnp.concatenate(out, 0)


def final_kernel(in_ref, own_ref, freq_ref, solve_ref, boxes_ref, out_hbm, out_ref, sems):
    total = (in_ref[0:CHUNK, :] + in_ref[CHUNK : 2 * CHUNK, :]) + (in_ref[2 * CHUNK : 3 * CHUNK, :] + in_ref[3 * CHUNK :, :])
    sides = unpack([total[i : i + 1] for i in range(6)])
    rims = total[6:10] + own_ref[0:4, :]
    sine, sine_z = boxes_ref[:SINE_Z, :ROWS], boxes_ref[SINE_Z:ENDS, :]
    ends_y, ends_z = boxes_ref[ENDS:EDGES, :ROWS].astype(F32), boxes_ref[EDGES:PICK, :COLS].astype(F32)
    ends_y, ends_z = ends_y[0:2] + ends_y[8:10], ends_z[0:2] + ends_z[8:10]
    freqs = []
    for plane in range(2):
        rows = slice(ROWS * plane, ROWS * (plane + 1))
        lhs = pieces(jnp.concatenate([ends_y] + sides[2 * plane : 2 * plane + 2] + [jnp.zeros((4, ROWS), F32)], 0))
        rhs = pieces(jnp.concatenate([rims[2 * plane : 2 * plane + 2], ends_z, jnp.zeros((4, COLS), F32)], 0))
        lhs = jnp.concatenate([lhs[0], lhs[0], lhs[1], lhs[1]], 0).astype(BF16)
        rhs = jnp.concatenate([rhs[0], rhs[1], rhs[0], rhs[1]], 0).astype(BF16)
        freqs.append(beside((freq_ref[rows, :] - fast(lhs, rhs, ((0,), (0,)))) * solve_ref[rows, :]))
    product = summed(fast(jnp.concatenate(freqs, 0), sine_z))
    lines = [beside(product[ROWS * p : ROWS * (p + 1)]) for p in range(2)]
    product = fast(sine, jnp.concatenate(lines, 1))
    copies = []
    for plane in range(2):
        out_ref[plane] = joined(product, ROWS, at=256 * plane)
        copies += start([(out_ref.at[plane], out_hbm.at[plane])], sems.at[pl.ds(plane, 1)])
    for copy in copies:
        copy.wait()


VMEM = pl.BlockSpec(memory_space=pltpu.VMEM)
HBM = pl.BlockSpec(memory_space=pltpu.HBM)


def call(kernel, shapes, specs, *operands, scratch=(), into=VMEM):
    outs = [jax.ShapeDtypeStruct(s[0], s[1]) if isinstance(s[0], tuple) else jax.ShapeDtypeStruct(s, F32) for s in shapes]
    operands = [pltpu.with_memory_space_constraint(x, pltpu.HBM) if s is HBM else x for s, x in zip(specs, operands)]
    return pl.pallas_call(
        kernel,
        out_shape=outs if len(outs) > 1 else outs[0],
        in_specs=specs,
        out_specs=[into] * len(outs) if len(outs) > 1 else into,
        scratch_shapes=list(scratch),
        compiler_params=pltpu.CompilerParams(vmem_limit_bytes=24 << 20),
    )(*operands)


def exchange(block, axes, order=None):
    groups = None if order is None else [order]
    return lax.all_to_all(block, axes, split_axis=0, concat_axis=0, tiled=True, axis_index_groups=groups)


def on_device(velocity, wave_x):
    whole, half = tables()
    t = {k: jnp.asarray(v) for k, v in whole.items()} | {k: jnp.asarray(v, BF16) for k, v in half.items()}
    sent, freq, solve, boxes, chain, reach, cauchy, ring, pair, rims, mix, into, back = call(
        box_kernel,
        [
            (PEERS * CHUNK, COLS), (2 * ROWS, COLS), (2 * ROWS, COLS), ((BOX_ROWS, 256), BF16),
            (64 * WALLS, COLS), ((2 * COLS, 512), BF16), ((2 * GROUP * OWNED, 256), BF16), (12 * PAIRS, COLS), (80, COLS),
            (32, COLS), ((128, COLS), BF16), ((2 * GROUP * ROWS, 256), BF16), ((GROUP * OWNED, 4 * ROWS), BF16),
        ],
        [HBM] * 9,
        wave_x, velocity, t["both"], t["boxes"], t["shared"], t["known"], t["mix"], t["into"], t["back"],
        scratch=[
            pltpu.SMEM((2,), F32), pltpu.VMEM((3, 2, ROWS, COLS), F32), pltpu.VMEM((ROWS, COLS), F32),
            pltpu.VMEM((SHARED_ROWS, 256), F32), pltpu.VMEM((CLASS_ROWS, COLS), F32), pltpu.SemaphoreType.DMA((10,)),
        ],
    )
    near = [2 * core + low for core in (1, 0) for low in range(2)]
    order = [WALLS * core + (FIRST_WALL + i) % WALLS for core in (1, 0) for i in range(WALLS)]
    sent = exchange(sent.reshape(PEERS * CHUNK // 2, 2, COLS), ("core", "high", "low"), order).reshape(PEERS * CHUNK, COLS)
    modes, own, sums = call(
        strip_kernel, [(12 * PAIRS, COLS), (8, COLS), (32, COLS)], [VMEM] * 7,
        sent, chain, reach, pair, rims, mix, into, scratch=[pltpu.VMEM((8 * PEERS, COLS), F32)],
    )
    modes = exchange(modes.reshape(6 * PAIRS, 2, COLS), "pair", [(FIRST + i) % PAIRS for i in range(PAIRS)]).reshape(12 * PAIRS, COLS)
    cells = call(
        ring_kernel, [(GROUP * CHUNK, COLS)], [VMEM] * 7, modes, sums, ring, pair, rims, back, cauchy,
        scratch=[pltpu.VMEM((32, COLS), F32)] * 2,
    )
    cells = exchange(cells.reshape(GROUP * CHUNK // 2, 2, COLS), ("core", "low"), near).reshape(GROUP * CHUNK, COLS)
    return call(
        final_kernel, [(2, ROWS, COLS)], [VMEM] * 5, cells, own, freq, solve, boxes,
        scratch=[pltpu.VMEM((2, ROWS, COLS), F32), pltpu.SemaphoreType.DMA((2,))], into=HBM,
    )


def solution(mesh):
    fine = Mesh(mesh.devices.reshape(PAIRS, 2, WALLS // 2, 2), ("pair", "core", "high", "low"))
    wall, span = ("high", "low"), ("pair", "core")
    return jax.shard_map(
        on_device, mesh=fine, in_specs=(P(None, None, wall, span), P()), out_specs=P(None, wall, span), check_vma=False
    )
```

```python
import jax
import jax.numpy as jnp
import numpy as np
from jax import lax
from jax.experimental import pallas as pl
from jax.experimental.pallas import tpu as pltpu
from jax.sharding import Mesh, PartitionSpec as P

F32 = jnp.float32
BF16 = jnp.bfloat16
EXACT = lax.Precision.HIGHEST
NY, NZ = 1536, 8192
WALLS, STRIPS = 8, 64
PAIRS, PEERS = STRIPS // 2, 2 * WALLS
WALL_ORDER = (4, 5, 3, 6, 2, 7, 1, 0)
PAIR_ORDER = [8 * x + z for z in range(7, -1, -1) for x in (2, 3, 1, 0)]
ROWS, COLS = NY // WALLS, NZ // STRIPS
GROUP = 4
OWNED = NY // PEERS
TILES = GROUP * OWNED // COLS
CHUNK = 10
SINE_Z, ENDS, EDGES, PICK, BOX_ROWS = 384, 640, 656, 672, 688
GHOST, MU_ROW, MU_COL, CLASS_ROWS = 0, 24, 48, 432
PHI, LAM_ROW, ENDS_Z, MU_BOX, SHARED_ROWS = 128, 136, 144, 152, 152


def halves(table):
    high = table.astype(np.float32).astype(BF16).astype(np.float64)
    return high, table - high


def sine_table(n):
    i = np.arange(1, n + 1)
    return np.sqrt(2 / (n + 1)) * np.sin(np.pi * np.outer(i, i) / (n + 1)), 4 * np.sin(np.pi * i / (2 * (n + 1))) ** 2


def tables():
    sine_y, mu_box = sine_table(ROWS)
    sine_z, lam = sine_table(COLS)
    ends_y, ends_z = sine_y[[0, -1]], sine_z[[0, -1]]
    boxes = np.zeros((BOX_ROWS, 256))
    boxes[:ROWS, :ROWS], boxes[ROWS:SINE_Z, :ROWS] = halves(sine_y)
    boxes[SINE_Z : SINE_Z + COLS, :COLS], boxes[SINE_Z : SINE_Z + COLS, COLS:] = halves(sine_z)
    boxes[SINE_Z + COLS : ENDS, :COLS] = boxes[SINE_Z : SINE_Z + COLS, :COLS]
    boxes[ENDS : ENDS + 2, :ROWS], boxes[ENDS + 8 : ENDS + 10, :ROWS] = halves(ends_y)
    boxes[EDGES : EDGES + 2, :COLS], boxes[EDGES + 8 : EDGES + 10, :COLS] = halves(ends_z)
    boxes[PICK, 0], boxes[PICK + 1, COLS - 1] = -0.5, 0.5
    both = mu_box[:, None] + lam[None, :]
    shared = np.zeros((SHARED_ROWS, 256))
    shared[:PHI, :ROWS] = both.T
    shared[:PHI, ROWS:] = 1.0
    shared[PHI:LAM_ROW, :ROWS] = ends_y[0]
    shared[LAM_ROW:ENDS_Z, :COLS] = lam
    shared[ENDS_Z : ENDS_Z + 2, :COLS] = ends_z
    r, wall = np.arange(ROWS), np.arange(WALLS)
    known = np.zeros((GROUP, 4, CLASS_ROWS, COLS))
    mix = np.zeros((GROUP, 128, COLS))
    into = np.zeros((GROUP, 2 * GROUP * ROWS, 256))
    back = np.zeros((GROUP, 4, GROUP * OWNED, 4 * ROWS))
    for c in range(GROUP):
        fold = np.zeros((64, 64))
        for k in range(GROUP):
            mode = c + 4 * k + PEERS * np.arange(OWNED)
            norm = np.where(mode == 0, np.sqrt(1 / NY), np.sqrt(2 / NY))
            angle = np.pi * np.outer(2 * r + 1, mode) / (2 * NY)
            turn = np.pi * (c + 4 * k) * wall / 8
            for n, wave in enumerate((np.cos(angle), np.sin(angle))):
                rows = slice(ROWS * (2 * k + n), ROWS * (2 * k + n + 1))
                into[c, rows, :OWNED], into[c, rows, COLS : COLS + OWNED] = halves(sine_y @ (norm * wave))
            for line in range(4):
                for core in range(2):
                    box = 16 * line + 8 * (1 - core) + np.argsort(WALL_ORDER)
                    fold[16 * k + 2 * line + core, box] = np.cos(turn)
                    fold[16 * k + 8 + 2 * line + core, box] = -np.sin(turn)
        mix[c, :64, :64], mix[c, 64:, :64] = halves(fold)
        mode = (c + 4 * np.arange(GROUP)[:, None] + PEERS * np.arange(OWNED)[None, :]).reshape(-1)
        norm = np.where(mode == 0, np.sqrt(1 / NY), np.sqrt(2 / NY))
        mu = 4 * np.sin(np.pi * mode / (2 * NY)) ** 2
        for high in range(4):
            for low in range(2):
                w = 2 * high + low
                table = norm[:, None] * np.cos(np.pi * np.outer(mode, 2 * (ROWS * w + r) + 1) / (2 * NY)) @ sine_y
                here, other = slice(ROWS * low, ROWS * (low + 1)), slice(ROWS * (2 + low), ROWS * (3 + low))
                back[c, high, :, here], back[c, high, :, other] = halves(table)
                for g in range(2):
                    y = ROWS * (w + g) + g - 1
                    row = (norm * np.cos(np.pi * mode * (2 * y + 1) / (2 * NY))).reshape(TILES, COLS)
                    for core in range(2):
                        known[c, high, 4 * g + 2 * core + low : MU_ROW : 8] = row
            known[c, high, MU_ROW:MU_COL] = np.concatenate([np.repeat(mu.reshape(TILES, COLS), 4, 0)] * 2)
            known[c, high, MU_COL:] = mu[:, None]
    whole = dict(both=both, shared=shared, known=known)
    half = dict(boxes=boxes, mix=mix, into=into, back=back)
    return {k: np.asarray(v, np.float32) for k, v in whole.items()}, {k: np.asarray(v, np.float32) for k, v in half.items()}


def dot(a, b, dims):
    return lax.dot_general(a, b, (dims, ((), ())), precision=EXACT, preferred_element_type=F32)


def fast(a, b, dims=((1,), (0,))):
    return lax.dot_general(a, b, (dims, ((), ())), preferred_element_type=F32)


def ids(shape, dim):
    return lax.broadcasted_iota(jnp.int32, shape, dim)


def pieces(value):
    high = value.astype(BF16).astype(F32)
    return high, value - high


def parts(value):
    return [piece.astype(BF16) for piece in pieces(value)]


def stacked(value):
    return jnp.concatenate(pieces(value), 0).astype(BF16)


def beside(value):
    return jnp.concatenate(parts(value), 1)


def summed(product):
    return product[:, :COLS] + product[:, COLS:]


def joined(product, rows, width=COLS, at=0):
    here, other = slice(at, at + width), slice(at + width, at + 2 * width)
    return product[:rows, here] + (product[:rows, other] + product[rows:, here])


def start(pairs, sems):
    copies = [pltpu.make_async_copy(*pair, sems.at[i]) for i, pair in enumerate(pairs)]
    for copy in copies:
        copy.start()
    return copies


def pack(lines):
    tails = [jnp.concatenate([lines[side][:, COLS:ROWS], lines[2 + side][:, COLS:ROWS]], 1) for side in range(2)]
    return [line[:, :COLS] for line in lines] + tails


def unpack(rows):
    return [
        jnp.concatenate([rows[2 * plane + side], rows[4 + side][:, 64 * plane : 64 * plane + 64]], 1)
        for plane in range(2) for side in range(2)
    ]


def box_kernel(
    wave_hbm, vel_hbm, both_hbm, boxes_hbm, shared_hbm, known_hbm, mix_hbm, into_hbm, back_hbm,
    out_ref, freq_ref, solve_ref, boxes_ref,
    chain_ref, reach_ref, cauchy_ref, ring_ref, pair_ref, rims_ref, mix_ref, into_ref, back_ref,
    wave_ref, vel_ref, both_ref, shared_ref, known_ref, sems,
):
    mine, high = 2 * lax.axis_index("core") + lax.axis_index("low"), lax.axis_index("high")
    copies = start([
        (wave_hbm, wave_ref), (both_hbm, both_ref), (vel_hbm.at[:, 0], vel_ref.at[:, 0]),
        (vel_hbm.at[:, 1], vel_ref.at[:, 1]), (boxes_hbm, boxes_ref), (shared_hbm, shared_ref),
        (known_hbm.at[mine, high], known_ref), (mix_hbm.at[mine], mix_ref), (into_hbm.at[mine], into_ref),
        (back_hbm.at[mine, high], back_ref),
    ], sems)
    row, lane = ids((ROWS, COLS), 0), ids((ROWS, COLS), 1)
    wall = 2 * lax.axis_index("high") + lax.axis_index("low")
    low = jnp.where(wall > 0, -0.5, 0.0)
    high = jnp.where(wall < WALLS - 1, 0.5, 0.0)
    copies[0].wait()
    copies[1].wait()
    for plane in range(2):
        wave = wave_ref[plane]
        solve_ref[ROWS * plane : ROWS * (plane + 1), :] = -1.0 / (wave * wave + both_ref[...])
    sources, rims, sides = [], [], []
    for plane in range(2):
        copies[2 + plane].wait()
        u, v, w = (vel_ref[c, plane] for c in range(3))
        above = jnp.where(row == ROWS - 1, 0.0, pltpu.roll(v, ROWS - 1, 0))
        below = jnp.where(row == 0, 0.0, pltpu.roll(v, 1, 0))
        after = jnp.where(lane == COLS - 1, 0.0, pltpu.roll(w, COLS - 1, 1))
        before = jnp.where(lane == 0, 0.0, pltpu.roll(w, 1, 1))
        sources += parts(wave_ref[plane] * u + 0.5 * ((above - below) + (after - before)))
        rims += [low * v[0:1], high * v[ROWS - 1 :]]
        sides.append(parts(w))
    for copy in copies[4:7]:
        copy.wait()
    sine, sine_z = boxes_ref[:SINE_Z, :ROWS], boxes_ref[SINE_Z : SINE_Z + COLS, :]
    product = fast(sine, jnp.concatenate(sources, 1))
    product = fast(jnp.concatenate([stacked(joined(product, ROWS, at=256 * p)) for p in range(2)], 0), sine_z)
    insides = []
    for plane in range(2):
        freq = joined(product[2 * ROWS * plane : 2 * ROWS * (plane + 1)], ROWS)
        rows = slice(ROWS * plane, ROWS * (plane + 1))
        freq_ref[rows, :] = freq
        insides.append(parts(freq * solve_ref[rows, :]))
    pick, edge = boxes_ref[PICK:BOX_ROWS, :COLS], boxes_ref[EDGES:PICK, :COLS]
    across = ((1,), (1,))
    halo = [(fast(pick, high, across) + fast(pick, low, across))[0:2] for high, low in sides]
    halo = stacked(jnp.concatenate(halo + [jnp.zeros((4, ROWS), F32)], 0))
    left, right = fast(halo, boxes_ref[:ROWS, :]), fast(halo, boxes_ref[ROWS:SINE_Z, :])
    halo = (left[0:8] + (left[8:16] + right[0:8]))[:, :ROWS]
    lines = []
    for plane, (high, low) in enumerate(insides):
        left, right = fast(edge, high, across), fast(edge, low, across)
        line = left[0:2] + (left[8:10] + right[0:2]) + halo[2 * plane : 2 * plane + 2]
        lines += [line[0:1], line[1:2]]
    ends = fast(boxes_ref[ENDS:EDGES, :ROWS], jnp.concatenate(insides[0] + insides[1], 1))
    ends = [joined(ends, 8, at=256 * p)[0:2] for p in range(2)]
    rims = fast(stacked(jnp.concatenate(rims + [jnp.zeros((4, COLS), F32)], 0)), sine_z)
    ends = jnp.concatenate(ends, 0) + joined(rims, 8)[0:4]
    four = jnp.concatenate((pack(lines) + [ends]) * 4, 0)
    for group in range(PEERS // 4):
        out_ref[4 * CHUNK * group : 4 * CHUNK * (group + 1), :] = four
    factors(wave_ref, shared_ref, known_ref, chain_ref, reach_ref, cauchy_ref, ring_ref, pair_ref, rims_ref)
    for copy in copies[7:]:
        copy.wait()


def decay(shift):
    root = jnp.sqrt(shift * (shift + 4.0))
    delta = (shift + root) / (2.0 + shift + root)
    return 1.0 - delta, delta * (2.0 - delta), -jnp.log1p(-delta)


def factors(
    wave_ref, shared_ref, known_ref, chain_ref, reach_ref, cauchy_ref, ring_ref, pair_ref, rims_ref,
):
    pair = lax.axis_index("pair")
    waves = [wave_ref[p] * wave_ref[p] for p in range(2)]
    row = ids((8, COLS), 0)
    lam = shared_ref[LAM_ROW:ENDS_Z, :COLS]
    for p in range(2):
        at = COLS * p
        reach_ref[at : at + COLS, :] = beside(shared_ref[PHI : PHI + 1, :] / (waves[p] + shared_ref[:PHI, :]))
        rows = slice(GROUP * OWNED * p, GROUP * OWNED * (p + 1))
        cauchy_ref[rows, :] = beside(1.0 / (known_ref[MU_COL:, :] + (waves[p] + lam[0:1])))
        rho, gap, theta = decay(waves[p] + lam)
        step = -1.0 * ROWS * theta
        scale = 1.0 / (gap * (1.0 - jnp.exp(-2.0 * NY * theta)))
        cross = jnp.exp(-(ROWS + 1.0) * theta)

        def reach(n):
            return jnp.exp(step * lax.bitwise_and(n, 15).astype(F32))

        here = sum(jnp.where(row == i, w, 0) for i, w in enumerate(WALL_ORDER))
        for place in range(WALLS):
            other = WALL_ORDER[place]
            up = reach(here - 1 - other) + rho * reach(15 - here - other)
            down = reach(here + other) + rho * reach(other - here)
            at = 32 * (WALLS * p + place)
            chain_ref[at : at + 8, :] = scale * (cross * up + down)
            chain_ref[at + 8 : at + 16, :] = scale * (up + cross * down)
            up = rho * reach(here - other) + reach(14 - here - other)
            down = rho * reach(here + 1 + other) + reach(other - here - 1)
            chain_ref[at + 16 : at + 24, :] = scale * (cross * up + down)
            chain_ref[at + 24 : at + 32, :] = scale * (up + cross * down)
    place = ids((24, COLS), 0)
    second, leftward = place % 4 >= 2, place % 2 == 0
    mu = known_ref[MU_ROW:MU_COL, :]
    _, _, theta = decay(jnp.where(second, waves[1], waves[0]) + mu)
    step = -2.0 * COLS * theta
    for group in range(PAIRS // 2):
        other = jnp.where(place < 12, PAIR_ORDER[2 * group], PAIR_ORDER[2 * group + 1])
        n = lax.bitwise_and(jnp.where(leftward, other - pair - 1, pair - 1 - other), PAIRS - 1)
        ring_ref[24 * group : 24 * group + 24, :] = jnp.exp(step * n.astype(F32))
    coefs = [[], [], [], []]
    for tile in range(TILES):
        rho, gap, theta = decay(jnp.where(row >= 4, waves[1], waves[0]) + mu[4 * tile : 4 * tile + 1])
        block = jnp.exp(-1.0 * COLS * theta)
        pair_ref[8 * tile : 8 * tile + 8, :] = jnp.exp(-(COLS + 1.0) * theta)
        pair_ref[24 + 8 * tile : 32 + 8 * tile, :] = block
        period = 1.0 - jnp.exp(-1.0 * NZ * theta)
        for i, value in enumerate((rho, 1.0 / (gap * period), period, block)):
            coefs[i] += [value[0:1], value[4:5]]
    for i in range(4):
        pair_ref[48 + 8 * i : 56 + 8 * i, :] = jnp.concatenate(coefs[i] + coefs[i][:2], 0)
    rims_ref[0:24, :] = known_ref[GHOST:MU_ROW, :]
    rims_ref[24:32, :] = shared_ref[ENDS_Z:MU_BOX, :COLS]


def strip_kernel(in_ref, chain_ref, reach_ref, pair_ref, rims_ref, mix_ref, into_ref, out_ref, own_ref, sums_ref, near_ref):
    box = [in_ref[pl.ds(i, PEERS, stride=CHUNK), :] for i in range(6)]
    ends = rims_ref[24:26, :]
    lines = unpack(box)
    even = ids((2 * PEERS, ROWS), 1) % 2 == 0
    added = []
    for plane in range(2):
        tops, bottoms = [], []
        for core in range(2):
            top = bottom = None
            for other in range(WALLS):
                at = 32 * (WALLS * plane + other)
                source = CHUNK * (WALLS * core + other) + 6 + 2 * plane
                first, last = in_ref[source : source + 1, :], in_ref[source + 1 : source + 2, :]
                weight = [chain_ref[at + 8 * i : at + 8 * i + 8, :] for i in range(4)]
                one, two = weight[0] * first + weight[1] * last, weight[2] * first + weight[3] * last
                top, bottom = (one, two) if top is None else (top + one, bottom + two)
            tops.append(top)
            bottoms.append(bottom)
        top, bottom = jnp.concatenate(tops, 0), jnp.concatenate(bottoms, 0)
        near_ref[pl.ds(2 * plane, PEERS, stride=8), :] = top
        near_ref[pl.ds(2 * plane + 1, PEERS, stride=8), :] = bottom
        sums = [value * ends[side : side + 1] for value in (top + bottom, top - bottom) for side in range(2)]
        product = fast(stacked(jnp.concatenate(sums, 0)), reach_ref[COLS * plane : COLS * (plane + 1), :])
        product = joined(product, 4 * PEERS, 256)[:, :ROWS]
        added.append(jnp.where(even, product[: 2 * PEERS], product[2 * PEERS :]))
    wall = 2 * lax.axis_index("high") + lax.axis_index("low")
    mine = 8 * (1 - lax.axis_index("core")) + sum(jnp.where(wall == w, i, 0) for i, w in enumerate(WALL_ORDER))
    own_ref[...] = near_ref[pl.ds(pl.multiple_of(8 * mine, 8), 8), :]
    lines = jnp.concatenate(lines, 0) + jnp.concatenate(added, 0)
    lines = jnp.concatenate([lines, jnp.zeros((4 * PEERS, 256 - ROWS), F32)], 1)
    folded = joined(fast(mix_ref[:, :64], beside(lines)), 64, 256)
    modes = []
    for k in range(GROUP):
        both = jnp.concatenate([folded[16 * k : 16 * k + 8, :ROWS], folded[16 * k + 8 : 16 * k + 16, :ROWS]], 1)
        modes.append(joined(fast(stacked(both), into_ref[2 * ROWS * k : 2 * ROWS * (k + 1), :]), 8))
    modes = [modes[0]] + [pltpu.roll(modes[k], COLS - 32 * k, 1) for k in range(1, GROUP)]
    row, lane = ids((8, COLS), 0), ids((8, COLS), 1)
    out = []
    for tile in range(TILES):
        value = jnp.where(lane < 96 - 32 * tile, modes[tile], modes[tile + 1])
        at = 8 * tile
        near = jnp.where(row % 4 < 2, pltpu.roll(value, 6, 0), pltpu.roll(value, 2, 0))
        value = value + pair_ref[at : at + 8, :] * near
        sums_ref[at : at + 8, :] = value
        near = jnp.where(row % 2 == 0, pltpu.roll(value, 7, 0), pltpu.roll(value, 1, 0))
        value = value + pair_ref[24 + at : 32 + at, :] * near
        out += [value[0:1], value[3:5], value[7:8]]
    sums_ref[24:32, :] = jnp.zeros((8, COLS), F32)
    out = jnp.concatenate(out * 2, 0)
    for group in range(PAIRS // 2):
        out_ref[24 * group : 24 * group + 24, :] = out


def ring_kernel(in_ref, sums_ref, ring_ref, pair_ref, rims_ref, back_ref, cauchy_ref, out_ref, far_ref, line_ref):
    total = in_ref[0:24, :] * ring_ref[0:24, :]
    for group in range(1, PAIRS // 2):
        total = total + in_ref[24 * group : 24 * group + 24, :] * ring_ref[24 * group : 24 * group + 24, :]
    far_ref[0:24, :] = total
    far_ref[24:32, :] = jnp.zeros((8, COLS), F32)
    count = 2 * TILES
    after, before = (
        far_ref[pl.ds(i, count, stride=2), :] + far_ref[pl.ds(12 + i, count, stride=2), :] for i in range(2)
    )
    rho, scale, period, block = (pair_ref[48 + 8 * i : 48 + 8 * i + count, :] for i in range(4))
    left0, left1, right0, right1 = (period * sums_ref[pl.ds(i, count, stride=4), :] for i in range(4))
    coming, going = block * before + right0, block * after + left1
    ghosts = (
        scale * (before + rho * (left0 + block * going)), scale * (coming + rho * going),
        scale * (rho * coming + going), scale * (rho * (right1 + block * coming) + after),
    )
    for i, value in enumerate(ghosts):
        line_ref[pl.ds(i, count, stride=4), :] = value
    tiles = [line_ref[8 * tile : 8 * tile + 8, :] for tile in range(TILES)]
    cells = joined(fast(stacked(jnp.concatenate(tiles, 1)), back_ref[...]), 8, 2 * ROWS)
    ends = rims_ref[24:26, :]
    is_first = ids((8, COLS), 0) % 4 < 2
    rims = []
    for plane in range(2):
        both = []
        for side in range(2):
            at = 4 * plane + 2 * side
            lines = [jnp.where(is_first, tile[at : at + 1], tile[at + 1 : at + 2]) for tile in tiles]
            both.append(jnp.concatenate([rims_ref[8 * i : 8 * i + 8, :] * line for i, line in enumerate(lines)], 1))
        rows = slice(GROUP * OWNED * plane, GROUP * OWNED * (plane + 1))
        product = joined(fast(stacked(jnp.concatenate(both, 0)), cauchy_ref[rows, :]), 16)
        rims.append(product[:8] * ends[0:1] + product[8:] * ends[1:2])
    out = []
    for core in (1, 0):
        for low in range(2):
            at = 2 * core + low
            out += pack([cells[2 * i + core : 2 * i + core + 1, ROWS * low : ROWS * (low + 1)] for i in range(4)])
            out += [rims[plane][4 * g + at : 4 * g + at + 1] for plane in range(2) for g in range(2)]
    out_ref[...] = jnp.concatenate(out, 0)


def final_kernel(in_ref, own_ref, freq_ref, solve_ref, boxes_ref, out_hbm, out_ref, sems):
    total = (in_ref[0:CHUNK, :] + in_ref[CHUNK : 2 * CHUNK, :]) + (in_ref[2 * CHUNK : 3 * CHUNK, :] + in_ref[3 * CHUNK :, :])
    sides = unpack([total[i : i + 1] for i in range(6)])
    rims = total[6:10] + own_ref[0:4, :]
    sine, sine_z = boxes_ref[:SINE_Z, :ROWS], boxes_ref[SINE_Z:ENDS, :]
    ends_y, ends_z = boxes_ref[ENDS:EDGES, :ROWS].astype(F32), boxes_ref[EDGES:PICK, :COLS].astype(F32)
    ends_y, ends_z = ends_y[0:2] + ends_y[8:10], ends_z[0:2] + ends_z[8:10]
    freqs = []
    for plane in range(2):
        rows = slice(ROWS * plane, ROWS * (plane + 1))
        lhs = pieces(jnp.concatenate([ends_y] + sides[2 * plane : 2 * plane + 2] + [jnp.zeros((4, ROWS), F32)], 0))
        rhs = pieces(jnp.concatenate([rims[2 * plane : 2 * plane + 2], ends_z, jnp.zeros((4, COLS), F32)], 0))
        lhs = jnp.concatenate([lhs[0], lhs[0], lhs[1], lhs[1]], 0).astype(BF16)
        rhs = jnp.concatenate([rhs[0], rhs[1], rhs[0], rhs[1]], 0).astype(BF16)
        freqs.append(beside((freq_ref[rows, :] - fast(lhs, rhs, ((0,), (0,)))) * solve_ref[rows, :]))
    product = summed(fast(jnp.concatenate(freqs, 0), sine_z))
    lines = [beside(product[ROWS * p : ROWS * (p + 1)]) for p in range(2)]
    product = fast(sine, jnp.concatenate(lines, 1))
    copies = []
    for plane in range(2):
        out_ref[plane] = joined(product, ROWS, at=256 * plane)
        copies += start([(out_ref.at[plane], out_hbm.at[plane])], sems.at[pl.ds(plane, 1)])
    for copy in copies:
        copy.wait()


VMEM = pl.BlockSpec(memory_space=pltpu.VMEM)
HBM = pl.BlockSpec(memory_space=pltpu.HBM)


def call(kernel, shapes, specs, *operands, scratch=(), into=VMEM):
    outs = [jax.ShapeDtypeStruct(s[0], s[1]) if isinstance(s[0], tuple) else jax.ShapeDtypeStruct(s, F32) for s in shapes]
    operands = [pltpu.with_memory_space_constraint(x, pltpu.HBM) if s is HBM else x for s, x in zip(specs, operands)]
    return pl.pallas_call(
        kernel,
        out_shape=outs if len(outs) > 1 else outs[0],
        in_specs=specs,
        out_specs=[into] * len(outs) if len(outs) > 1 else into,
        scratch_shapes=list(scratch),
        compiler_params=pltpu.CompilerParams(vmem_limit_bytes=24 << 20),
    )(*operands)


def exchange(block, axes, order=None):
    groups = None if order is None else [order]
    return lax.all_to_all(block, axes, split_axis=0, concat_axis=0, tiled=True, axis_index_groups=groups)


def on_device(velocity, wave_x):
    whole, half = tables()
    t = {k: jnp.asarray(v) for k, v in whole.items()} | {k: jnp.asarray(v, BF16) for k, v in half.items()}
    sent, freq, solve, boxes, chain, reach, cauchy, ring, pair, rims, mix, into, back = call(
        box_kernel,
        [
            (PEERS * CHUNK, COLS), (2 * ROWS, COLS), (2 * ROWS, COLS), ((BOX_ROWS, 256), BF16),
            (64 * WALLS, COLS), ((2 * COLS, 512), BF16), ((2 * GROUP * OWNED, 256), BF16), (12 * PAIRS, COLS), (80, COLS),
            (32, COLS), ((128, COLS), BF16), ((2 * GROUP * ROWS, 256), BF16), ((GROUP * OWNED, 4 * ROWS), BF16),
        ],
        [HBM] * 9,
        wave_x, velocity, t["both"], t["boxes"], t["shared"], t["known"], t["mix"], t["into"], t["back"],
        scratch=[
            pltpu.SMEM((2,), F32), pltpu.VMEM((3, 2, ROWS, COLS), F32), pltpu.VMEM((ROWS, COLS), F32),
            pltpu.VMEM((SHARED_ROWS, 256), F32), pltpu.VMEM((CLASS_ROWS, COLS), F32), pltpu.SemaphoreType.DMA((10,)),
        ],
    )
    near = [2 * core + low for core in (1, 0) for low in range(2)]
    order = [WALLS * core + w for core in (1, 0) for w in WALL_ORDER]
    sent = exchange(sent.reshape(PEERS * CHUNK // 2, 2, COLS), ("core", "high", "low"), order).reshape(PEERS * CHUNK, COLS)
    modes, own, sums = call(
        strip_kernel, [(12 * PAIRS, COLS), (8, COLS), (32, COLS)], [VMEM] * 7,
        sent, chain, reach, pair, rims, mix, into, scratch=[pltpu.VMEM((8 * PEERS, COLS), F32)],
    )
    modes = exchange(modes.reshape(6 * PAIRS, 2, COLS), "pair", PAIR_ORDER).reshape(12 * PAIRS, COLS)
    cells = call(
        ring_kernel, [(GROUP * CHUNK, COLS)], [VMEM] * 7, modes, sums, ring, pair, rims, back, cauchy,
        scratch=[pltpu.VMEM((32, COLS), F32)] * 2,
    )
    cells = exchange(cells.reshape(GROUP * CHUNK // 2, 2, COLS), ("core", "low"), near).reshape(GROUP * CHUNK, COLS)
    return call(
        final_kernel, [(2, ROWS, COLS)], [VMEM] * 5, cells, own, freq, solve, boxes,
        scratch=[pltpu.VMEM((2, ROWS, COLS), F32), pltpu.SemaphoreType.DMA((2,))], into=HBM,
    )


def solution(mesh):
    fine = Mesh(mesh.devices.reshape(PAIRS, 2, WALLS // 2, 2), ("pair", "core", "high", "low"))
    wall, span = ("high", "low"), ("pair", "core")
    return jax.shard_map(
        on_device, mesh=fine, in_specs=(P(None, None, wall, span), P()), out_specs=P(None, wall, span), check_vma=False
    )
```

```python
import jax
import jax.numpy as jnp
import numpy as np
from jax import lax
from jax.experimental import pallas as pl
from jax.experimental.pallas import tpu as pltpu
from jax.sharding import Mesh, PartitionSpec as P

F32 = jnp.float32
BF16 = jnp.bfloat16
EXACT = lax.Precision.HIGHEST
NY, NZ = 1536, 8192
WALLS, STRIPS = 8, 64
PAIRS, PEERS = STRIPS // 2, 2 * WALLS
NEAR_ORDER = (3, 2, 1, 0)
WALL_ORDER = (4, 5, 3, 6, 2, 7, 1, 0)
PAIR_ORDER = [8 * x + z for z in range(7, -1, -1) for x in (2, 3, 1, 0)]
ROWS, COLS = NY // WALLS, NZ // STRIPS
GROUP = 4
OWNED = NY // PEERS
TILES = GROUP * OWNED // COLS
CHUNK = 10
SINE_Z, ENDS, EDGES, PICK, BOX_ROWS = 384, 640, 656, 672, 688
GHOST, MU_ROW, MU_COL, CLASS_ROWS = 0, 24, 48, 432
PHI, LAM_ROW, ENDS_Z, MU_BOX, SHARED_ROWS = 128, 136, 144, 152, 152


def halves(table):
    high = table.astype(np.float32).astype(BF16).astype(np.float64)
    return high, table - high


def sine_table(n):
    i = np.arange(1, n + 1)
    return np.sqrt(2 / (n + 1)) * np.sin(np.pi * np.outer(i, i) / (n + 1)), 4 * np.sin(np.pi * i / (2 * (n + 1))) ** 2


def tables():
    sine_y, mu_box = sine_table(ROWS)
    sine_z, lam = sine_table(COLS)
    ends_y, ends_z = sine_y[[0, -1]], sine_z[[0, -1]]
    boxes = np.zeros((BOX_ROWS, 256))
    boxes[:ROWS, :ROWS], boxes[ROWS:SINE_Z, :ROWS] = halves(sine_y)
    boxes[SINE_Z : SINE_Z + COLS, :COLS], boxes[SINE_Z : SINE_Z + COLS, COLS:] = halves(sine_z)
    boxes[SINE_Z + COLS : ENDS, :COLS] = boxes[SINE_Z : SINE_Z + COLS, :COLS]
    boxes[ENDS : ENDS + 2, :ROWS], boxes[ENDS + 8 : ENDS + 10, :ROWS] = halves(ends_y)
    boxes[EDGES : EDGES + 2, :COLS], boxes[EDGES + 8 : EDGES + 10, :COLS] = halves(ends_z)
    boxes[PICK, 0], boxes[PICK + 1, COLS - 1] = -0.5, 0.5
    both = mu_box[:, None] + lam[None, :]
    shared = np.zeros((SHARED_ROWS, 256))
    shared[:PHI, :ROWS] = both.T
    shared[:PHI, ROWS:] = 1.0
    shared[PHI:LAM_ROW, :ROWS] = ends_y[0]
    shared[LAM_ROW:ENDS_Z, :COLS] = lam
    shared[ENDS_Z : ENDS_Z + 2, :COLS] = ends_z
    r, wall = np.arange(ROWS), np.arange(WALLS)
    known = np.zeros((GROUP, 4, CLASS_ROWS, COLS))
    mix = np.zeros((GROUP, 128, COLS))
    into = np.zeros((GROUP, 2 * GROUP * ROWS, 256))
    back = np.zeros((GROUP, 4, GROUP * OWNED, 4 * ROWS))
    for c in range(GROUP):
        fold = np.zeros((64, 64))
        for k in range(GROUP):
            mode = c + 4 * k + PEERS * np.arange(OWNED)
            norm = np.where(mode == 0, np.sqrt(1 / NY), np.sqrt(2 / NY))
            angle = np.pi * np.outer(2 * r + 1, mode) / (2 * NY)
            turn = np.pi * (c + 4 * k) * wall / 8
            for n, wave in enumerate((np.cos(angle), np.sin(angle))):
                rows = slice(ROWS * (2 * k + n), ROWS * (2 * k + n + 1))
                into[c, rows, :OWNED], into[c, rows, COLS : COLS + OWNED] = halves(sine_y @ (norm * wave))
            for line in range(4):
                for core in range(2):
                    box = 16 * line + 8 * (1 - core) + np.argsort(WALL_ORDER)
                    fold[16 * k + 2 * line + core, box] = np.cos(turn)
                    fold[16 * k + 8 + 2 * line + core, box] = -np.sin(turn)
        mix[c, :64, :64], mix[c, 64:, :64] = halves(fold)
        mode = (c + 4 * np.arange(GROUP)[:, None] + PEERS * np.arange(OWNED)[None, :]).reshape(-1)
        norm = np.where(mode == 0, np.sqrt(1 / NY), np.sqrt(2 / NY))
        mu = 4 * np.sin(np.pi * mode / (2 * NY)) ** 2
        for high in range(4):
            for low in range(2):
                w = 2 * high + low
                table = norm[:, None] * np.cos(np.pi * np.outer(mode, 2 * (ROWS * w + r) + 1) / (2 * NY)) @ sine_y
                here, other = slice(ROWS * low, ROWS * (low + 1)), slice(ROWS * (2 + low), ROWS * (3 + low))
                back[c, high, :, here], back[c, high, :, other] = halves(table)
                for g in range(2):
                    y = ROWS * (w + g) + g - 1
                    row = (norm * np.cos(np.pi * mode * (2 * y + 1) / (2 * NY))).reshape(TILES, COLS)
                    for core in range(2):
                        known[c, high, 4 * g + 2 * core + low : MU_ROW : 8] = row
            known[c, high, MU_ROW:MU_COL] = np.concatenate([np.repeat(mu.reshape(TILES, COLS), 4, 0)] * 2)
            known[c, high, MU_COL:] = mu[:, None]
    whole = dict(both=both, shared=shared, known=known)
    half = dict(boxes=boxes, mix=mix, into=into, back=back)
    return {k: np.asarray(v, np.float32) for k, v in whole.items()}, {k: np.asarray(v, np.float32) for k, v in half.items()}


def dot(a, b, dims):
    return lax.dot_general(a, b, (dims, ((), ())), precision=EXACT, preferred_element_type=F32)


def fast(a, b, dims=((1,), (0,))):
    return lax.dot_general(a, b, (dims, ((), ())), preferred_element_type=F32)


def ids(shape, dim):
    return lax.broadcasted_iota(jnp.int32, shape, dim)


def pieces(value):
    high = value.astype(BF16).astype(F32)
    return high, value - high


def parts(value):
    return [piece.astype(BF16) for piece in pieces(value)]


def stacked(value):
    return jnp.concatenate(pieces(value), 0).astype(BF16)


def beside(value):
    return jnp.concatenate(parts(value), 1)


def summed(product):
    return product[:, :COLS] + product[:, COLS:]


def joined(product, rows, width=COLS, at=0):
    here, other = slice(at, at + width), slice(at + width, at + 2 * width)
    return product[:rows, here] + (product[:rows, other] + product[rows:, here])


def start(pairs, sems):
    copies = [pltpu.make_async_copy(*pair, sems.at[i]) for i, pair in enumerate(pairs)]
    for copy in copies:
        copy.start()
    return copies


def pack(lines):
    tails = [jnp.concatenate([lines[side][:, COLS:ROWS], lines[2 + side][:, COLS:ROWS]], 1) for side in range(2)]
    return [line[:, :COLS] for line in lines] + tails


def unpack(rows):
    return [
        jnp.concatenate([rows[2 * plane + side], rows[4 + side][:, 64 * plane : 64 * plane + 64]], 1)
        for plane in range(2) for side in range(2)
    ]


def box_kernel(
    wave_hbm, vel_hbm, both_hbm, boxes_hbm, shared_hbm, known_hbm, mix_hbm, into_hbm, back_hbm,
    out_ref, freq_ref, solve_ref, boxes_ref,
    chain_ref, reach_ref, cauchy_ref, ring_ref, pair_ref, rims_ref, mix_ref, into_ref, back_ref,
    wave_ref, vel_ref, both_ref, shared_ref, known_ref, sems,
):
    mine, high = 2 * lax.axis_index("core") + lax.axis_index("low"), lax.axis_index("high")
    copies = start([
        (wave_hbm, wave_ref), (both_hbm, both_ref), (vel_hbm.at[:, 0], vel_ref.at[:, 0]),
        (vel_hbm.at[:, 1], vel_ref.at[:, 1]), (boxes_hbm, boxes_ref), (shared_hbm, shared_ref),
        (known_hbm.at[mine, high], known_ref), (mix_hbm.at[mine], mix_ref), (into_hbm.at[mine], into_ref),
        (back_hbm.at[mine, high], back_ref),
    ], sems)
    row, lane = ids((ROWS, COLS), 0), ids((ROWS, COLS), 1)
    wall = 2 * lax.axis_index("high") + lax.axis_index("low")
    low = jnp.where(wall > 0, -0.5, 0.0)
    high = jnp.where(wall < WALLS - 1, 0.5, 0.0)
    copies[0].wait()
    copies[1].wait()
    for plane in range(2):
        wave = wave_ref[plane]
        solve_ref[ROWS * plane : ROWS * (plane + 1), :] = -1.0 / (wave * wave + both_ref[...])
    sources, rims, sides = [], [], []
    for plane in range(2):
        copies[2 + plane].wait()
        u, v, w = (vel_ref[c, plane] for c in range(3))
        above = jnp.where(row == ROWS - 1, 0.0, pltpu.roll(v, ROWS - 1, 0))
        below = jnp.where(row == 0, 0.0, pltpu.roll(v, 1, 0))
        after = jnp.where(lane == COLS - 1, 0.0, pltpu.roll(w, COLS - 1, 1))
        before = jnp.where(lane == 0, 0.0, pltpu.roll(w, 1, 1))
        sources += parts(wave_ref[plane] * u + 0.5 * ((above - below) + (after - before)))
        rims += [low * v[0:1], high * v[ROWS - 1 :]]
        sides.append(parts(w))
    for copy in copies[4:7]:
        copy.wait()
    sine, sine_z = boxes_ref[:SINE_Z, :ROWS], boxes_ref[SINE_Z : SINE_Z + COLS, :]
    product = fast(sine, jnp.concatenate(sources, 1))
    product = fast(jnp.concatenate([stacked(joined(product, ROWS, at=256 * p)) for p in range(2)], 0), sine_z)
    insides = []
    for plane in range(2):
        freq = joined(product[2 * ROWS * plane : 2 * ROWS * (plane + 1)], ROWS)
        rows = slice(ROWS * plane, ROWS * (plane + 1))
        freq_ref[rows, :] = freq
        insides.append(parts(freq * solve_ref[rows, :]))
    pick, edge = boxes_ref[PICK:BOX_ROWS, :COLS], boxes_ref[EDGES:PICK, :COLS]
    across = ((1,), (1,))
    halo = [(fast(pick, high, across) + fast(pick, low, across))[0:2] for high, low in sides]
    halo = stacked(jnp.concatenate(halo + [jnp.zeros((4, ROWS), F32)], 0))
    left, right = fast(halo, boxes_ref[:ROWS, :]), fast(halo, boxes_ref[ROWS:SINE_Z, :])
    halo = (left[0:8] + (left[8:16] + right[0:8]))[:, :ROWS]
    lines = []
    for plane, (high, low) in enumerate(insides):
        left, right = fast(edge, high, across), fast(edge, low, across)
        line = left[0:2] + (left[8:10] + right[0:2]) + halo[2 * plane : 2 * plane + 2]
        lines += [line[0:1], line[1:2]]
    ends = fast(boxes_ref[ENDS:EDGES, :ROWS], jnp.concatenate(insides[0] + insides[1], 1))
    ends = [joined(ends, 8, at=256 * p)[0:2] for p in range(2)]
    rims = fast(stacked(jnp.concatenate(rims + [jnp.zeros((4, COLS), F32)], 0)), sine_z)
    ends = jnp.concatenate(ends, 0) + joined(rims, 8)[0:4]
    four = jnp.concatenate((pack(lines) + [ends]) * 4, 0)
    for group in range(PEERS // 4):
        out_ref[4 * CHUNK * group : 4 * CHUNK * (group + 1), :] = four
    factors(wave_ref, shared_ref, known_ref, chain_ref, reach_ref, cauchy_ref, ring_ref, pair_ref, rims_ref)
    for copy in copies[7:]:
        copy.wait()


def decay(shift):
    root = jnp.sqrt(shift * (shift + 4.0))
    delta = (shift + root) / (2.0 + shift + root)
    return 1.0 - delta, delta * (2.0 - delta), -jnp.log1p(-delta)


def factors(
    wave_ref, shared_ref, known_ref, chain_ref, reach_ref, cauchy_ref, ring_ref, pair_ref, rims_ref,
):
    pair = lax.axis_index("pair")
    waves = [wave_ref[p] * wave_ref[p] for p in range(2)]
    row = ids((8, COLS), 0)
    lam = shared_ref[LAM_ROW:ENDS_Z, :COLS]
    for p in range(2):
        at = COLS * p
        reach_ref[at : at + COLS, :] = beside(shared_ref[PHI : PHI + 1, :] / (waves[p] + shared_ref[:PHI, :]))
        rows = slice(GROUP * OWNED * p, GROUP * OWNED * (p + 1))
        cauchy_ref[rows, :] = beside(1.0 / (known_ref[MU_COL:, :] + (waves[p] + lam[0:1])))
        rho, gap, theta = decay(waves[p] + lam)
        step = -1.0 * ROWS * theta
        scale = 1.0 / (gap * (1.0 - jnp.exp(-2.0 * NY * theta)))
        cross = jnp.exp(-(ROWS + 1.0) * theta)

        def reach(n):
            return jnp.exp(step * lax.bitwise_and(n, 15).astype(F32))

        here = sum(jnp.where(row == i, w, 0) for i, w in enumerate(WALL_ORDER))
        for place in range(WALLS):
            other = WALL_ORDER[place]
            up = reach(here - 1 - other) + rho * reach(15 - here - other)
            down = reach(here + other) + rho * reach(other - here)
            at = 32 * (WALLS * p + place)
            chain_ref[at : at + 8, :] = scale * (cross * up + down)
            chain_ref[at + 8 : at + 16, :] = scale * (up + cross * down)
            up = rho * reach(here - other) + reach(14 - here - other)
            down = rho * reach(here + 1 + other) + reach(other - here - 1)
            chain_ref[at + 16 : at + 24, :] = scale * (cross * up + down)
            chain_ref[at + 24 : at + 32, :] = scale * (up + cross * down)
    place = ids((24, COLS), 0)
    second, leftward = place % 4 >= 2, place % 2 == 0
    mu = known_ref[MU_ROW:MU_COL, :]
    _, _, theta = decay(jnp.where(second, waves[1], waves[0]) + mu)
    step = -2.0 * COLS * theta
    for group in range(PAIRS // 2):
        other = jnp.where(place < 12, PAIR_ORDER[2 * group], PAIR_ORDER[2 * group + 1])
        n = lax.bitwise_and(jnp.where(leftward, other - pair - 1, pair - 1 - other), PAIRS - 1)
        ring_ref[24 * group : 24 * group + 24, :] = jnp.exp(step * n.astype(F32))
    coefs = [[], [], [], []]
    for tile in range(TILES):
        rho, gap, theta = decay(jnp.where(row >= 4, waves[1], waves[0]) + mu[4 * tile : 4 * tile + 1])
        block = jnp.exp(-1.0 * COLS * theta)
        pair_ref[8 * tile : 8 * tile + 8, :] = jnp.exp(-(COLS + 1.0) * theta)
        pair_ref[24 + 8 * tile : 32 + 8 * tile, :] = block
        period = 1.0 - jnp.exp(-1.0 * NZ * theta)
        for i, value in enumerate((rho, 1.0 / (gap * period), period, block)):
            coefs[i] += [value[0:1], value[4:5]]
    for i in range(4):
        pair_ref[48 + 8 * i : 56 + 8 * i, :] = jnp.concatenate(coefs[i] + coefs[i][:2], 0)
    rims_ref[0:24, :] = known_ref[GHOST:MU_ROW, :]
    rims_ref[24:32, :] = shared_ref[ENDS_Z:MU_BOX, :COLS]


def strip_kernel(in_ref, chain_ref, reach_ref, pair_ref, rims_ref, mix_ref, into_ref, out_ref, own_ref, sums_ref, near_ref):
    box = [in_ref[pl.ds(i, PEERS, stride=CHUNK), :] for i in range(6)]
    ends = rims_ref[24:26, :]
    lines = unpack(box)
    even = ids((2 * PEERS, ROWS), 1) % 2 == 0
    added = []
    for plane in range(2):
        tops, bottoms = [], []
        for core in range(2):
            top = bottom = None
            for other in range(WALLS):
                at = 32 * (WALLS * plane + other)
                source = CHUNK * (WALLS * core + other) + 6 + 2 * plane
                first, last = in_ref[source : source + 1, :], in_ref[source + 1 : source + 2, :]
                weight = [chain_ref[at + 8 * i : at + 8 * i + 8, :] for i in range(4)]
                one, two = weight[0] * first + weight[1] * last, weight[2] * first + weight[3] * last
                top, bottom = (one, two) if top is None else (top + one, bottom + two)
            tops.append(top)
            bottoms.append(bottom)
        top, bottom = jnp.concatenate(tops, 0), jnp.concatenate(bottoms, 0)
        near_ref[pl.ds(2 * plane, PEERS, stride=8), :] = top
        near_ref[pl.ds(2 * plane + 1, PEERS, stride=8), :] = bottom
        sums = [value * ends[side : side + 1] for value in (top + bottom, top - bottom) for side in range(2)]
        product = fast(stacked(jnp.concatenate(sums, 0)), reach_ref[COLS * plane : COLS * (plane + 1), :])
        product = joined(product, 4 * PEERS, 256)[:, :ROWS]
        added.append(jnp.where(even, product[: 2 * PEERS], product[2 * PEERS :]))
    wall = 2 * lax.axis_index("high") + lax.axis_index("low")
    mine = 8 * (1 - lax.axis_index("core")) + sum(jnp.where(wall == w, i, 0) for i, w in enumerate(WALL_ORDER))
    own_ref[...] = near_ref[pl.ds(pl.multiple_of(8 * mine, 8), 8), :]
    lines = jnp.concatenate(lines, 0) + jnp.concatenate(added, 0)
    lines = jnp.concatenate([lines, jnp.zeros((4 * PEERS, 256 - ROWS), F32)], 1)
    folded = joined(fast(mix_ref[:, :64], beside(lines)), 64, 256)
    modes = []
    for k in range(GROUP):
        both = jnp.concatenate([folded[16 * k : 16 * k + 8, :ROWS], folded[16 * k + 8 : 16 * k + 16, :ROWS]], 1)
        modes.append(joined(fast(stacked(both), into_ref[2 * ROWS * k : 2 * ROWS * (k + 1), :]), 8))
    modes = [modes[0]] + [pltpu.roll(modes[k], COLS - 32 * k, 1) for k in range(1, GROUP)]
    row, lane = ids((8, COLS), 0), ids((8, COLS), 1)
    out = []
    for tile in range(TILES):
        value = jnp.where(lane < 96 - 32 * tile, modes[tile], modes[tile + 1])
        at = 8 * tile
        near = jnp.where(row % 4 < 2, pltpu.roll(value, 6, 0), pltpu.roll(value, 2, 0))
        value = value + pair_ref[at : at + 8, :] * near
        sums_ref[at : at + 8, :] = value
        near = jnp.where(row % 2 == 0, pltpu.roll(value, 7, 0), pltpu.roll(value, 1, 0))
        value = value + pair_ref[24 + at : 32 + at, :] * near
        out += [value[0:1], value[3:5], value[7:8]]
    sums_ref[24:32, :] = jnp.zeros((8, COLS), F32)
    out = jnp.concatenate(out * 2, 0)
    for group in range(PAIRS // 2):
        out_ref[24 * group : 24 * group + 24, :] = out


def ring_kernel(in_ref, sums_ref, ring_ref, pair_ref, rims_ref, back_ref, cauchy_ref, out_ref, far_ref, line_ref):
    total = in_ref[0:24, :] * ring_ref[0:24, :]
    for group in range(1, PAIRS // 2):
        total = total + in_ref[24 * group : 24 * group + 24, :] * ring_ref[24 * group : 24 * group + 24, :]
    far_ref[0:24, :] = total
    far_ref[24:32, :] = jnp.zeros((8, COLS), F32)
    count = 2 * TILES
    after, before = (
        far_ref[pl.ds(i, count, stride=2), :] + far_ref[pl.ds(12 + i, count, stride=2), :] for i in range(2)
    )
    rho, scale, period, block = (pair_ref[48 + 8 * i : 48 + 8 * i + count, :] for i in range(4))
    left0, left1, right0, right1 = (period * sums_ref[pl.ds(i, count, stride=4), :] for i in range(4))
    coming, going = block * before + right0, block * after + left1
    ghosts = (
        scale * (before + rho * (left0 + block * going)), scale * (coming + rho * going),
        scale * (rho * coming + going), scale * (rho * (right1 + block * coming) + after),
    )
    for i, value in enumerate(ghosts):
        line_ref[pl.ds(i, count, stride=4), :] = value
    tiles = [line_ref[8 * tile : 8 * tile + 8, :] for tile in range(TILES)]
    cells = joined(fast(stacked(jnp.concatenate(tiles, 1)), back_ref[...]), 8, 2 * ROWS)
    ends = rims_ref[24:26, :]
    is_first = ids((8, COLS), 0) % 4 < 2
    rims = []
    for plane in range(2):
        both = []
        for side in range(2):
            at = 4 * plane + 2 * side
            lines = [jnp.where(is_first, tile[at : at + 1], tile[at + 1 : at + 2]) for tile in tiles]
            both.append(jnp.concatenate([rims_ref[8 * i : 8 * i + 8, :] * line for i, line in enumerate(lines)], 1))
        rows = slice(GROUP * OWNED * plane, GROUP * OWNED * (plane + 1))
        product = joined(fast(stacked(jnp.concatenate(both, 0)), cauchy_ref[rows, :]), 16)
        rims.append(product[:8] * ends[0:1] + product[8:] * ends[1:2])
    out = []
    for at in NEAR_ORDER:
        core, low = at // 2, at % 2
        out += pack([cells[2 * i + core : 2 * i + core + 1, ROWS * low : ROWS * (low + 1)] for i in range(4)])
        out += [rims[plane][4 * g + at : 4 * g + at + 1] for plane in range(2) for g in range(2)]
    out_ref[...] = jnp.concatenate(out, 0)


def final_kernel(in_ref, own_ref, freq_ref, solve_ref, boxes_ref, out_hbm, out_ref, sems):
    total = (in_ref[0:CHUNK, :] + in_ref[CHUNK : 2 * CHUNK, :]) + (in_ref[2 * CHUNK : 3 * CHUNK, :] + in_ref[3 * CHUNK :, :])
    sides = unpack([total[i : i + 1] for i in range(6)])
    rims = total[6:10] + own_ref[0:4, :]
    sine, sine_z = boxes_ref[:SINE_Z, :ROWS], boxes_ref[SINE_Z:ENDS, :]
    ends_y, ends_z = boxes_ref[ENDS:EDGES, :ROWS].astype(F32), boxes_ref[EDGES:PICK, :COLS].astype(F32)
    ends_y, ends_z = ends_y[0:2] + ends_y[8:10], ends_z[0:2] + ends_z[8:10]
    freqs = []
    for plane in range(2):
        rows = slice(ROWS * plane, ROWS * (plane + 1))
        lhs = pieces(jnp.concatenate([ends_y] + sides[2 * plane : 2 * plane + 2] + [jnp.zeros((4, ROWS), F32)], 0))
        rhs = pieces(jnp.concatenate([rims[2 * plane : 2 * plane + 2], ends_z, jnp.zeros((4, COLS), F32)], 0))
        lhs = jnp.concatenate([lhs[0], lhs[0], lhs[1], lhs[1]], 0).astype(BF16)
        rhs = jnp.concatenate([rhs[0], rhs[1], rhs[0], rhs[1]], 0).astype(BF16)
        freqs.append(beside((freq_ref[rows, :] - fast(lhs, rhs, ((0,), (0,)))) * solve_ref[rows, :]))
    product = summed(fast(jnp.concatenate(freqs, 0), sine_z))
    lines = [beside(product[ROWS * p : ROWS * (p + 1)]) for p in range(2)]
    product = fast(sine, jnp.concatenate(lines, 1))
    copies = []
    for plane in range(2):
        out_ref[plane] = joined(product, ROWS, at=256 * plane)
        copies += start([(out_ref.at[plane], out_hbm.at[plane])], sems.at[pl.ds(plane, 1)])
    for copy in copies:
        copy.wait()


VMEM = pl.BlockSpec(memory_space=pltpu.VMEM)
HBM = pl.BlockSpec(memory_space=pltpu.HBM)


def call(kernel, shapes, specs, *operands, scratch=(), into=VMEM):
    outs = [jax.ShapeDtypeStruct(s[0], s[1]) if isinstance(s[0], tuple) else jax.ShapeDtypeStruct(s, F32) for s in shapes]
    operands = [pltpu.with_memory_space_constraint(x, pltpu.HBM) if s is HBM else x for s, x in zip(specs, operands)]
    return pl.pallas_call(
        kernel,
        out_shape=outs if len(outs) > 1 else outs[0],
        in_specs=specs,
        out_specs=[into] * len(outs) if len(outs) > 1 else into,
        scratch_shapes=list(scratch),
        compiler_params=pltpu.CompilerParams(vmem_limit_bytes=24 << 20),
    )(*operands)


def exchange(block, axes, order=None):
    groups = None if order is None else [order]
    return lax.all_to_all(block, axes, split_axis=0, concat_axis=0, tiled=True, axis_index_groups=groups)


def on_device(velocity, wave_x):
    whole, half = tables()
    t = {k: jnp.asarray(v) for k, v in whole.items()} | {k: jnp.asarray(v, BF16) for k, v in half.items()}
    sent, freq, solve, boxes, chain, reach, cauchy, ring, pair, rims, mix, into, back = call(
        box_kernel,
        [
            (PEERS * CHUNK, COLS), (2 * ROWS, COLS), (2 * ROWS, COLS), ((BOX_ROWS, 256), BF16),
            (64 * WALLS, COLS), ((2 * COLS, 512), BF16), ((2 * GROUP * OWNED, 256), BF16), (12 * PAIRS, COLS), (80, COLS),
            (32, COLS), ((128, COLS), BF16), ((2 * GROUP * ROWS, 256), BF16), ((GROUP * OWNED, 4 * ROWS), BF16),
        ],
        [HBM] * 9,
        wave_x, velocity, t["both"], t["boxes"], t["shared"], t["known"], t["mix"], t["into"], t["back"],
        scratch=[
            pltpu.SMEM((2,), F32), pltpu.VMEM((3, 2, ROWS, COLS), F32), pltpu.VMEM((ROWS, COLS), F32),
            pltpu.VMEM((SHARED_ROWS, 256), F32), pltpu.VMEM((CLASS_ROWS, COLS), F32), pltpu.SemaphoreType.DMA((10,)),
        ],
    )
    near = list(NEAR_ORDER)
    order = [WALLS * core + w for core in (1, 0) for w in WALL_ORDER]
    sent = exchange(sent.reshape(PEERS * CHUNK // 2, 2, COLS), ("core", "high", "low"), order).reshape(PEERS * CHUNK, COLS)
    modes, own, sums = call(
        strip_kernel, [(12 * PAIRS, COLS), (8, COLS), (32, COLS)], [VMEM] * 7,
        sent, chain, reach, pair, rims, mix, into, scratch=[pltpu.VMEM((8 * PEERS, COLS), F32)],
    )
    modes = exchange(modes.reshape(6 * PAIRS, 2, COLS), "pair", PAIR_ORDER).reshape(12 * PAIRS, COLS)
    cells = call(
        ring_kernel, [(GROUP * CHUNK, COLS)], [VMEM] * 7, modes, sums, ring, pair, rims, back, cauchy,
        scratch=[pltpu.VMEM((32, COLS), F32)] * 2,
    )
    cells = exchange(cells.reshape(GROUP * CHUNK // 2, 2, COLS), ("core", "low"), near).reshape(GROUP * CHUNK, COLS)
    return call(
        final_kernel, [(2, ROWS, COLS)], [VMEM] * 5, cells, own, freq, solve, boxes,
        scratch=[pltpu.VMEM((2, ROWS, COLS), F32), pltpu.SemaphoreType.DMA((2,))], into=HBM,
    )


def solution(mesh):
    fine = Mesh(mesh.devices.reshape(PAIRS, 2, WALLS // 2, 2), ("pair", "core", "high", "low"))
    wall, span = ("high", "low"), ("pair", "core")
    return jax.shard_map(
        on_device, mesh=fine, in_specs=(P(None, None, wall, span), P()), out_specs=P(None, wall, span), check_vma=False
    )
```
